32 devices in a mesh: group: 2 (over y), gx: 4 (over z), gz: 2 (over x), col: 2 (over core).
Axes of the slice: x: 2, y: 2, z: 4, core: 2. Of those that a mesh axis runs over, the one named last changes fastest.
Arguments:
- features: bfloat16 [32, 64, 16, 256], P(None, 'col', ('group', 'gx'), 'gz'), parts along dimension 2, may hold values from -6 to 6
- labels: int32 [64, 16, 256], P(None, ('group', 'gx'), 'gz'), parts along dimension 1, may hold values from 0 to 3
- grid_index: int32 [64], replicated, may hold values from 0 to 15
- stretch: float32 [16, 9], replicated, may hold values from 0.5 to 2
- tile_filter: float32 [32, 25], replicated, may hold values from -1.25 to 1.25
- wall_filter: float32 [32, 9], replicated, may hold values from -2 to 2
- class_weight: float32 [4, 32], replicated, may hold values from -1 to 1
Outputs:
- grad_features: bfloat16 [32, 64, 16, 256], P(None, 'col', ('group', 'gx'), 'gz'), parts along dimension 2
- grad_tile_filter: float32 [64, 25], P('group'), parts along dimension 0
- grad_wall_filter: float32 [64, 9], P('group'), parts along dimension 0
- grad_class_weight: float32 [8, 32], P('group'), parts along dimension 0
The draws below stay inside these ranges and needn't reach their ends.
There are 2 independent parts, one for each index of `group`. The reference program is written for one: setup_inputs(seed, part) draws one part's arguments, and reference() takes and returns one part's arrays. A program takes and returns all parts, laid end to end along the dimension named above; an argument that names none is the same for every part. Nothing has to cross between parts.
All inputs are finite; a program needn't handle non-finite values.
Results may differ from the reference program's by a relative error of at most 0.0064.
Values may be sent and summed in bfloat16 or wider, within the bound.
A program may use at most 64 MiB of HBM per device.

```python
import math
import jax
import jax.numpy as jnp
from jax import lax

C = 32
K = 4
L = 16
NY = 64
NX = 8
NZ = 256


def with_ends(entries, own_key, low, largest):
    longest = entries.shape.index(max(entries.shape))
    spots = []
    for shift in (0, 1):
        where = [jax.random.randint(jax.random.fold_in(own_key, axis), (), 0, length) for axis, length in enumerate(entries.shape)]
        where[longest] = (where[longest] + shift) % entries.shape[longest]
        spots.append(tuple(where))
    return entries.at[spots[0]].set(low).at[spots[1]].set(largest)


def block_levels(own_key, shape, shards, low, high):
    loudness, own = 1.0, jax.random.fold_in(own_key, 6)
    for position, parts in shards:
        draws = jnp.exp(jax.random.uniform(jax.random.fold_in(own, position), (parts,), jnp.float32, low / len(shards), high / len(shards)))
        loudness = loudness * jnp.repeat(draws, shape[position] // parts).reshape([-1 if axis == position else 1 for axis in range(len(shape))])
    return loudness


def centred(stream_key, shape, deviation, reach, cuts=(), kind=jnp.bfloat16):
    level = block_levels(stream_key, shape, cuts, -0.22, 0.18) if cuts else 1.0
    values = jax.random.normal(stream_key, shape, jnp.float32) * deviation * level
    return jnp.minimum(jnp.maximum(values, -reach), reach).astype(kind)


def setup_inputs(seed: int = 0, part: int = 0) -> dict:
    splits = jax.random.split(jax.random.key(seed), 8)
    part_splits = jax.random.split(jax.random.fold_in(splits[7], part), 8)
    features = centred(part_splits[0], (C, NY, NX, NZ), 1.0, 6.0, ((1, 2), (2, 4), (3, 2)))
    labels = with_ends(jax.random.randint(part_splits[1], (NY, NX, NZ), 0, K), jax.random.fold_in(part_splits[1], 1), 0, K - 1).astype(jnp.int32)
    grid_index = with_ends(jax.random.randint(splits[2], (NY,), 0, L), jax.random.fold_in(splits[2], 1), 0, L - 1).astype(jnp.int32)
    stretch = jnp.clip(jnp.exp(jax.random.uniform(splits[3], (L, 9), jnp.float32, math.log(0.5), math.log(2.0))), 0.5, 2.0)
    tile_filter = centred(splits[4], (C, 25), 25 ** -0.5, 1.25, (), jnp.float32)
    wall_filter = centred(splits[5], (C, 9), 9 ** -0.5, 2.0, (), jnp.float32)
    class_weight = centred(splits[6], (K, C), C ** -0.5, 1.0, (), jnp.float32)
    return dict(features=features, labels=labels, grid_index=grid_index, stretch=stretch, tile_filter=tile_filter, wall_filter=wall_filter, class_weight=class_weight)


def band_table(grid_index, stretch):
    levels = stretch.shape[0]
    onehot = (grid_index[:, None] == jnp.arange(levels, dtype=jnp.int32)[None, :]).astype(jnp.float32)
    return jnp.dot(onehot, stretch, precision=lax.Precision.HIGHEST)


def channel_forward(field, tile_row, wall_row, bands):
    rows = field.shape[0]
    values = field.astype(jnp.float32)
    smooth = jnp.zeros(values.shape, jnp.float32)
    for i in range(5):
        for j in range(5):
            smooth = smooth + tile_row[5 * i + j] * jnp.roll(values, (2 - i, 2 - j), axis=(1, 2))
    smoothed = smooth.astype(jnp.bfloat16)
    padded = jnp.pad(smoothed.astype(jnp.float32), ((4, 4), (0, 0), (0, 0)))
    wall_out = jnp.zeros(values.shape, jnp.float32)
    for k in range(9):
        tap = wall_row[k] * bands[:, k]
        wall_out = wall_out + tap[:, None, None] * padded[k:k + rows]
    return values, padded, wall_out


def reference(features, labels, grid_index, stretch, tile_filter, wall_filter, class_weight):
    classes = class_weight.shape[0]
    rows = features.shape[1]
    volume = features.shape[1] * features.shape[2] * features.shape[3]
    bands = band_table(grid_index, stretch)
    bands_pad = jnp.pad(bands, ((4, 4), (0, 0)))

    def forward_step(total, items):
        field, tile_row, wall_row, class_col = items
        values, padded, wall_out = channel_forward(field, tile_row, wall_row, bands)
        hidden = wall_out * jax.nn.sigmoid(wall_out)
        return total + class_col[:, None, None, None] * hidden[None], None

    start = jnp.zeros((classes,) + features.shape[1:], jnp.float32)
    scores, unused = lax.scan(forward_step, start, (features, tile_filter, wall_filter, class_weight.T))
    targets = (labels[None] == jnp.arange(classes, dtype=jnp.int32)[:, None, None, None]).astype(jnp.float32)
    errors = scores - targets

    def backward_step(carry, items):
        field, tile_row, wall_row, class_col = items
        values, padded, wall_out = channel_forward(field, tile_row, wall_row, bands)
        sig = jax.nn.sigmoid(wall_out)
        hidden = wall_out * sig
        grad_hidden = jnp.einsum('k,kyxz->yxz', class_col, errors, precision=lax.Precision.HIGHEST)
        grad_wall = (grad_hidden * sig * (1.0 + wall_out * (1.0 - sig))).astype(jnp.bfloat16)
        class_grad = jnp.einsum('kyxz,yxz->k', errors, hidden, precision=lax.Precision.HIGHEST)
        wall_vals = grad_wall.astype(jnp.float32)
        wall_grad = jnp.stack([jnp.sum(wall_vals * bands[:, k][:, None, None] * padded[k:k + rows]) for k in range(9)])
        wall_pad = jnp.pad(wall_vals, ((4, 4), (0, 0), (0, 0)))
        back = jnp.zeros(values.shape, jnp.float32)
        for k in range(9):
            first = 8 - k
            tap = wall_row[k] * bands_pad[first:first + rows, k]
            back = back + tap[:, None, None] * wall_pad[first:first + rows]
        grad_smooth = back.astype(jnp.bfloat16).astype(jnp.float32)
        grad_field = jnp.zeros(values.shape, jnp.float32)
        tile_grad = []
        for i in range(5):
            for j in range(5):
                grad_field = grad_field + tile_row[5 * i + j] * jnp.roll(grad_smooth, (i - 2, j - 2), axis=(1, 2))
                tile_grad.append(jnp.sum(jnp.roll(values, (2 - i, 2 - j), axis=(1, 2)) * grad_smooth))
        return carry, (grad_field.astype(jnp.bfloat16), jnp.stack(tile_grad), wall_grad, class_grad)

    unused, outs = lax.scan(backward_step, jnp.zeros((), jnp.float32), (features, tile_filter, wall_filter, class_weight.T))
    grad_features, tile_grads, wall_grads, class_grads = outs
    return grad_features, tile_grads / volume, wall_grads / volume, class_grads.T / volume
```

```python
import functools

import jax
import jax.numpy as jnp
from jax import lax
from jax.experimental import pallas as pl
from jax.experimental.pallas import tpu as pltpu
from jax.sharding import PartitionSpec as P

F32 = jnp.float32
BF16 = jnp.bfloat16
MESH = pl.DeviceIdType.MESH


def fold(value):
    total = value[0:8]
    for row in range(8, value.shape[0], 8):
        total = total + value[row : row + 8]
    return total


def rounded(value):
    return value.astype(BF16).astype(F32)


def kernel(
    dims,
    feat, labels, bands, tile_w, wall_w, class_w,
    out, tile_out, wall_out, class_out,
    recv, band_pad, halo_out, halo_in, zfeat, smooth, stage, taps, band_rows, hid, slope,
    part_own, part_out, part_in, err, gwall, gsm, ghalo_out, ghalo_in, zgrad, gout, gstage,
    acc, red, sums,
    a_send, a_recv, own_sem, h_send, h_recv, s_send, s_recv, p_send, p_recv, e_send, e_recv,
    w_send, w_recv, g_send, g_recv, o_send, o_recv, r_send, r_recv,
):
    size, depth, cpg, chunks, volume = dims
    per = cpg // chunks
    xs = 2 * size
    xgroups = xs // 8
    everyone = size * depth * 2
    gx, gz, col = lax.axis_index("gx"), lax.axis_index("gz"), lax.axis_index("col")
    me = (gx * depth + gz) * 2 + col
    other = 1 - col
    right, left = lax.rem(gz + 1, depth), lax.rem(gz + depth - 1, depth)
    chan0 = gx * cpg

    def peer(step):
        return lax.rem(gx + step, size)

    def source(step):
        return lax.rem(gx + size - step, size)

    def coords(step):
        index = lax.rem(me + step, everyone)
        return {
            "gx": index // (2 * depth),
            "gz": lax.rem(index // 2, depth),
            "col": lax.rem(index, 2),
        }

    barrier = pltpu.get_barrier_semaphore()

    @pl.loop(1, everyone)
    def _(step):
        pl.semaphore_signal(barrier, inc=1, device_id=coords(step), device_id_type=MESH)

    pl.semaphore_wait(barrier, everyone - 1)

    def remote(src, dst, send, rec, device):
        return pltpu.make_async_remote_copy(
            src_ref=src, dst_ref=dst, send_sem=send, recv_sem=rec,
            device_id=device, device_id_type=MESH,
        )

    def a_copy(chunk, step):
        return remote(
            feat.at[pl.ds(peer(step) * cpg + chunk * per, per)],
            recv.at[step, pl.ds(chunk * per, per)],
            a_send.at[chunk, step], a_recv.at[chunk, step], {"gx": peer(step)},
        )

    def h_copy(way, step):
        return remote(
            halo_out.at[peer(step)], halo_in.at[way, step],
            h_send.at[way, step], h_recv.at[way, step],
            {"gx": peer(step), "gz": right if way == 0 else left},
        )

    own_copy = pltpu.make_async_copy(feat.at[pl.ds(chan0, cpg)], recv.at[0], own_sem)
    own_copy.start()
    for step in range(1, size):
        a_copy(0, step).start()

    lane = lax.broadcasted_iota(jnp.int32, (8, 128), 1)
    quad = lane // 4

    @pl.loop(0, size)
    def _(group):
        for first in range(0, cpg, 4):
            packed = jnp.zeros((8, 128), F32)
            for c in range(first, min(first + 4, cpg)):
                stage[c] = feat[group * cpg + c].astype(F32)
                for xl in range(2):
                    rows = stage[c, pl.ds(xl, 32, stride=2), :]
                    for t in range(4):
                        m = (c - first) * 8 + xl * 4 + t
                        turned = pltpu.roll(rows[8 * t : 8 * t + 8], (2 + 4 * m) % 128, 1)
                        packed = jnp.where(quad == m, turned, packed)
            halo_out[group, pl.ds(first // 4 * 8, 8), :] = packed

    for way in range(2):
        for step in range(size):
            h_copy(way, step).start()
    for chunk in range(1, chunks):
        for step in range(1, size):
            a_copy(chunk, step).start()

    band_pad[0:8] = jnp.zeros((8, 9), F32)
    band_pad[8:72] = bands[...]
    band_pad[72:80] = jnp.zeros((8, 9), F32)
    for k in range(9):
        band_rows[k] = jnp.broadcast_to(band_pad[pl.ds(32 * col, 48), k : k + 1], (48, 128))

    @pl.loop(0, cpg)
    def _(c):
        for k in range(9):
            taps[c, k] = wall_w[k, chan0 + c] * band_rows[k]
        for x_group in range(0, xs, 8):
            blank = jnp.zeros((8, 8, 128), F32)
            smooth[c, pl.ds(x_group, 8), pl.ds(pl.multiple_of(40 * col, 8), 8), :] = blank
            gwall[c, pl.ds(x_group, 8), pl.ds(pl.multiple_of(40 * col, 8), 8), :] = blank
        for q in range(40):
            acc[c, q] = jnp.zeros((8, 128), F32)

    red[...] = jnp.zeros((128, 128), F32)

    def shifts(value, edge):
        return (
            pltpu.roll(jnp.where(lane >= 126, edge, value), 2, 1),
            pltpu.roll(jnp.where(lane == 127, edge, value), 1, 1),
            value,
            pltpu.roll(jnp.where(lane == 0, edge, value), 127, 1),
            pltpu.roll(jnp.where(lane < 2, edge, value), 126, 1),
        )

    def filtered(field, c, x, flip):
        total = None
        for i in range(5):
            at = lax.rem(x + (4 - i if flip else i) - 2 + xs, xs)
            for j in range(5):
                term = tile_w[chan0 + c, 5 * i + j] * field[4 - j if flip else j, c, at]
                total = term if total is None else total + term
        return total

    def y_copy(ref, index, send, rec):
        src = pl.multiple_of(32 - 24 * col, 8)
        dst = pl.multiple_of(40 * col, 8)
        return remote(
            ref.at[index + (pl.ds(src, 8),)], ref.at[index + (pl.ds(dst, 8),)],
            send, rec, {"col": other},
        )

    def s_copy(c):
        return y_copy(smooth, (c, pl.ds(0, xs)), s_send.at[c], s_recv.at[c])

    own_copy.wait()
    for way in range(2):
        for step in range(size):
            h_copy(way, step).wait_recv()

    def edges_of(ref_left, ref_right):
        return jnp.where(lax.rem(lane, 4) < 2, ref_left, ref_right)

    for chunk in range(chunks):
        for step in range(1, size):
            a_copy(chunk, step).wait_recv()
        for c in range(chunk * per, chunk * per + per):

            @pl.loop(0, size, unroll=2)
            def _(step, c=c):
                s = source(step)
                stage[step] = recv[step, c].astype(F32)
                at = pl.ds(c // 4 * 8, 8)
                packed = edges_of(halo_in[0, step, at, :], halo_in[1, step, at, :])
                for xl in range(2):
                    rows = stage[step, pl.ds(xl, 32, stride=2), :]
                    for t in range(4):
                        m = c % 4 * 8 + xl * 4 + t
                        edge = pltpu.roll(packed, (126 - 4 * m) % 128, 1)
                        moved = shifts(rows[8 * t : 8 * t + 8], edge)
                        for j in range(5):
                            zfeat[j, c, 2 * s + xl, pl.ds(8 * t, 8), :] = moved[j]

            @pl.loop(0, xs, unroll=4)
            def _(x, c=c):
                smooth[c, x, pl.ds(8, 32), :] = rounded(filtered(zfeat, c, x, False))

            s_copy(c).start()

    for c in range(cpg):
        s_copy(c).wait_recv()

    def p_copy(step):
        return remote(
            part_out.at[step], part_in.at[step], p_send.at[step], p_recv.at[step],
            {"gx": peer(step)},
        )

    def scores_at(x):
        def body(c, totals):
            wall = None
            for k in range(9):
                term = taps[c, k, pl.ds(8, 32), :] * smooth[c, x, pl.ds(4 + k, 32), :]
                wall = term if wall is None else wall + term
            sig = jax.nn.sigmoid(wall)
            hidden = wall * sig
            hid[c, x] = hidden
            slope[c, x] = sig * (1.0 + wall * (1.0 - sig))
            return tuple(
                total + class_w[k, chan0 + c] * hidden for k, total in enumerate(totals)
            )

        return lax.fori_loop(
            0, cpg, body, tuple(jnp.zeros((32, 128), F32) for k in range(4)), unroll=min(4, cpg)
        )

    @pl.loop(1, size)
    def _(step):
        for xl in range(2):
            totals = scores_at(2 * peer(step) + xl)
            for k in range(4):
                part_out[step, pl.ds((2 * k + xl) * 32, 32), :] = totals[k].astype(BF16)
        p_copy(step).start()

    for xl in range(2):
        totals = scores_at(2 * gx + xl)
        for k in range(4):
            part_own[pl.ds((2 * k + xl) * 32, 32), :] = totals[k]

    @pl.loop(1, size)
    def _(step):
        p_copy(step).wait_recv()
        part_own[...] = part_own[...] + part_in[step].astype(F32)

    for xl in range(2):
        marks = labels[pl.ds(64 * col + xl, 32, stride=2), :]
        for k in range(4):
            at = pl.ds((2 * k + xl) * 32, 32)
            err[0, at, :] = (part_own[at, :] - jnp.where(marks == k, 1.0, 0.0)).astype(BF16)

    def e_copy(step):
        return remote(
            err.at[0], err.at[step], e_send.at[step], e_recv.at[step], {"gx": peer(step)}
        )

    for step in range(1, size):
        e_copy(step).start()

    def w_copy(step):
        return y_copy(
            gwall, (pl.ds(0, cpg), pl.ds(2 * source(step), 2)), w_send.at[step], w_recv.at[step]
        )

    def wall_grads(step):
        for xl in range(2):
            x = 2 * source(step) + xl
            errors = [err[step, pl.ds((2 * k + xl) * 32, 32), :].astype(F32) for k in range(4)]

            @pl.loop(0, cpg, unroll=min(4, cpg))
            def _(c):
                hidden = hid[c, x]
                grad = None
                for k in range(4):
                    term = class_w[k, chan0 + c] * errors[k]
                    grad = term if grad is None else grad + term
                    acc[c, 34 + k] = acc[c, 34 + k] + fold(errors[k] * hidden)
                gwall[c, x, pl.ds(8, 32), :] = rounded(grad * slope[c, x])

        w_copy(step).start()

    wall_grads(0)

    @pl.loop(1, size)
    def _(step):
        e_copy(step).wait_recv()
        wall_grads(step)

    @pl.loop(0, size)
    def _(step):
        w_copy(step).wait_recv()

    def g_copy(way, c):
        return remote(
            ghalo_out.at[c], ghalo_in.at[way, c], g_send.at[way, c], g_recv.at[way, c],
            {"gz": right if way == 0 else left},
        )

    @pl.loop(0, cpg)
    def _(c):
        def body(x, sums9):
            grad = gwall[c, x, pl.ds(8, 32), :]
            total = None
            news = []
            for k in range(9):
                term = taps[c, k, pl.ds(12 - k, 32), :] * gwall[c, x, pl.ds(12 - k, 32), :]
                total = term if total is None else total + term
                product = grad * band_rows[k, pl.ds(8, 32), :] * smooth[c, x, pl.ds(4 + k, 32), :]
                news.append(sums9[k] + fold(product))
            gsm[c, x] = rounded(total)
            return tuple(news)

        sums9 = lax.fori_loop(0, xs, body, tuple(jnp.zeros((8, 128), F32) for k in range(9)), unroll=2)
        for k in range(9):
            acc[c, 25 + k] = sums9[k]

        @pl.loop(0, xgroups)
        def _(group):
            packed = jnp.zeros((8, 128), F32)
            for m in range(32):
                piece = gsm[c, group * 8 + m // 4, pl.ds(m % 4 * 8, 8), :]
                packed = jnp.where(quad == m, pltpu.roll(piece, (2 + 4 * m) % 128, 1), packed)
            ghalo_out[c, group] = packed

        for way in range(2):
            g_copy(way, c).start()

    def o_copy(chunk, step):
        return remote(
            gout.at[peer(step), pl.ds(chunk * per, per)],
            out.at[pl.ds(chan0 + chunk * per, per)],
            o_send.at[chunk, step], o_recv.at[chunk, step], {"gx": peer(step)},
        )

    @pl.loop(0, chunks)
    def _(chunk):
        @pl.loop(0, per)
        def _(lower):
            c = chunk * per + lower
            for way in range(2):
                g_copy(way, c).wait_recv()

            @pl.loop(0, xgroups)
            def _(group):
                packed = edges_of(ghalo_in[0, c, group], ghalo_in[1, c, group])
                for m in range(32):
                    at = pl.ds(m % 4 * 8, 8)
                    x = group * 8 + m // 4
                    edge = pltpu.roll(packed, (126 - 4 * m) % 128, 1)
                    moved = shifts(gsm[c, x, at, :], edge)
                    for j in range(5):
                        zgrad[j, c, x, at, :] = moved[j]

            @pl.loop(0, size, unroll=2)
            def _(s):
                for xl in range(2):
                    gstage[s, pl.ds(xl, 32, stride=2), :] = filtered(zgrad, c, 2 * s + xl, True)
                gout[s, c] = gstage[s].astype(BF16)

            out[chan0 + c] = gout[gx, c]

        for step in range(1, size):
            o_copy(chunk, step).start()

    row = lax.broadcasted_iota(jnp.int32, (8, 128), 0)

    @pl.loop(0, cpg)
    def _(c):
        def body(x, sums25):
            grad = gsm[c, x]
            news = []
            for i in range(5):
                at = lax.rem(x + i - 2 + xs, xs)
                for j in range(5):
                    news.append(sums25[5 * i + j] + fold(zfeat[j, c, at] * grad))
            return tuple(news)

        sums25 = lax.fori_loop(0, xs, body, tuple(jnp.zeros((8, 128), F32) for q in range(25)), unroll=2)
        for q in range(38):
            value = sums25[q] if q < 25 else acc[c, q]
            red[pl.ds(q, 1), :] = jnp.sum(value, axis=0, keepdims=True)
        line = lax.dot_general(
            jnp.ones((8, 128), F32), red[...], (((1,), (1,)), ((), ())),
            precision=lax.Precision.HIGHEST, preferred_element_type=F32,
        )
        before = jnp.where(c == 0, jnp.zeros((8, 128), F32), sums[me])
        sums[me] = jnp.where(row == c, line, before)

    def r_copy(step):
        return remote(sums.at[me], sums.at[me], r_send.at[step], r_recv.at[step], coords(step))

    @pl.loop(1, everyone)
    def _(step):
        r_copy(step).start()

    @pl.loop(1, everyone)
    def _(step):
        r_copy(step).wait_recv()

    @pl.loop(0, size)
    def _(group):
        total = sums[group * depth * 2]
        for member in range(1, depth * 2):
            total = total + sums[group * depth * 2 + member]
        red[pl.ds(group * cpg, cpg), :] = total[0:cpg] / volume

    turned = red[...].T
    chans = size * cpg
    tile_out[...] = red[0:chans, 0:25]
    wall_out[...] = turned[25:34, 0:chans]
    class_out[...] = turned[34:38, 0:chans]

    for chunk in range(chunks):
        for step in range(1, size):
            o_copy(chunk, step).wait()
            a_copy(chunk, step).wait_send()
    for way in range(2):
        for step in range(size):
            h_copy(way, step).wait_send()
        for c in range(cpg):
            g_copy(way, c).wait_send()
    for c in range(cpg):
        s_copy(c).wait_send()
    for step in range(1, size):
        p_copy(step).wait_send()
        e_copy(step).wait_send()
    for step in range(size):
        w_copy(step).wait_send()

    @pl.loop(1, everyone)
    def _(step):
        r_copy(step).wait_send()


OWN = 32
WIN = OWN + 8
BLOCK = 12
BLOCKS = (WIN - 4) // BLOCK
ROWS = BLOCK * 8
HALF = ROWS // 2
PIECES = ((0, 2), (2, 6), (8, 6), (14, 4), (18, 2))
ARRIVE = ((0, 1), (2,), (3, 4))
WANTED = 38
HIGH = lax.Precision.HIGHEST


def dot(a, b, dims=((1,), (0,))):
    return lax.dot_general(a, b, (dims, ((), ())), precision=HIGH, preferred_element_type=F32)


def region_kernel(
    dims,
    feat_h, lab_h, index_h, stretch_h, tile_h, wall_h, class_h,
    out, tile_out, wall_out, class_out,
    feat, lab, index, stretch, tile_w, wall_w, class_w,
    turn, send, recv, lab_rows, lab_send, lab_recv, lab_wide, lab_win,
    field, odd, smooth, gwall, gsm, godd, hid, slope, part_out, part_in,
    taps, fore, back, band_back, wall_acc, acc, gram, params, classes, classes_t,
    gout, ghome, sums, red,
    in_sem, f_send, f_recv, l_send, l_recv, p_send, p_recv, g_send, g_recv, r_send, r_recv,
):
    size, depth, volume = dims
    everyone = size * depth * 2
    gx, gz, col = lax.axis_index("gx"), lax.axis_index("gz"), lax.axis_index("col")
    me = (gx * depth + gz) * 2 + col
    right, left = lax.rem(gz + 1, depth), lax.rem(gz + depth - 1, depth)
    zps = OWN // 2
    lane = lax.broadcasted_iota(jnp.int32, (8, 128), 1)
    row = lax.broadcasted_iota(jnp.int32, (8, 128), 0)
    first = lane < 64
    y_lane = lax.rem(lane, 64) // 2
    x_even = lax.rem(lane, 2) == 0

    ins = [
        pltpu.make_async_copy(src, dst, in_sem.at[n])
        for n, (src, dst) in enumerate((
            (feat_h, feat), (lab_h, lab), (index_h, index), (stretch_h, stretch),
            (tile_h, tile_w), (wall_h, wall_w), (class_h, class_w),
        ))
    ]
    for copy in ins:
        copy.start()

    def coords(step):
        place = lax.rem(me + step, everyone)
        return {
            "gx": place // (2 * depth),
            "gz": lax.rem(place // 2, depth),
            "col": lax.rem(place, 2),
        }

    barrier = pltpu.get_barrier_semaphore()

    @pl.loop(1, everyone)
    def _(step):
        pl.semaphore_signal(barrier, inc=1, device_id=coords(step), device_id_type=MESH)

    def remote(src, dst, sent, got, device):
        return pltpu.make_async_remote_copy(
            src_ref=src, dst_ref=dst, send_sem=sent, recv_sem=got,
            device_id=device, device_id_type=MESH,
        )

    def target(sx):
        return lax.rem(gx + sx, size)

    def origin(sx):
        return lax.rem(gx + size - sx, size)

    ins[0].wait()
    for side in range(2):
        for cp in range(8):
            block = feat[pl.ds(side * 16 + 2 * cp, 2)].astype(F32).reshape(128, 128)
            turn[side, pl.ds(cp, 128, stride=8), :] = block.T

        @pl.loop(0, 64, unroll=8)
        def _(zp, side=side):
            at = pl.ds(pl.multiple_of(zp * 16, 16), 16)
            send[side, zp] = turn[side, at, :].astype(BF16)

    ins[1].wait()
    turn[2, 0:128, :] = lab[...].astype(F32).T
    even, uneven = turn[2, pl.ds(0, 64, stride=2), :], turn[2, pl.ds(1, 64, stride=2), :]
    here = jnp.where(col == 0, even, pltpu.roll(even, 64, 1))
    there = jnp.where(col == 0, pltpu.roll(uneven, 64, 1), uneven)
    lab_rows[...] = jnp.where(lax.broadcasted_iota(jnp.int32, (64, 128), 1) < 64, here, there)
    for t in range(size):
        lab_send[t] = lab_rows[pl.ds(zps * t, zps), :].astype(BF16)
    edge_rows = [jnp.zeros((1, 128), F32)] * 16
    for t in range(size):
        edge_rows[2 * t] = lab_rows[pl.ds((zps * t - 1) % 64, 1), :]
        edge_rows[2 * t + 1] = lab_rows[pl.ds((zps * t + zps) % 64, 1), :]
    lab_send[size] = jnp.concatenate(edge_rows, axis=0).astype(BF16)

    pl.semaphore_wait(barrier, everyone - 1)

    def f_spot(piece, t):
        at, count = PIECES[piece]
        return pl.ds(lax.rem(t * zps + at - 2 + 64, 64), count), pl.ds(at, count)

    def f_far(piece, sx, sc):
        t, ct = target(sx), lax.rem(col + sc, 2)
        src, dst = f_spot(piece, t)
        if piece == 0:
            tz = lax.rem(gz + 1 - (t + size - 1) // size, depth)
        elif piece == len(PIECES) - 1:
            tz = lax.rem(gz + depth - (t + 1) // size, depth)
        else:
            tz = gz
        return remote(
            send.at[ct, src], recv.at[gx, col, dst],
            f_send.at[piece, sx, sc], f_recv.at[piece, sx, sc],
            {"gx": t, "gz": tz, "col": ct},
        )

    def f_near(piece):
        src, dst = f_spot(piece, gx)
        return pltpu.make_async_copy(
            send.at[col, src], recv.at[gx, col, dst], f_recv.at[piece, 0, 0]
        )

    def f_wait(piece, sx, sc):
        at, count = PIECES[piece]
        slot = recv.at[origin(sx), lax.rem(col + sc, 2), pl.ds(at, count)]
        return remote(
            slot, slot, f_send.at[piece, sx, sc], f_recv.at[piece, sx, sc],
            {"gx": target(sx), "gz": gz, "col": lax.rem(col + sc, 2)},
        )

    def own_piece(piece, near, far):
        if piece == 0:
            pl.when(gx > 0)(near)
            pl.when(gx == 0)(far)
        elif piece == len(PIECES) - 1:
            pl.when(gx < size - 1)(near)
            pl.when(gx == size - 1)(far)
        else:
            near()

    others = [(sx, sc) for sx in (2, 1, 3, 0) for sc in range(2) if sx or sc]

    def l_mid(sx):
        return remote(
            lab_send.at[target(sx)], lab_recv.at[gx, 0], l_send.at[0, sx], l_recv.at[0, sx],
            {"gx": target(sx)},
        )

    def l_edge(sx):
        return remote(
            lab_send.at[size], lab_recv.at[gx, 1], l_send.at[1, sx], l_recv.at[1, sx],
            {"gx": target(sx)},
        )

    def l_far(sx):
        t = target(sx)
        tz = lax.rem(gz + depth + 1 - 2 * ((t + 1) // size), depth)
        return remote(
            lab_send.at[size], lab_recv.at[gx, 2], l_send.at[2, sx], l_recv.at[2, sx],
            {"gx": t, "gz": tz},
        )

    l_own = [
        pltpu.make_async_copy(lab_send.at[gx], lab_recv.at[gx, 0], l_recv.at[0, 0]),
        pltpu.make_async_copy(lab_send.at[size], lab_recv.at[gx, 1], l_recv.at[1, 0]),
    ]

    for block in range(BLOCKS):
        for piece in ARRIVE[block]:
            for sx, sc in others:
                f_far(piece, sx, sc).start()
            own_piece(
                piece,
                lambda piece=piece: f_near(piece).start(),
                lambda piece=piece: f_far(piece, 0, 0).start(),
            )
        if block == 0:
            for copy in l_own:
                copy.start()
            for sx in range(size):
                if sx:
                    l_mid(sx).start()
                    l_edge(sx).start()
                l_far(sx).start()

    for copy in ins[2:]:
        copy.wait()
    params[...] = jnp.zeros((128, 128), F32)
    params[0:9, 0:32] = wall_w[...]
    params[16:20, 0:32] = class_w[...]
    params[64:96, 0:25] = tile_w[...]
    red[...] = params[...].T

    def pairs(ref, start):
        return ref[pl.ds(start + col * 16, 8, stride=2), :], ref[pl.ds(start + col * 16 + 1, 8, stride=2), :]

    def spread(both, q):
        low, high = (jnp.broadcast_to(rows[:, q : q + 1], (8, 128)) for rows in both)
        return jnp.where(first, low, high)

    tile_pairs, wall_pairs = pairs(params, 64), pairs(red, 0)
    for q in range(25):
        taps[q] = spread(tile_pairs, q)

    levels = stretch.shape[0]
    hot = lax.broadcasted_iota(jnp.int32, (levels, 64), 0) == index[...]
    params[32:41, 0:64] = dot(stretch[...], hot.astype(F32), ((0,), (0,)))
    band_t = params[32:48, 0:64]
    y_row = lax.broadcasted_iota(jnp.int32, (64, 128), 0)
    y_col = lax.rem(lax.broadcasted_iota(jnp.int32, (64, 128), 1), 64) // 2
    for yh in range(2):
        ahead = dot(band_t, (y_row == y_col + 32 * yh).astype(F32))
        for k in range(9):
            m = k - 4
            weight = spread(wall_pairs, k)
            inside = (y_lane + (32 * yh + m) >= 0) & (y_lane + (32 * yh + m) < 64)
            fore[k, yh] = jnp.where(inside, weight * ahead[k : k + 1, :], 0.0)
            behind = dot(band_t, (y_row == y_col + (32 * yh - m)).astype(F32))
            band_back[k, yh] = jnp.broadcast_to(behind[k : k + 1, :], (8, 128))
            back[k, yh] = weight * band_back[k, yh]
            wall_acc[k, yh] = jnp.zeros((8, 128), F32)

    chan = lax.broadcasted_iota(jnp.int32, (128, 128), 0)
    unit = lax.rem(lax.broadcasted_iota(jnp.int32, (128, 128), 1), 8)
    half_row = lax.broadcasted_iota(jnp.int32, (HALF, 128), 0)
    half_z = lax.broadcasted_iota(jnp.int32, (HALF, 128), 1) // 8
    half_k = lax.rem(half_row, 8) // 2
    same_z = (half_row // 8) * 2 + lax.rem(half_row, 2) == half_z
    classes[...] = jnp.zeros((128, 128), F32)
    for par in range(2):
        rows = dot(params[16:24, :], (chan == col * 16 + 2 * unit + par).astype(F32))
        value = jnp.zeros((HALF, 128), F32)
        for k in range(4):
            value = jnp.where(same_z & (half_k == k), rows[k : k + 1, :], value)
        classes[pl.ds(HALF * par, HALF), :] = value
    classes_t[...] = classes[...].T

    def arrived(block):
        for piece in ARRIVE[block]:
            for sx, sc in others:
                f_wait(piece, sx, sc).wait_recv()
            own_piece(
                piece,
                lambda piece=piece: f_near(piece).wait(),
                lambda piece=piece: f_wait(piece, 0, 0).wait_recv(),
            )
        low, high = PIECES[ARRIVE[block][0]][0], sum(PIECES[ARRIVE[block][-1]])

        @pl.loop(0, 2 * size)
        def _(t):
            for zp in range(low, high):
                pair = recv[t // 2, lax.rem(t, 2), zp].astype(F32)
                field[t, 2 * zp] = pair[0:8]
                field[t, 2 * zp + 1] = pair[8:16]

        between(field, odd, 2 * low, 2 * high)

    def between(src, dst, low, high):
        @pl.loop(0, 2 * size)
        def _(t):
            after = lax.rem(t + 2, 2 * size)
            for z in range(low, high):
                dst[t, z] = jnp.where(
                    x_even, pltpu.roll(src[t, z], 127, 1), pltpu.roll(src[after, z], 1, 1)
                )

    def filtered(src, mid, t, low, count, flip, put):
        before, after = lax.rem(t + 2 * size - 2, 2 * size), lax.rem(t + 2, 2 * size)
        totals = [None] * count
        for z in range(count + 4):
            at = low + z - 2
            views = (src[before, at], mid[before, at], src[t, at], mid[t, at], src[after, at])
            for j in range(5):
                if 0 <= z - j < count:
                    for i in range(5):
                        q = 5 * (4 - i) + 4 - j if flip else 5 * i + j
                        term = taps[q] * views[i]
                        old = totals[z - j]
                        totals[z - j] = term if old is None else old + term
            if z >= 4:
                put(z - 4, totals)

    def moved(low, high, low_turned, high_turned, m):
        if m == 0:
            return low, high
        if m > 0:
            mixed = jnp.where(y_lane < m, high_turned, low)
            return pltpu.roll(mixed, 128 - 2 * m, 1), pltpu.roll(high, 128 - 2 * m, 1)
        mixed = jnp.where(y_lane >= 32 + m, low_turned, high)
        return pltpu.roll(low, -2 * m, 1), pltpu.roll(mixed, -2 * m, 1)

    def p_copy(block):
        return remote(
            part_out.at[block], part_in.at[block], p_send.at[block], p_recv.at[block],
            {"col": 1 - col},
        )

    def ahead_of(block):
        base = 2 + BLOCK * block

        @pl.loop(0, 2 * size)
        def _(t):
            def put(z, totals):
                smooth[t, base + z] = rounded(totals[z])

            filtered(field, odd, t, base, BLOCK, False, put)

        @pl.loop(0, BLOCK)
        def _(z):
            at = pl.ds(pl.multiple_of(8 * z, 8), 8)
            for p in range(size):
                low, high = smooth[2 * p, base + z], smooth[2 * p + 1, base + z]
                turned = pltpu.roll(low, 64, 1), pltpu.roll(high, 64, 1)
                walls = [None, None]
                for k in range(9):
                    pair = moved(low, high, *turned, k - 4)
                    for yh in range(2):
                        term = fore[k, yh] * pair[yh]
                        walls[yh] = term if walls[yh] is None else walls[yh] + term
                for yh, wall in enumerate(walls):
                    sig = jax.nn.sigmoid(wall)
                    lanes = slice(128 * yh, 128 * yh + 128)
                    hid[block, p, at, lanes] = wall * sig
                    slope[block, p, at, lanes] = sig * (1.0 + wall * (1.0 - sig))

        left_half = lax.rem(lax.broadcasted_iota(jnp.int32, (HALF, 256), 1), 128) < 64

        @pl.loop(0, size)
        def _(p):
            part = dot(classes[0:ROWS, 0:ROWS], hid[block, p])
            part_out[block, p] = jnp.where(left_half, part[0:HALF], part[HALF:ROWS])
            lanes = pl.ds(pl.multiple_of(128 * col, 128), 128)
            for zp in range(BLOCK // 2):
                at = slice(8 * zp, 8 * zp + 8)
                mark = lab_win[p, pl.ds(BLOCK // 2 * block + zp, 1), :]
                mark = jnp.broadcast_to(mark, (8, 128))
                mark = jnp.where(lax.rem(row, 2) == 0, mark, pltpu.roll(mark, 64, 1))
                hit = first & (mark == (row // 2).astype(F32))
                part_out[block, p, at, lanes] = part_out[block, p, at, lanes] - jnp.where(hit, 1.0, 0.0)

        p_copy(block).start()

    def back_of(block):
        base = 2 + BLOCK * block
        p_copy(block).wait_recv()
        left_half = lax.rem(lax.broadcasted_iota(jnp.int32, (HALF, 256), 1), 128) < 64

        @pl.loop(0, size)
        def _(p):
            err = part_out[block, p] + part_in[block, p]
            swapped = jnp.concatenate(
                [pltpu.roll(err[:, 0:128], 64, 1), pltpu.roll(err[:, 128:256], 64, 1)], axis=1
            )
            err = err + swapped
            both = jnp.concatenate(
                [jnp.where(left_half, err, 0.0), jnp.where(left_half, 0.0, err)], axis=0
            )
            grad = dot(classes_t[0:ROWS, 0:ROWS], both) * slope[block, p]
            for z in range(BLOCK):
                for yh in range(2):
                    gwall[2 * p + yh, base + z] = rounded(
                        grad[8 * z : 8 * z + 8, 128 * yh : 128 * yh + 128]
                    )
            new = dot(both, hid[block, p], ((1,), (1,)))
            gram[block, p] = new

        @pl.loop(0, BLOCK)
        def _(z):
            own = (base + z >= 4) & (base + z < 4 + OWN)
            sums9 = [[None, None] for k in range(9)]
            for p in range(size):
                low, high = gwall[2 * p, base + z], gwall[2 * p + 1, base + z]
                turned = pltpu.roll(low, 64, 1), pltpu.roll(high, 64, 1)
                fields = [
                    jnp.where(own, smooth[2 * p + yh, base + z], 0.0) for yh in range(2)
                ]
                totals = [None, None]
                for k in range(9):
                    pair = moved(low, high, *turned, 4 - k)
                    for yh in range(2):
                        term = back[k, yh] * pair[yh]
                        totals[yh] = term if totals[yh] is None else totals[yh] + term
                        term = pair[yh] * fields[yh]
                        old = sums9[k][yh]
                        sums9[k][yh] = term if old is None else old + term
                for yh in range(2):
                    gsm[2 * p + yh, base + z] = rounded(totals[yh])
            for k in range(9):
                for yh in range(2):
                    wall_acc[k, yh] = wall_acc[k, yh] + sums9[k][yh]

        between(gsm, godd, base, base + BLOCK)

    def g_spot(block):
        low = 4 if block == 0 else BLOCK * block
        return low, BLOCK * block + BLOCK - low

    def g_copy(block, step):
        low, count = g_spot(block)
        at, many = (low - 4) // 2, count // 2
        p, yh = target(step // 2), lax.rem(col + step, 2)
        return remote(
            gout.at[2 * p + yh, pl.ds(at, many)],
            ghome.at[col, pl.ds(gx * zps + at, many)],
            g_send.at[block, step], g_recv.at[block, step], {"gx": p, "col": yh},
        )

    def g_near(block):
        low, count = g_spot(block)
        at, many = (low - 4) // 2, count // 2
        return pltpu.make_async_copy(
            gout.at[2 * gx + col, pl.ds(at, many)],
            ghome.at[col, pl.ds(gx * zps + at, many)],
            g_recv.at[block, 0],
        )

    def g_wait(block, step):
        low, count = g_spot(block)
        at, many = (low - 4) // 2, count // 2
        slot = ghome.at[lax.rem(col + step, 2), pl.ds(origin(step // 2) * zps + at, many)]
        return remote(
            slot, slot, g_send.at[block, step], g_recv.at[block, step],
            {"gx": target(step // 2), "col": lax.rem(col + step, 2)},
        )

    def home(block):
        low, count = g_spot(block)

        @pl.loop(0, 2 * size)
        def _(turn_at):
            step = lax.rem(turn_at + 4, 2 * size)
            t = 2 * target(step // 2) + lax.rem(col + step, 2)

            def put(z, totals):
                if z % 2:
                    pair = jnp.concatenate([totals[z - 1], totals[z]], axis=0)
                    gout[t, (low - 4 + z) // 2] = pair.astype(BF16)

            filtered(gsm, godd, t, low, count, True, put)

            @pl.when(step > 0)
            def _():
                g_copy(block, step).start()

            @pl.when(step == 0)
            def _():
                g_near(block).start()

    def labels_in():
        for sx in range(size):
            if sx:
                for slot in range(2):
                    at = lab_recv.at[origin(sx), slot]
                    remote(
                        at, at, l_send.at[slot, sx], l_recv.at[slot, sx], {"gx": target(sx)}
                    ).wait_recv()
            at = lab_recv.at[origin(sx), 2]
            remote(
                at, at, l_send.at[2, sx], l_recv.at[2, sx], {"gx": target(sx), "gz": right}
            ).wait_recv()
        for copy in l_own:
            copy.wait()
        low_edge = 2 - (gx + size - 1) // size
        high_edge = 1 + (gx + 1) // size
        for p in range(size):
            lab_win[p, 1 : 1 + zps, :] = lab_recv[p, 0].astype(F32)
            for slot in range(1, 3):
                lab_wide[p, slot] = lab_recv[p, slot].astype(F32)
            lab_win[p, 0:1, :] = lab_wide[p, low_edge, pl.ds(2 * gx, 1), :]
            lab_win[p, 1 + zps : 2 + zps, :] = lab_wide[p, high_edge, pl.ds(2 * gx + 1, 1), :]

    arrived(0)
    labels_in()
    ahead_of(0)
    arrived(1)
    ahead_of(1)
    back_of(0)
    home(0)
    arrived(2)
    ahead_of(2)
    back_of(1)
    home(1)
    back_of(2)
    home(2)

    def tile_body(it, sums25):
        t, base = it // 4, 4 + 8 * lax.rem(it, 4)
        before, after = lax.rem(t + 2 * size - 2, 2 * size), lax.rem(t + 2, 2 * size)
        grads = [gsm[t, base + z] for z in range(8)]
        news = list(sums25)
        for z in range(12):
            at = base + z - 2
            views = (
                field[before, at], odd[before, at], field[t, at], odd[t, at], field[after, at]
            )
            for j in range(5):
                if 0 <= z - j < 8:
                    for i in range(5):
                        news[5 * i + j] = news[5 * i + j] + views[i] * grads[z - j]
        return tuple(news)

    sums25 = lax.fori_loop(
        0, 8 * size, tile_body, tuple(jnp.zeros((8, 128), F32) for q in range(25))
    )
    for q in range(25):
        acc[8 * q : 8 * q + 8, :] = sums25[q]
    for k in range(9):
        q = 25 + k
        acc[8 * q : 8 * q + 8, :] = (
            wall_acc[k, 0] * band_back[k, 0] + wall_acc[k, 1] * band_back[k, 1]
        )
    halves = lax.broadcasted_iota(jnp.int32, (128, 128), 0) // 64
    parity = lax.rem(lax.broadcasted_iota(jnp.int32, (128, 128), 1), 2)
    lines = dot(acc[...], (halves == parity).astype(F32))
    total = jnp.zeros((8, 128), F32)
    for q in range(34):
        total = jnp.where(lane // 2 == q, lines[8 * q : 8 * q + 8, :], total)

    full_row = lax.broadcasted_iota(jnp.int32, (ROWS, ROWS), 0)
    full_lane = lax.broadcasted_iota(jnp.int32, (ROWS, ROWS), 1)
    row_z = lax.rem(full_row, HALF) // 8 * 2 + lax.rem(full_row, 2)
    matrix = jnp.zeros((ROWS, ROWS), F32)
    for block in range(BLOCKS):
        base = 2 + BLOCK * block
        value = gram[block, 0]
        for p in range(1, size):
            value = value + gram[block, p]
        keep = (row_z == full_lane // 8) & (row_z + base >= 4) & (row_z + base < 4 + OWN)
        matrix = matrix + jnp.where(keep, value, 0.0)
    gather = (
        lax.broadcasted_iota(jnp.int32, (8, ROWS), 0)
        == lax.rem(lax.broadcasted_iota(jnp.int32, (8, ROWS), 1), 8)
    ).astype(F32)
    by_row = dot(gather, matrix, ((1,), (1,)))
    source_row = lax.broadcasted_iota(jnp.int32, (ROWS, 128), 0)
    place = 2 * (34 + lax.rem(source_row, 8) // 2) + source_row // HALF
    place = place == lax.broadcasted_iota(jnp.int32, (ROWS, 128), 1)
    sums[me] = total + dot(by_row, place.astype(F32))

    def r_copy(step):
        return remote(sums.at[me], sums.at[me], r_send.at[step], r_recv.at[step], coords(step))

    @pl.loop(1, everyone)
    def _(step):
        r_copy(step).start()

    for block in range(BLOCKS):
        for step in range(1, 2 * size):
            g_wait(block, step).wait_recv()
        g_near(block).wait()

    for side in range(2):
        @pl.loop(0, 64, unroll=8)
        def _(zp, side=side):
            at = pl.ds(pl.multiple_of(zp * 16, 16), 16)
            turn[side, at, :] = ghome[side, zp].astype(F32)

        for cp in range(8):
            block = turn[side, pl.ds(cp, 128, stride=8), :].T
            out[pl.ds(side * 16 + 2 * cp, 2)] = block.reshape(2, 64, 128).astype(BF16)

    def r_wait(step):
        place = lax.rem(me + everyone - step, everyone)
        return remote(
            sums.at[place], sums.at[place], r_send.at[step], r_recv.at[step], coords(step)
        )

    @pl.loop(1, everyone)
    def _(step):
        r_wait(step).wait_recv()

    spot = lax.broadcasted_iota(jnp.int32, (128, 128), 0)
    want = 2 * lax.broadcasted_iota(jnp.int32, (128, 128), 1)
    red[...] = jnp.zeros((128, 128), F32)
    for side in range(2):
        total = sums[side]
        for member in range(1, size * depth):
            total = total + sums[2 * member + side]
        total = total / volume
        for par in range(2):
            red[pl.ds(side * 16 + par, 8, stride=2), :] = dot(total, (spot == want + par).astype(F32))
    turned = red[...].T
    tile_out[...] = red[0:32, 0:25]
    wall_out[...] = turned[25:34, 0:32]
    class_out[...] = turned[34:38, 0:32]

    for piece in range(len(PIECES)):
        for sx, sc in others:
            f_far(piece, sx, sc).wait_send()
    pl.when(gx == 0)(lambda: f_far(0, 0, 0).wait_send())
    pl.when(gx == size - 1)(lambda: f_far(len(PIECES) - 1, 0, 0).wait_send())
    for sx in range(size):
        if sx:
            l_mid(sx).wait_send()
            l_edge(sx).wait_send()
        l_far(sx).wait_send()
    for block in range(BLOCKS):
        p_copy(block).wait_send()
        for step in range(1, 2 * size):
            g_copy(block, step).wait_send()

    @pl.loop(1, everyone)
    def _(step):
        r_copy(step).wait_send()


def regional(
    size, depth, volume,
    features, labels, grid_index, stretch, tile_filter, wall_filter, class_weight,
):
    chans = features.shape[0]
    levels = stretch.shape[0]
    everyone = size * depth * 2
    dma = pltpu.SemaphoreType.DMA
    vmem = pl.BlockSpec(memory_space=pltpu.VMEM)
    far = pl.BlockSpec(memory_space=pl.ANY)
    wide = pltpu.VMEM((2 * size, WIN, 8, 128), F32)
    block = pltpu.VMEM((BLOCKS, size, ROWS, 256), F32)
    half = pltpu.VMEM((BLOCKS, size, HALF, 256), F32)
    grad, tile_grad, wall_grad, class_grad = pl.pallas_call(
        functools.partial(region_kernel, (size, depth, volume)),
        out_shape=(
            jax.ShapeDtypeStruct((chans, 64, 128), BF16),
            jax.ShapeDtypeStruct((chans, 25), F32),
            jax.ShapeDtypeStruct((9, chans), F32),
            jax.ShapeDtypeStruct((4, chans), F32),
        ),
        in_specs=[far] * 7,
        out_specs=(vmem, vmem, vmem, vmem),
        scratch_shapes=[
            pltpu.VMEM((chans, 64, 128), BF16),
            pltpu.VMEM((128, 128), jnp.int32),
            pltpu.VMEM((1, 64), jnp.int32),
            pltpu.VMEM((levels, 9), F32),
            pltpu.VMEM((chans, 25), F32),
            pltpu.VMEM((9, chans), F32),
            pltpu.VMEM((4, chans), F32),
            pltpu.VMEM((3, 1024, 128), F32),
            pltpu.VMEM((2, 64, 16, 128), BF16),
            pltpu.VMEM((size, 2, WIN // 2, 16, 128), BF16),
            pltpu.VMEM((64, 128), F32),
            pltpu.VMEM((size + 1, 16, 128), BF16),
            pltpu.VMEM((size, 3, 16, 128), BF16),
            pltpu.VMEM((size, 3, 16, 128), F32),
            pltpu.VMEM((size, 24, 128), F32),
            wide, wide, wide, wide, wide, wide,
            block, block, half, half,
            pltpu.VMEM((25, 8, 128), F32),
            pltpu.VMEM((9, 2, 8, 128), F32),
            pltpu.VMEM((9, 2, 8, 128), F32),
            pltpu.VMEM((9, 2, 8, 128), F32),
            pltpu.VMEM((9, 2, 8, 128), F32),
            pltpu.VMEM((34 * 8, 128), F32),
            pltpu.VMEM((BLOCKS, size, ROWS, ROWS), F32),
            pltpu.VMEM((128, 128), F32),
            pltpu.VMEM((128, 128), F32),
            pltpu.VMEM((128, 128), F32),
            pltpu.VMEM((2 * size, OWN // 2, 16, 128), BF16),
            pltpu.VMEM((2, 64, 16, 128), BF16),
            pltpu.VMEM((everyone, 8, 128), F32),
            pltpu.VMEM((128, 128), F32),
            dma((7,)),
            dma((len(PIECES), size, 2)), dma((len(PIECES), size, 2)),
            dma((3, size)), dma((3, size)),
            dma((BLOCKS,)), dma((BLOCKS,)),
            dma((BLOCKS, 2 * size)), dma((BLOCKS, 2 * size)),
            dma((everyone,)), dma((everyone,)),
        ],
        compiler_params=pltpu.CompilerParams(
            collective_id=0, has_side_effects=True, vmem_limit_bytes=48 * 1024 * 1024
        ),
    )(
        features.reshape(chans, 64, 128), labels.reshape(128, 128), grid_index.reshape(1, 64),
        stretch, tile_filter, wall_filter.T, class_weight,
    )
    return grad.reshape(features.shape), tile_grad, wall_grad.T, class_grad


def shards(features, labels, grid_index, stretch, tile_filter, wall_filter, class_weight):
    chans, rows, cells_x, cells_z = features.shape
    size, depth = lax.axis_size("gx"), lax.axis_size("gz")
    volume = labels.shape[0] * cells_x * size * cells_z * depth
    cpg = chans // size
    if 128 // size == OWN:
        return regional(
            size, depth, volume,
            features, labels, grid_index, stretch, tile_filter, wall_filter, class_weight,
        )
    chunks = min(4, cpg)
    per_dest = max(cpg // 4, 1) * 8
    xs = 2 * size
    everyone = size * depth * 2
    onehot = (grid_index[:, None] == jnp.arange(stretch.shape[0], dtype=jnp.int32)).astype(F32)
    bands = jnp.dot(onehot, stretch, precision=lax.Precision.HIGHEST)
    dma = pltpu.SemaphoreType.DMA
    vmem = pl.BlockSpec(memory_space=pltpu.VMEM)
    smem = pl.BlockSpec(memory_space=pltpu.SMEM)
    grad, tile_grad, wall_grad, class_grad = pl.pallas_call(
        functools.partial(kernel, (size, depth, cpg, chunks, volume)),
        out_shape=(
            jax.ShapeDtypeStruct((chans, 64, 128), BF16),
            jax.ShapeDtypeStruct((chans, 25), F32),
            jax.ShapeDtypeStruct((9, chans), F32),
            jax.ShapeDtypeStruct((4, chans), F32),
        ),
        in_specs=[vmem, vmem, vmem, smem, smem, smem],
        out_specs=(vmem, vmem, vmem, vmem),
        scratch_shapes=[
            pltpu.VMEM((size, cpg, 64, 128), BF16),
            pltpu.VMEM((80, 9), F32),
            pltpu.VMEM((size, per_dest, 128), F32),
            pltpu.VMEM((2, size, per_dest, 128), F32),
            pltpu.VMEM((5, cpg, xs, 32, 128), F32),
            pltpu.VMEM((cpg, xs, 48, 128), F32),
            pltpu.VMEM((max(cpg, size), 64, 128), F32),
            pltpu.VMEM((cpg, 9, 48, 128), F32),
            pltpu.VMEM((9, 48, 128), F32),
            pltpu.VMEM((cpg, xs, 32, 128), F32),
            pltpu.VMEM((cpg, xs, 32, 128), F32),
            pltpu.VMEM((256, 128), F32),
            pltpu.VMEM((size, 256, 128), BF16),
            pltpu.VMEM((size, 256, 128), BF16),
            pltpu.VMEM((size, 256, 128), BF16),
            pltpu.VMEM((cpg, xs, 48, 128), F32),
            pltpu.VMEM((cpg, xs, 32, 128), F32),
            pltpu.VMEM((cpg, xs // 8, 8, 128), F32),
            pltpu.VMEM((2, cpg, xs // 8, 8, 128), F32),
            pltpu.VMEM((5, cpg, xs, 32, 128), F32),
            pltpu.VMEM((size, cpg, 64, 128), BF16),
            pltpu.VMEM((size, 64, 128), F32),
            pltpu.VMEM((cpg, 40, 8, 128), F32),
            pltpu.VMEM((128, 128), F32),
            pltpu.VMEM((everyone, 8, 128), F32),
            dma((chunks, size)), dma((chunks, size)), dma(()),
            dma((2, size)), dma((2, size)),
            dma((cpg,)), dma((cpg,)),
            dma((size,)), dma((size,)),
            dma((size,)), dma((size,)),
            dma((size,)), dma((size,)),
            dma((2, cpg)), dma((2, cpg)),
            dma((chunks, size)), dma((chunks, size)),
            dma((everyone,)), dma((everyone,)),
        ],
        compiler_params=pltpu.CompilerParams(
            collective_id=0, has_side_effects=True, vmem_limit_bytes=48 * 1024 * 1024
        ),
    )(
        features.reshape(chans, 64, 128), labels.reshape(128, 128), bands,
        tile_filter, wall_filter.T, class_weight,
    )
    return grad.reshape(features.shape), tile_grad, wall_grad.T, class_grad


def solution(mesh):
    return jax.shard_map(
        shards,
        mesh=mesh,
        in_specs=(
            P(None, "col", ("group", "gx"), "gz"),
            P(None, ("group", "gx"), "gz"),
            P(),
            P(),
            P(),
            P(),
            P(),
        ),
        out_specs=(
            P(None, "col", ("group", "gx"), "gz"),
            P("group", None),
            P("group", None),
            P("group", None),
        ),
        check_vma=False,
    )
```

```python
import functools

import jax
import jax.numpy as jnp
from jax import lax
from jax.experimental import pallas as pl
from jax.experimental.pallas import tpu as pltpu
from jax.sharding import PartitionSpec as P

F32 = jnp.float32
BF16 = jnp.bfloat16
MESH = pl.DeviceIdType.MESH


def fold(value):
    total = value[0:8]
    for row in range(8, value.shape[0], 8):
        total = total + value[row : row + 8]
    return total


def rounded(value):
    return value.astype(BF16).astype(F32)


def kernel(
    dims,
    feat, labels, bands, tile_w, wall_w, class_w,
    out, tile_out, wall_out, class_out,
    recv, band_pad, halo_out, halo_in, zfeat, smooth, stage, taps, band_rows, hid, slope,
    part_own, part_out, part_in, err, gwall, gsm, ghalo_out, ghalo_in, zgrad, gout, gstage,
    acc, red, sums,
    a_send, a_recv, own_sem, h_send, h_recv, s_send, s_recv, p_send, p_recv, e_send, e_recv,
    w_send, w_recv, g_send, g_recv, o_send, o_recv, r_send, r_recv,
):
    size, depth, cpg, chunks, volume = dims
    per = cpg // chunks
    xs = 2 * size
    xgroups = xs // 8
    everyone = size * depth * 2
    gx, gz, col = lax.axis_index("gx"), lax.axis_index("gz"), lax.axis_index("col")
    me = (gx * depth + gz) * 2 + col
    other = 1 - col
    right, left = lax.rem(gz + 1, depth), lax.rem(gz + depth - 1, depth)
    chan0 = gx * cpg

    def peer(step):
        return lax.rem(gx + step, size)

    def source(step):
        return lax.rem(gx + size - step, size)

    def coords(step):
        index = lax.rem(me + step, everyone)
        return {
            "gx": index // (2 * depth),
            "gz": lax.rem(index // 2, depth),
            "col": lax.rem(index, 2),
        }

    barrier = pltpu.get_barrier_semaphore()

    @pl.loop(1, everyone)
    def _(step):
        pl.semaphore_signal(barrier, inc=1, device_id=coords(step), device_id_type=MESH)

    pl.semaphore_wait(barrier, everyone - 1)

    def remote(src, dst, send, rec, device):
        return pltpu.make_async_remote_copy(
            src_ref=src, dst_ref=dst, send_sem=send, recv_sem=rec,
            device_id=device, device_id_type=MESH,
        )

    def a_copy(chunk, step):
        return remote(
            feat.at[pl.ds(peer(step) * cpg + chunk * per, per)],
            recv.at[step, pl.ds(chunk * per, per)],
            a_send.at[chunk, step], a_recv.at[chunk, step], {"gx": peer(step)},
        )

    def h_copy(way, step):
        return remote(
            halo_out.at[peer(step)], halo_in.at[way, step],
            h_send.at[way, step], h_recv.at[way, step],
            {"gx": peer(step), "gz": right if way == 0 else left},
        )

    own_copy = pltpu.make_async_copy(feat.at[pl.ds(chan0, cpg)], recv.at[0], own_sem)
    own_copy.start()
    for step in range(1, size):
        a_copy(0, step).start()

    lane = lax.broadcasted_iota(jnp.int32, (8, 128), 1)
    quad = lane // 4

    @pl.loop(0, size)
    def _(group):
        for first in range(0, cpg, 4):
            packed = jnp.zeros((8, 128), F32)
            for c in range(first, min(first + 4, cpg)):
                stage[c] = feat[group * cpg + c].astype(F32)
                for xl in range(2):
                    rows = stage[c, pl.ds(xl, 32, stride=2), :]
                    for t in range(4):
                        m = (c - first) * 8 + xl * 4 + t
                        turned = pltpu.roll(rows[8 * t : 8 * t + 8], (2 + 4 * m) % 128, 1)
                        packed = jnp.where(quad == m, turned, packed)
            halo_out[group, pl.ds(first // 4 * 8, 8), :] = packed

    for way in range(2):
        for step in range(size):
            h_copy(way, step).start()
    for chunk in range(1, chunks):
        for step in range(1, size):
            a_copy(chunk, step).start()

    band_pad[0:8] = jnp.zeros((8, 9), F32)
    band_pad[8:72] = bands[...]
    band_pad[72:80] = jnp.zeros((8, 9), F32)
    for k in range(9):
        band_rows[k] = jnp.broadcast_to(band_pad[pl.ds(32 * col, 48), k : k + 1], (48, 128))

    @pl.loop(0, cpg)
    def _(c):
        for k in range(9):
            taps[c, k] = wall_w[k, chan0 + c] * band_rows[k]
        for x_group in range(0, xs, 8):
            blank = jnp.zeros((8, 8, 128), F32)
            smooth[c, pl.ds(x_group, 8), pl.ds(pl.multiple_of(40 * col, 8), 8), :] = blank
            gwall[c, pl.ds(x_group, 8), pl.ds(pl.multiple_of(40 * col, 8), 8), :] = blank
        for q in range(40):
            acc[c, q] = jnp.zeros((8, 128), F32)

    red[...] = jnp.zeros((128, 128), F32)

    def shifts(value, edge):
        return (
            pltpu.roll(jnp.where(lane >= 126, edge, value), 2, 1),
            pltpu.roll(jnp.where(lane == 127, edge, value), 1, 1),
            value,
            pltpu.roll(jnp.where(lane == 0, edge, value), 127, 1),
            pltpu.roll(jnp.where(lane < 2, edge, value), 126, 1),
        )

    def filtered(field, c, x, flip):
        total = None
        for i in range(5):
            at = lax.rem(x + (4 - i if flip else i) - 2 + xs, xs)
            for j in range(5):
                term = tile_w[chan0 + c, 5 * i + j] * field[4 - j if flip else j, c, at]
                total = term if total is None else total + term
        return total

    def y_copy(ref, index, send, rec):
        src = pl.multiple_of(32 - 24 * col, 8)
        dst = pl.multiple_of(40 * col, 8)
        return remote(
            ref.at[index + (pl.ds(src, 8),)], ref.at[index + (pl.ds(dst, 8),)],
            send, rec, {"col": other},
        )

    def s_copy(c):
        return y_copy(smooth, (c, pl.ds(0, xs)), s_send.at[c], s_recv.at[c])

    own_copy.wait()
    for way in range(2):
        for step in range(size):
            h_copy(way, step).wait_recv()

    def edges_of(ref_left, ref_right):
        return jnp.where(lax.rem(lane, 4) < 2, ref_left, ref_right)

    for chunk in range(chunks):
        for step in range(1, size):
            a_copy(chunk, step).wait_recv()
        for c in range(chunk * per, chunk * per + per):

            @pl.loop(0, size, unroll=2)
            def _(step, c=c):
                s = source(step)
                stage[step] = recv[step, c].astype(F32)
                at = pl.ds(c // 4 * 8, 8)
                packed = edges_of(halo_in[0, step, at, :], halo_in[1, step, at, :])
                for xl in range(2):
                    rows = stage[step, pl.ds(xl, 32, stride=2), :]
                    for t in range(4):
                        m = c % 4 * 8 + xl * 4 + t
                        edge = pltpu.roll(packed, (126 - 4 * m) % 128, 1)
                        moved = shifts(rows[8 * t : 8 * t + 8], edge)
                        for j in range(5):
                            zfeat[j, c, 2 * s + xl, pl.ds(8 * t, 8), :] = moved[j]

            @pl.loop(0, xs, unroll=4)
            def _(x, c=c):
                smooth[c, x, pl.ds(8, 32), :] = rounded(filtered(zfeat, c, x, False))

            s_copy(c).start()

    for c in range(cpg):
        s_copy(c).wait_recv()

    def p_copy(step):
        return remote(
            part_out.at[step], part_in.at[step], p_send.at[step], p_recv.at[step],
            {"gx": peer(step)},
        )

    def scores_at(x):
        def body(c, totals):
            wall = None
            for k in range(9):
                term = taps[c, k, pl.ds(8, 32), :] * smooth[c, x, pl.ds(4 + k, 32), :]
                wall = term if wall is None else wall + term
            sig = jax.nn.sigmoid(wall)
            hidden = wall * sig
            hid[c, x] = hidden
            slope[c, x] = sig * (1.0 + wall * (1.0 - sig))
            return tuple(
                total + class_w[k, chan0 + c] * hidden for k, total in enumerate(totals)
            )

        return lax.fori_loop(
            0, cpg, body, tuple(jnp.zeros((32, 128), F32) for k in range(4)), unroll=min(4, cpg)
        )

    @pl.loop(1, size)
    def _(step):
        for xl in range(2):
            totals = scores_at(2 * peer(step) + xl)
            for k in range(4):
                part_out[step, pl.ds((2 * k + xl) * 32, 32), :] = totals[k].astype(BF16)
        p_copy(step).start()

    for xl in range(2):
        totals = scores_at(2 * gx + xl)
        for k in range(4):
            part_own[pl.ds((2 * k + xl) * 32, 32), :] = totals[k]

    @pl.loop(1, size)
    def _(step):
        p_copy(step).wait_recv()
        part_own[...] = part_own[...] + part_in[step].astype(F32)

    for xl in range(2):
        marks = labels[pl.ds(64 * col + xl, 32, stride=2), :]
        for k in range(4):
            at = pl.ds((2 * k + xl) * 32, 32)
            err[0, at, :] = (part_own[at, :] - jnp.where(marks == k, 1.0, 0.0)).astype(BF16)

    def e_copy(step):
        return remote(
            err.at[0], err.at[step], e_send.at[step], e_recv.at[step], {"gx": peer(step)}
        )

    for step in range(1, size):
        e_copy(step).start()

    def w_copy(step):
        return y_copy(
            gwall, (pl.ds(0, cpg), pl.ds(2 * source(step), 2)), w_send.at[step], w_recv.at[step]
        )

    def wall_grads(step):
        for xl in range(2):
            x = 2 * source(step) + xl
            errors = [err[step, pl.ds((2 * k + xl) * 32, 32), :].astype(F32) for k in range(4)]

            @pl.loop(0, cpg, unroll=min(4, cpg))
            def _(c):
                hidden = hid[c, x]
                grad = None
                for k in range(4):
                    term = class_w[k, chan0 + c] * errors[k]
                    grad = term if grad is None else grad + term
                    acc[c, 34 + k] = acc[c, 34 + k] + fold(errors[k] * hidden)
                gwall[c, x, pl.ds(8, 32), :] = rounded(grad * slope[c, x])

        w_copy(step).start()

    wall_grads(0)

    @pl.loop(1, size)
    def _(step):
        e_copy(step).wait_recv()
        wall_grads(step)

    @pl.loop(0, size)
    def _(step):
        w_copy(step).wait_recv()

    def g_copy(way, c):
        return remote(
            ghalo_out.at[c], ghalo_in.at[way, c], g_send.at[way, c], g_recv.at[way, c],
            {"gz": right if way == 0 else left},
        )

    @pl.loop(0, cpg)
    def _(c):
        def body(x, sums9):
            grad = gwall[c, x, pl.ds(8, 32), :]
            total = None
            news = []
            for k in range(9):
                term = taps[c, k, pl.ds(12 - k, 32), :] * gwall[c, x, pl.ds(12 - k, 32), :]
                total = term if total is None else total + term
                product = grad * band_rows[k, pl.ds(8, 32), :] * smooth[c, x, pl.ds(4 + k, 32), :]
                news.append(sums9[k] + fold(product))
            gsm[c, x] = rounded(total)
            return tuple(news)

        sums9 = lax.fori_loop(0, xs, body, tuple(jnp.zeros((8, 128), F32) for k in range(9)), unroll=2)
        for k in range(9):
            acc[c, 25 + k] = sums9[k]

        @pl.loop(0, xgroups)
        def _(group):
            packed = jnp.zeros((8, 128), F32)
            for m in range(32):
                piece = gsm[c, group * 8 + m // 4, pl.ds(m % 4 * 8, 8), :]
                packed = jnp.where(quad == m, pltpu.roll(piece, (2 + 4 * m) % 128, 1), packed)
            ghalo_out[c, group] = packed

        for way in range(2):
            g_copy(way, c).start()

    def o_copy(chunk, step):
        return remote(
            gout.at[peer(step), pl.ds(chunk * per, per)],
            out.at[pl.ds(chan0 + chunk * per, per)],
            o_send.at[chunk, step], o_recv.at[chunk, step], {"gx": peer(step)},
        )

    @pl.loop(0, chunks)
    def _(chunk):
        @pl.loop(0, per)
        def _(lower):
            c = chunk * per + lower
            for way in range(2):
                g_copy(way, c).wait_recv()

            @pl.loop(0, xgroups)
            def _(group):
                packed = edges_of(ghalo_in[0, c, group], ghalo_in[1, c, group])
                for m in range(32):
                    at = pl.ds(m % 4 * 8, 8)
                    x = group * 8 + m // 4
                    edge = pltpu.roll(packed, (126 - 4 * m) % 128, 1)
                    moved = shifts(gsm[c, x, at, :], edge)
                    for j in range(5):
                        zgrad[j, c, x, at, :] = moved[j]

            @pl.loop(0, size, unroll=2)
            def _(s):
                for xl in range(2):
                    gstage[s, pl.ds(xl, 32, stride=2), :] = filtered(zgrad, c, 2 * s + xl, True)
                gout[s, c] = gstage[s].astype(BF16)

            out[chan0 + c] = gout[gx, c]

        for step in range(1, size):
            o_copy(chunk, step).start()

    row = lax.broadcasted_iota(jnp.int32, (8, 128), 0)

    @pl.loop(0, cpg)
    def _(c):
        def body(x, sums25):
            grad = gsm[c, x]
            news = []
            for i in range(5):
                at = lax.rem(x + i - 2 + xs, xs)
                for j in range(5):
                    news.append(sums25[5 * i + j] + fold(zfeat[j, c, at] * grad))
            return tuple(news)

        sums25 = lax.fori_loop(0, xs, body, tuple(jnp.zeros((8, 128), F32) for q in range(25)), unroll=2)
        for q in range(38):
            value = sums25[q] if q < 25 else acc[c, q]
            red[pl.ds(q, 1), :] = jnp.sum(value, axis=0, keepdims=True)
        line = lax.dot_general(
            jnp.ones((8, 128), F32), red[...], (((1,), (1,)), ((), ())),
            precision=lax.Precision.HIGHEST, preferred_element_type=F32,
        )
        before = jnp.where(c == 0, jnp.zeros((8, 128), F32), sums[me])
        sums[me] = jnp.where(row == c, line, before)

    def r_copy(step):
        return remote(sums.at[me], sums.at[me], r_send.at[step], r_recv.at[step], coords(step))

    @pl.loop(1, everyone)
    def _(step):
        r_copy(step).start()

    @pl.loop(1, everyone)
    def _(step):
        r_copy(step).wait_recv()

    @pl.loop(0, size)
    def _(group):
        total = sums[group * depth * 2]
        for member in range(1, depth * 2):
            total = total + sums[group * depth * 2 + member]
        red[pl.ds(group * cpg, cpg), :] = total[0:cpg] / volume

    turned = red[...].T
    chans = size * cpg
    tile_out[...] = red[0:chans, 0:25]
    wall_out[...] = turned[25:34, 0:chans]
    class_out[...] = turned[34:38, 0:chans]

    for chunk in range(chunks):
        for step in range(1, size):
            o_copy(chunk, step).wait()
            a_copy(chunk, step).wait_send()
    for way in range(2):
        for step in range(size):
            h_copy(way, step).wait_send()
        for c in range(cpg):
            g_copy(way, c).wait_send()
    for c in range(cpg):
        s_copy(c).wait_send()
    for step in range(1, size):
        p_copy(step).wait_send()
        e_copy(step).wait_send()
    for step in range(size):
        w_copy(step).wait_send()

    @pl.loop(1, everyone)
    def _(step):
        r_copy(step).wait_send()


OWN = 32
WIN = OWN + 8
BLOCK = 12
BLOCKS = (WIN - 4) // BLOCK
ROWS = BLOCK * 8
HALF = ROWS // 2
PIECES = ((0, 2), (2, 6), (8, 6), (14, 4), (18, 2))
ARRIVE = ((0, 1), (2,), (3, 4))
WANTED = 38
HIGH = lax.Precision.HIGHEST


def cast_dot(a, b, dims=((1,), (0,))):
    return lax.dot_general(
        a.astype(BF16), b.astype(BF16), (dims, ((), ())), preferred_element_type=F32
    )


def split_dot(a, b):
    a_high, b_high = a.astype(BF16), b.astype(BF16)
    a_low, b_low = (a - a_high.astype(F32)).astype(BF16), (b - b_high.astype(F32)).astype(BF16)
    return cast_dot(a_high, b_high) + (cast_dot(a_high, b_low) + cast_dot(a_low, b_high))


def dot(a, b, dims=((1,), (0,))):
    return lax.dot_general(a, b, (dims, ((), ())), precision=HIGH, preferred_element_type=F32)


def region_kernel(
    dims,
    feat_h, lab_h, index_h, stretch_h, tile_h, wall_h, class_h,
    out, tile_out, wall_out, class_out,
    feat, lab, index, stretch, tile_w, wall_w, class_w,
    turn, send, recv, lab_rows, lab_send, lab_recv, lab_wide, lab_win,
    field, odd, smooth, gwall, gsm, godd, hid, slope, part_out, part_in,
    taps, fore, wide, wide_t, band_tile, wall, wall_acc, acc, gram, params, classes, classes_t,
    gout, ghome, sums, red,
    in_sem, f_send, f_recv, l_send, l_recv, p_send, p_recv, g_send, g_recv, r_send, r_recv,
):
    size, depth, volume = dims
    everyone = size * depth * 2
    gx, gz, col = lax.axis_index("gx"), lax.axis_index("gz"), lax.axis_index("col")
    me = (gx * depth + gz) * 2 + col
    right, left = lax.rem(gz + 1, depth), lax.rem(gz + depth - 1, depth)
    zps = OWN // 2
    lane = lax.broadcasted_iota(jnp.int32, (8, 128), 1)
    row = lax.broadcasted_iota(jnp.int32, (8, 128), 0)
    first = lane < 64
    y_lane = lax.rem(lane, 64) // 2
    x_even = lax.rem(lane, 2) == 0

    ins = [
        pltpu.make_async_copy(src, dst, in_sem.at[n])
        for n, (src, dst) in enumerate((
            (feat_h, feat), (lab_h, lab), (index_h, index), (stretch_h, stretch),
            (tile_h, tile_w), (wall_h, wall_w), (class_h, class_w),
        ))
    ]
    for copy in ins:
        copy.start()

    def coords(step):
        place = lax.rem(me + step, everyone)
        return {
            "gx": place // (2 * depth),
            "gz": lax.rem(place // 2, depth),
            "col": lax.rem(place, 2),
        }

    barrier = pltpu.get_barrier_semaphore()

    @pl.loop(1, everyone)
    def _(step):
        pl.semaphore_signal(barrier, inc=1, device_id=coords(step), device_id_type=MESH)

    def remote(src, dst, sent, got, device):
        return pltpu.make_async_remote_copy(
            src_ref=src, dst_ref=dst, send_sem=sent, recv_sem=got,
            device_id=device, device_id_type=MESH,
        )

    def target(sx):
        return lax.rem(gx + sx, size)

    def origin(sx):
        return lax.rem(gx + size - sx, size)

    ins[0].wait()
    for side in range(2):
        for cp in range(8):
            block = feat[pl.ds(side * 16 + 2 * cp, 2)].astype(F32).reshape(128, 128)
            turn[side, pl.ds(cp, 128, stride=8), :] = block.T

        @pl.loop(0, 64, unroll=8)
        def _(zp, side=side):
            at = pl.ds(pl.multiple_of(zp * 16, 16), 16)
            send[side, zp] = turn[side, at, :].astype(BF16)

    ins[1].wait()
    turn[2, 0:128, :] = lab[...].astype(F32).T
    even, uneven = turn[2, pl.ds(0, 64, stride=2), :], turn[2, pl.ds(1, 64, stride=2), :]
    here = jnp.where(col == 0, even, pltpu.roll(even, 64, 1))
    there = jnp.where(col == 0, pltpu.roll(uneven, 64, 1), uneven)
    lab_rows[...] = jnp.where(lax.broadcasted_iota(jnp.int32, (64, 128), 1) < 64, here, there)
    for t in range(size):
        lab_send[t] = lab_rows[pl.ds(zps * t, zps), :].astype(BF16)
    edge_rows = [jnp.zeros((1, 128), F32)] * 16
    for t in range(size):
        edge_rows[2 * t] = lab_rows[pl.ds((zps * t - 1) % 64, 1), :]
        edge_rows[2 * t + 1] = lab_rows[pl.ds((zps * t + zps) % 64, 1), :]
    lab_send[size] = jnp.concatenate(edge_rows, axis=0).astype(BF16)

    pl.semaphore_wait(barrier, everyone - 1)

    def f_spot(piece, t):
        at, count = PIECES[piece]
        return pl.ds(lax.rem(t * zps + at - 2 + 64, 64), count), pl.ds(at, count)

    def f_far(piece, sx, sc):
        t, ct = target(sx), lax.rem(col + sc, 2)
        src, dst = f_spot(piece, t)
        if piece == 0:
            tz = lax.rem(gz + 1 - (t + size - 1) // size, depth)
        elif piece == len(PIECES) - 1:
            tz = lax.rem(gz + depth - (t + 1) // size, depth)
        else:
            tz = gz
        return remote(
            send.at[ct, src], recv.at[gx, col, dst],
            f_send.at[piece, sx, sc], f_recv.at[piece, sx, sc],
            {"gx": t, "gz": tz, "col": ct},
        )

    def f_near(piece):
        src, dst = f_spot(piece, gx)
        return pltpu.make_async_copy(
            send.at[col, src], recv.at[gx, col, dst], f_recv.at[piece, 0, 0]
        )

    def f_wait(piece, sx, sc):
        at, count = PIECES[piece]
        slot = recv.at[origin(sx), lax.rem(col + sc, 2), pl.ds(at, count)]
        return remote(
            slot, slot, f_send.at[piece, sx, sc], f_recv.at[piece, sx, sc],
            {"gx": target(sx), "gz": gz, "col": lax.rem(col + sc, 2)},
        )

    def own_piece(piece, near, far):
        if piece == 0:
            pl.when(gx > 0)(near)
            pl.when(gx == 0)(far)
        elif piece == len(PIECES) - 1:
            pl.when(gx < size - 1)(near)
            pl.when(gx == size - 1)(far)
        else:
            near()

    others = [(sx, sc) for sx in (2, 1, 3, 0) for sc in range(2) if sx or sc]

    def l_mid(sx):
        return remote(
            lab_send.at[target(sx)], lab_recv.at[gx, 0], l_send.at[0, sx], l_recv.at[0, sx],
            {"gx": target(sx)},
        )

    def l_edge(sx):
        return remote(
            lab_send.at[size], lab_recv.at[gx, 1], l_send.at[1, sx], l_recv.at[1, sx],
            {"gx": target(sx)},
        )

    def l_far(sx):
        t = target(sx)
        tz = lax.rem(gz + depth + 1 - 2 * ((t + 1) // size), depth)
        return remote(
            lab_send.at[size], lab_recv.at[gx, 2], l_send.at[2, sx], l_recv.at[2, sx],
            {"gx": t, "gz": tz},
        )

    l_own = [
        pltpu.make_async_copy(lab_send.at[gx], lab_recv.at[gx, 0], l_recv.at[0, 0]),
        pltpu.make_async_copy(lab_send.at[size], lab_recv.at[gx, 1], l_recv.at[1, 0]),
    ]

    for block in range(BLOCKS):
        for piece in ARRIVE[block]:
            for sx, sc in others:
                f_far(piece, sx, sc).start()
            own_piece(
                piece,
                lambda piece=piece: f_near(piece).start(),
                lambda piece=piece: f_far(piece, 0, 0).start(),
            )
        if block == 0:
            for copy in l_own:
                copy.start()
            for sx in range(size):
                if sx:
                    l_mid(sx).start()
                    l_edge(sx).start()
                l_far(sx).start()

    for copy in ins[2:]:
        copy.wait()
    params[...] = jnp.zeros((128, 128), F32)
    params[0:9, 0:32] = wall_w[...]
    params[16:20, 0:32] = class_w[...]
    params[64:96, 0:25] = tile_w[...]
    red[...] = params[...].T

    def pairs(ref, start):
        return ref[pl.ds(start + col * 16, 8, stride=2), :], ref[pl.ds(start + col * 16 + 1, 8, stride=2), :]

    def spread(both, q):
        low, high = (jnp.broadcast_to(rows[:, q : q + 1], (8, 128)) for rows in both)
        return jnp.where(first, low, high)

    tile_pairs, wall_pairs = pairs(params, 64), pairs(red, 0)
    for q in range(25):
        taps[q] = spread(tile_pairs, q)

    levels = stretch.shape[0]
    hot = lax.broadcasted_iota(jnp.int32, (levels, 64), 0) == index[...]
    params[32:41, 0:64] = dot(stretch[...], hot.astype(F32), ((0,), (0,)))
    band_t = params[32:48, 0:64]
    y_row = lax.broadcasted_iota(jnp.int32, (64, 128), 0)
    y_col = lax.rem(lax.broadcasted_iota(jnp.int32, (64, 128), 1), 64) // 2
    square_row = lax.broadcasted_iota(jnp.int32, (128, 128), 0)
    square_lane = lax.broadcasted_iota(jnp.int32, (128, 128), 1)
    k_of_lane = lax.rem(lax.broadcasted_iota(jnp.int32, (16, 128), 1) // 2 + 4, 64)
    k_of_lane = (k_of_lane == lax.broadcasted_iota(jnp.int32, (16, 128), 0)) & (
        lax.rem(lax.broadcasted_iota(jnp.int32, (16, 128), 1), 2) == 0
    )
    placed = dot(band_t, k_of_lane.astype(F32), ((0,), (0,)))
    for yh in range(2):
        ahead = dot(band_t, (y_row == y_col + 32 * yh).astype(F32))
        for k in range(9):
            m = k - 4
            value = spread(wall_pairs, k) * ahead[k : k + 1, :]
            inside = (y_lane + m >= 0) & (y_lane + m < 32)
            fore[k, yh] = jnp.where(inside, value, 0.0)
            across = (y_lane + m >= 32) if yh == 0 else (y_lane + m < 0)
            fore[k, 2 + yh] = jnp.where(across, value, 0.0)
        rows_y = lax.broadcasted_iota(jnp.int32, (128, 64), 0) % 64 // 2 + 32 * yh
        at_y = rows_y == lax.broadcasted_iota(jnp.int32, (128, 64), 1)
        value = dot(at_y.astype(F32), placed)
        shift = lax.rem(square_lane // 2 + 4, 64) - 4 + square_row % 64 // 2
        inner = jnp.where((shift >= 0) & (shift < 32), value, 0.0)
        outer = jnp.where((shift >= 0) & (shift < 32), 0.0, value)
        band_tile[yh] = pltpu.roll(inner, 0, 1, stride=1, stride_axis=0)
        band_tile[2 + yh] = pltpu.roll(outer, 64, 1, stride=1, stride_axis=0)

    @pl.loop(0, 8, unroll=2)
    def _(cp):
        for yh in range(2):
            tile = jnp.zeros((128, 128), F32)
            for k in range(9):
                line = fore[k, yh, pl.ds(cp, 1), :]
                tile = jnp.where(square_row == square_lane + 2 * (k - 4), line, tile)
            wide[cp, 128 * yh : 128 * yh + 128, 128 * yh : 128 * yh + 128] = tile.astype(BF16)
            wide_t[cp, 128 * yh : 128 * yh + 128, 128 * yh : 128 * yh + 128] = tile.T.astype(BF16)
            tile = jnp.zeros((128, 128), F32)
            for k in range(5, 9) if yh == 0 else range(4):
                line = fore[k, 2 + yh, pl.ds(cp, 1), :]
                far = 2 * (k - 4) - 64 if yh == 0 else 2 * (k - 4) + 64
                tile = jnp.where(square_row == square_lane + far, line, tile)
            low, high = 128 - 128 * yh, 128 * yh
            wide[cp, low : low + 128, high : high + 128] = tile.astype(BF16)
            wide_t[cp, high : high + 128, low : low + 128] = tile.T.astype(BF16)

    chan = lax.broadcasted_iota(jnp.int32, (128, 128), 0)
    unit = lax.rem(lax.broadcasted_iota(jnp.int32, (128, 128), 1), 8)
    half_row = lax.broadcasted_iota(jnp.int32, (HALF, 128), 0)
    half_z = lax.broadcasted_iota(jnp.int32, (HALF, 128), 1) // 8
    half_k = lax.rem(half_row, 8) // 2
    same_z = (half_row // 8) * 2 + lax.rem(half_row, 2) == half_z
    classes[...] = jnp.zeros((128, 128), F32)
    for par in range(2):
        rows = dot(params[16:24, :], (chan == col * 16 + 2 * unit + par).astype(F32))
        value = jnp.zeros((HALF, 128), F32)
        for k in range(4):
            value = jnp.where(same_z & (half_k == k), rows[k : k + 1, :], value)
        classes[pl.ds(HALF * par, HALF), :] = value
    classes_t[...] = classes[...].T

    def arrived(block):
        for piece in ARRIVE[block]:
            for sx, sc in others:
                f_wait(piece, sx, sc).wait_recv()
            own_piece(
                piece,
                lambda piece=piece: f_near(piece).wait(),
                lambda piece=piece: f_wait(piece, 0, 0).wait_recv(),
            )
        low, high = PIECES[ARRIVE[block][0]][0], sum(PIECES[ARRIVE[block][-1]])

        @pl.loop(0, 2 * size)
        def _(t):
            for zp in range(low, high):
                pair = recv[t // 2, lax.rem(t, 2), zp].astype(F32)
                field[t, 2 * zp] = pair[0:8]
                field[t, 2 * zp + 1] = pair[8:16]

        between(seen(field), odd, 2 * low, 2 * high)

    def seen(ref):
        return lambda t, z: ref[t, z]

    def seen_rows(ref):
        return lambda t, z: ref[lax.rem(t, 2), spot(z, t // 2), :]

    def between(src, dst, low, high):
        @pl.loop(0, 2 * size)
        def _(t):
            after = lax.rem(t + 2, 2 * size)
            for z in range(low, high):
                dst[t, z] = jnp.where(
                    x_even, pltpu.roll(src(t, z), 127, 1), pltpu.roll(src(after, z), 1, 1)
                )

    def filtered(src, mid, t, low, count, flip, put):
        before, after = lax.rem(t + 2 * size - 2, 2 * size), lax.rem(t + 2, 2 * size)
        totals = [None] * count
        for z in range(count + 4):
            at = low + z - 2
            views = (src(before, at), mid[before, at], src(t, at), mid[t, at], src(after, at))
            for j in range(5):
                if 0 <= z - j < count:
                    for i in range(5):
                        q = 5 * (4 - i) + 4 - j if flip else 5 * i + j
                        term = taps[q] * views[i]
                        old = totals[z - j]
                        totals[z - j] = term if old is None else old + term
            if z >= 4:
                put(z - 4, totals)

    def spot(z, p):
        return pl.ds(pl.multiple_of((z * size + p) * 8, 8), 8)

    def unit_rows(z, count, cp):
        return pl.ds(z * size * 8 + cp, count * size, stride=8)

    def unit_of(ref, z, count, cp):
        at = unit_rows(z, count, cp)
        return jnp.concatenate([ref[0, at, :], ref[1, at, :]], axis=1).astype(BF16)

    def p_copy(block):
        return remote(
            part_out.at[block], part_in.at[block], p_send.at[block], p_recv.at[block],
            {"col": 1 - col},
        )

    def ahead_of(block):
        base = 2 + BLOCK * block

        @pl.loop(0, 2 * size)
        def _(t):
            def put(z, totals):
                smooth[lax.rem(t, 2), spot(base + z, t // 2), :] = rounded(totals[z])

            filtered(seen(field), odd, t, base, BLOCK, False, put)

        @pl.loop(0, 8, unroll=8)
        def _(cp):
            both = jnp.dot(
                unit_of(smooth, base, BLOCK, cp), wide[cp], preferred_element_type=F32
            )
            for yh in range(2):
                wall[yh, unit_rows(0, BLOCK, cp), :] = both[:, 128 * yh : 128 * yh + 128]

        @pl.loop(0, BLOCK)
        def _(z):
            at = pl.ds(pl.multiple_of(8 * z, 8), 8)
            for p in range(size):
                for yh in range(2):
                    value = wall[yh, spot(z, p), :]
                    sig = jax.nn.sigmoid(value)
                    lanes = slice(128 * yh, 128 * yh + 128)
                    hid[block, p, at, lanes] = value * sig
                    slope[block, p, at, lanes] = sig * (1.0 + value * (1.0 - sig))

        left_half = lax.rem(lax.broadcasted_iota(jnp.int32, (HALF, 256), 1), 128) < 64

        @pl.loop(0, size, unroll=size)
        def _(p):
            part = split_dot(classes[0:ROWS, 0:ROWS], hid[block, p])
            part_out[block, p] = jnp.where(left_half, part[0:HALF], part[HALF:ROWS])
            lanes = pl.ds(pl.multiple_of(128 * col, 128), 128)
            for zp in range(BLOCK // 2):
                at = slice(8 * zp, 8 * zp + 8)
                mark = lab_win[p, pl.ds(BLOCK // 2 * block + zp, 1), :]
                mark = jnp.broadcast_to(mark, (8, 128))
                mark = jnp.where(lax.rem(row, 2) == 0, mark, pltpu.roll(mark, 64, 1))
                hit = first & (mark == (row // 2).astype(F32))
                part_out[block, p, at, lanes] = part_out[block, p, at, lanes] - jnp.where(hit, 1.0, 0.0)

        p_copy(block).start()

    def back_of(block):
        base = 2 + BLOCK * block
        p_copy(block).wait_recv()
        left_half = lax.rem(lax.broadcasted_iota(jnp.int32, (HALF, 256), 1), 128) < 64

        @pl.loop(0, size, unroll=size)
        def _(p):
            err = part_out[block, p] + part_in[block, p]
            swapped = jnp.concatenate(
                [pltpu.roll(err[:, 0:128], 64, 1), pltpu.roll(err[:, 128:256], 64, 1)], axis=1
            )
            err = err + swapped
            both = jnp.concatenate(
                [jnp.where(left_half, err, 0.0), jnp.where(left_half, 0.0, err)], axis=0
            )
            grad = split_dot(classes_t[0:ROWS, 0:ROWS], both) * slope[block, p]
            for z in range(BLOCK):
                for yh in range(2):
                    gwall[yh, spot(base + z, p), :] = rounded(
                        grad[8 * z : 8 * z + 8, 128 * yh : 128 * yh + 128]
                    )
            new = cast_dot(both, hid[block, p], ((1,), (1,)))
            gram[block, p] = new

        @pl.loop(0, 8, unroll=8)
        def _(cp):
            both = jnp.dot(
                unit_of(gwall, base, BLOCK, cp), wide_t[cp], preferred_element_type=F32
            )
            for yh in range(2):
                at = unit_rows(base, BLOCK, cp)
                gsm[yh, at, :] = rounded(both[:, 128 * yh : 128 * yh + 128])

        between(seen_rows(gsm), godd, base, base + BLOCK)

    def g_spot(block):
        low = 4 if block == 0 else BLOCK * block
        return low, BLOCK * block + BLOCK - low

    def g_copy(block, step):
        low, count = g_spot(block)
        at, many = (low - 4) // 2, count // 2
        p, yh = target(step // 2), lax.rem(col + step, 2)
        return remote(
            gout.at[2 * p + yh, pl.ds(at, many)],
            ghome.at[col, pl.ds(gx * zps + at, many)],
            g_send.at[block, step], g_recv.at[block, step], {"gx": p, "col": yh},
        )

    def g_near(block):
        low, count = g_spot(block)
        at, many = (low - 4) // 2, count // 2
        return pltpu.make_async_copy(
            gout.at[2 * gx + col, pl.ds(at, many)],
            ghome.at[col, pl.ds(gx * zps + at, many)],
            g_recv.at[block, 0],
        )

    def g_wait(block, step):
        low, count = g_spot(block)
        at, many = (low - 4) // 2, count // 2
        slot = ghome.at[lax.rem(col + step, 2), pl.ds(origin(step // 2) * zps + at, many)]
        return remote(
            slot, slot, g_send.at[block, step], g_recv.at[block, step],
            {"gx": target(step // 2), "col": lax.rem(col + step, 2)},
        )

    def home(block):
        low, count = g_spot(block)

        @pl.loop(0, 2 * size)
        def _(turn_at):
            step = lax.rem(turn_at + 4, 2 * size)
            t = 2 * target(step // 2) + lax.rem(col + step, 2)

            def put(z, totals):
                if z % 2:
                    pair = jnp.concatenate([totals[z - 1], totals[z]], axis=0)
                    gout[t, (low - 4 + z) // 2] = pair.astype(BF16)

            filtered(seen_rows(gsm), godd, t, low, count, True, put)

            @pl.when(step > 0)
            def _():
                g_copy(block, step).start()

            @pl.when(step == 0)
            def _():
                g_near(block).start()

    def labels_in():
        for sx in range(size):
            if sx:
                for slot in range(2):
                    at = lab_recv.at[origin(sx), slot]
                    remote(
                        at, at, l_send.at[slot, sx], l_recv.at[slot, sx], {"gx": target(sx)}
                    ).wait_recv()
            at = lab_recv.at[origin(sx), 2]
            remote(
                at, at, l_send.at[2, sx], l_recv.at[2, sx], {"gx": target(sx), "gz": right}
            ).wait_recv()
        for copy in l_own:
            copy.wait()
        low_edge = 2 - (gx + size - 1) // size
        high_edge = 1 + (gx + 1) // size
        for p in range(size):
            lab_win[p, 1 : 1 + zps, :] = lab_recv[p, 0].astype(F32)
            for slot in range(1, 3):
                lab_wide[p, slot] = lab_recv[p, slot].astype(F32)
            lab_win[p, 0:1, :] = lab_wide[p, low_edge, pl.ds(2 * gx, 1), :]
            lab_win[p, 1 + zps : 2 + zps, :] = lab_wide[p, high_edge, pl.ds(2 * gx + 1, 1), :]

    arrived(0)
    labels_in()
    ahead_of(0)
    arrived(1)
    ahead_of(1)
    back_of(0)
    home(0)
    arrived(2)
    ahead_of(2)
    back_of(1)
    home(1)
    back_of(2)
    home(2)

    def tile_body(it, sums25):
        t, base = it // 4, 4 + 8 * lax.rem(it, 4)
        before, after = lax.rem(t + 2 * size - 2, 2 * size), lax.rem(t + 2, 2 * size)
        grads = [seen_rows(gsm)(t, base + z) for z in range(8)]
        news = list(sums25)
        for z in range(12):
            at = base + z - 2
            views = (
                field[before, at], odd[before, at], field[t, at], odd[t, at], field[after, at]
            )
            for j in range(5):
                if 0 <= z - j < 8:
                    for i in range(5):
                        news[5 * i + j] = news[5 * i + j] + views[i] * grads[z - j]
        return tuple(news)

    sums25 = lax.fori_loop(
        0, 8 * size, tile_body, tuple(jnp.zeros((8, 128), F32) for q in range(25))
    )
    for q in range(25):
        acc[8 * q : 8 * q + 8, :] = sums25[q]

    @pl.loop(0, 8, unroll=8)
    def _(cp):
        grads, fields = unit_of(gwall, 4, OWN, cp), unit_of(smooth, 4, OWN, cp)
        both = cast_dot(grads, fields, ((0,), (0,)))
        for par in range(2):
            wall_acc[par, cp] = jnp.zeros((8, 128), F32)
        for yh in range(2):
            here, far = slice(128 * yh, 128 * yh + 128), slice(128 - 128 * yh, 256 - 128 * yh)
            for g in range(16):
                at = slice(128 * yh + 8 * g, 128 * yh + 8 * g + 8)
                tile = both[at, here] * band_tile[yh, 8 * g : 8 * g + 8, :]
                if g % 8 == (0 if yh else 7):
                    edge = both[at, far] * band_tile[2 + yh, 8 * g : 8 * g + 8, :]
                    tile = tile + pltpu.roll(edge, 64, 1)
                wall_acc[g // 8, cp] = wall_acc[g // 8, cp] + pltpu.roll(tile, (128 - 8 * g) % 128, 1)

    inner_row = lax.rem(lax.broadcasted_iota(jnp.int32, (64, 128), 0), 8)
    halves = lax.broadcasted_iota(jnp.int32, (128, 128), 0) // 64
    parity = lax.rem(lax.broadcasted_iota(jnp.int32, (128, 128), 1), 2)
    lines = dot(acc[...], (halves == parity).astype(F32))
    total = jnp.zeros((8, 128), F32)
    for q in range(25):
        total = jnp.where(lane // 2 == q, lines[8 * q : 8 * q + 8, :], total)

    full_row = lax.broadcasted_iota(jnp.int32, (ROWS, ROWS), 0)
    full_lane = lax.broadcasted_iota(jnp.int32, (ROWS, ROWS), 1)
    row_z = lax.rem(full_row, HALF) // 8 * 2 + lax.rem(full_row, 2)
    matrix = jnp.zeros((ROWS, ROWS), F32)
    for block in range(BLOCKS):
        base = 2 + BLOCK * block
        value = gram[block, 0]
        for p in range(1, size):
            value = value + gram[block, p]
        keep = (row_z == full_lane // 8) & (row_z + base >= 4) & (row_z + base < 4 + OWN)
        matrix = matrix + jnp.where(keep, value, 0.0)
    gather = (
        lax.broadcasted_iota(jnp.int32, (8, ROWS), 0)
        == lax.rem(lax.broadcasted_iota(jnp.int32, (8, ROWS), 1), 8)
    ).astype(F32)
    by_row = dot(gather, matrix, ((1,), (1,)))
    source_row = lax.broadcasted_iota(jnp.int32, (ROWS, 128), 0)
    place = 2 * (34 + lax.rem(source_row, 8) // 2) + source_row // HALF
    place = place == lax.broadcasted_iota(jnp.int32, (ROWS, 128), 1)
    total = total + dot(by_row, place.astype(F32))
    stack = (
        lax.broadcasted_iota(jnp.int32, (8, 64), 0)
        == lax.broadcasted_iota(jnp.int32, (8, 64), 1) // 8
    ).astype(F32)
    for par in range(2):
        value = wall_acc[par].reshape(64, 128)
        for r in range(1, 8):
            value = jnp.where(inner_row == r, pltpu.roll(value, 128 - r, 1), value)
        by_lane = dot(stack, value)
        source = lax.rem(square_row // 2 + 4, 64)
        place = (lax.rem(square_row, 2) == 0) & (source < 9) & (
            square_lane == 2 * (25 + source) + par
        )
        total = total + dot(by_lane, place.astype(F32))
    sums[me] = total

    def r_copy(step):
        return remote(sums.at[me], sums.at[me], r_send.at[step], r_recv.at[step], coords(step))

    @pl.loop(1, everyone)
    def _(step):
        r_copy(step).start()

    for block in range(BLOCKS):
        for step in range(1, 2 * size):
            g_wait(block, step).wait_recv()
        g_near(block).wait()

    for side in range(2):
        @pl.loop(0, 64, unroll=8)
        def _(zp, side=side):
            at = pl.ds(pl.multiple_of(zp * 16, 16), 16)
            turn[side, at, :] = ghome[side, zp].astype(F32)

        for cp in range(8):
            block = turn[side, pl.ds(cp, 128, stride=8), :].T
            out[pl.ds(side * 16 + 2 * cp, 2)] = block.reshape(2, 64, 128).astype(BF16)

    def r_wait(step):
        place = lax.rem(me + everyone - step, everyone)
        return remote(
            sums.at[place], sums.at[place], r_send.at[step], r_recv.at[step], coords(step)
        )

    @pl.loop(1, everyone)
    def _(step):
        r_wait(step).wait_recv()

    spot = lax.broadcasted_iota(jnp.int32, (128, 128), 0)
    want = 2 * lax.broadcasted_iota(jnp.int32, (128, 128), 1)
    red[...] = jnp.zeros((128, 128), F32)
    for side in range(2):
        total = sums[side]
        for member in range(1, size * depth):
            total = total + sums[2 * member + side]
        total = total / volume
        for par in range(2):
            red[pl.ds(side * 16 + par, 8, stride=2), :] = dot(total, (spot == want + par).astype(F32))
    turned = red[...].T
    tile_out[...] = red[0:32, 0:25]
    wall_out[...] = turned[25:34, 0:32]
    class_out[...] = turned[34:38, 0:32]

    for piece in range(len(PIECES)):
        for sx, sc in others:
            f_far(piece, sx, sc).wait_send()
    pl.when(gx == 0)(lambda: f_far(0, 0, 0).wait_send())
    pl.when(gx == size - 1)(lambda: f_far(len(PIECES) - 1, 0, 0).wait_send())
    for sx in range(size):
        if sx:
            l_mid(sx).wait_send()
            l_edge(sx).wait_send()
        l_far(sx).wait_send()
    for block in range(BLOCKS):
        p_copy(block).wait_send()
        for step in range(1, 2 * size):
            g_copy(block, step).wait_send()

    @pl.loop(1, everyone)
    def _(step):
        r_copy(step).wait_send()


def regional(
    size, depth, volume,
    features, labels, grid_index, stretch, tile_filter, wall_filter, class_weight,
):
    chans = features.shape[0]
    levels = stretch.shape[0]
    everyone = size * depth * 2
    dma = pltpu.SemaphoreType.DMA
    vmem = pl.BlockSpec(memory_space=pltpu.VMEM)
    far = pl.BlockSpec(memory_space=pl.ANY)
    wide = pltpu.VMEM((2 * size, WIN, 8, 128), F32)
    rows = pltpu.VMEM((2, WIN * size * 8, 128), F32)
    block = pltpu.VMEM((BLOCKS, size, ROWS, 256), F32)
    half = pltpu.VMEM((BLOCKS, size, HALF, 256), F32)
    grad, tile_grad, wall_grad, class_grad = pl.pallas_call(
        functools.partial(region_kernel, (size, depth, volume)),
        out_shape=(
            jax.ShapeDtypeStruct((chans, 64, 128), BF16),
            jax.ShapeDtypeStruct((chans, 25), F32),
            jax.ShapeDtypeStruct((9, chans), F32),
            jax.ShapeDtypeStruct((4, chans), F32),
        ),
        in_specs=[far] * 7,
        out_specs=(vmem, vmem, vmem, vmem),
        scratch_shapes=[
            pltpu.VMEM((chans, 64, 128), BF16),
            pltpu.VMEM((128, 128), jnp.int32),
            pltpu.VMEM((1, 64), jnp.int32),
            pltpu.VMEM((levels, 9), F32),
            pltpu.VMEM((chans, 25), F32),
            pltpu.VMEM((9, chans), F32),
            pltpu.VMEM((4, chans), F32),
            pltpu.VMEM((3, 1024, 128), F32),
            pltpu.VMEM((2, 64, 16, 128), BF16),
            pltpu.VMEM((size, 2, WIN // 2, 16, 128), BF16),
            pltpu.VMEM((64, 128), F32),
            pltpu.VMEM((size + 1, 16, 128), BF16),
            pltpu.VMEM((size, 3, 16, 128), BF16),
            pltpu.VMEM((size, 3, 16, 128), F32),
            pltpu.VMEM((size, 24, 128), F32),
            wide, wide, rows, rows, rows, wide,
            block, block, half, half,
            pltpu.VMEM((25, 8, 128), F32),
            pltpu.VMEM((9, 4, 8, 128), F32),
            pltpu.VMEM((8, 256, 256), BF16),
            pltpu.VMEM((8, 256, 256), BF16),
            pltpu.VMEM((4, 128, 128), F32),
            pltpu.VMEM((2, ROWS * size, 128), F32),
            pltpu.VMEM((2, 8, 8, 128), F32),
            pltpu.VMEM((25 * 8, 128), F32),
            pltpu.VMEM((BLOCKS, size, ROWS, ROWS), F32),
            pltpu.VMEM((128, 128), F32),
            pltpu.VMEM((128, 128), F32),
            pltpu.VMEM((128, 128), F32),
            pltpu.VMEM((2 * size, OWN // 2, 16, 128), BF16),
            pltpu.VMEM((2, 64, 16, 128), BF16),
            pltpu.VMEM((everyone, 8, 128), F32),
            pltpu.VMEM((128, 128), F32),
            dma((7,)),
            dma((len(PIECES), size, 2)), dma((len(PIECES), size, 2)),
            dma((3, size)), dma((3, size)),
            dma((BLOCKS,)), dma((BLOCKS,)),
            dma((BLOCKS, 2 * size)), dma((BLOCKS, 2 * size)),
            dma((everyone,)), dma((everyone,)),
        ],
        compiler_params=pltpu.CompilerParams(
            collective_id=0, has_side_effects=True, vmem_limit_bytes=63 * 1024 * 1024
        ),
    )(
        features.reshape(chans, 64, 128), labels.reshape(128, 128), grid_index.reshape(1, 64),
        stretch, tile_filter, wall_filter.T, class_weight,
    )
    return grad.reshape(features.shape), tile_grad, wall_grad.T, class_grad


def shards(features, labels, grid_index, stretch, tile_filter, wall_filter, class_weight):
    chans, rows, cells_x, cells_z = features.shape
    size, depth = lax.axis_size("gx"), lax.axis_size("gz")
    volume = labels.shape[0] * cells_x * size * cells_z * depth
    cpg = chans // size
    if 128 // size == OWN:
        return regional(
            size, depth, volume,
            features, labels, grid_index, stretch, tile_filter, wall_filter, class_weight,
        )
    chunks = min(4, cpg)
    per_dest = max(cpg // 4, 1) * 8
    xs = 2 * size
    everyone = size * depth * 2
    onehot = (grid_index[:, None] == jnp.arange(stretch.shape[0], dtype=jnp.int32)).astype(F32)
    bands = jnp.dot(onehot, stretch, precision=lax.Precision.HIGHEST)
    dma = pltpu.SemaphoreType.DMA
    vmem = pl.BlockSpec(memory_space=pltpu.VMEM)
    smem = pl.BlockSpec(memory_space=pltpu.SMEM)
    grad, tile_grad, wall_grad, class_grad = pl.pallas_call(
        functools.partial(kernel, (size, depth, cpg, chunks, volume)),
        out_shape=(
            jax.ShapeDtypeStruct((chans, 64, 128), BF16),
            jax.ShapeDtypeStruct((chans, 25), F32),
            jax.ShapeDtypeStruct((9, chans), F32),
            jax.ShapeDtypeStruct((4, chans), F32),
        ),
        in_specs=[vmem, vmem, vmem, smem, smem, smem],
        out_specs=(vmem, vmem, vmem, vmem),
        scratch_shapes=[
            pltpu.VMEM((size, cpg, 64, 128), BF16),
            pltpu.VMEM((80, 9), F32),
            pltpu.VMEM((size, per_dest, 128), F32),
            pltpu.VMEM((2, size, per_dest, 128), F32),
            pltpu.VMEM((5, cpg, xs, 32, 128), F32),
            pltpu.VMEM((cpg, xs, 48, 128), F32),
            pltpu.VMEM((max(cpg, size), 64, 128), F32),
            pltpu.VMEM((cpg, 9, 48, 128), F32),
            pltpu.VMEM((9, 48, 128), F32),
            pltpu.VMEM((cpg, xs, 32, 128), F32),
            pltpu.VMEM((cpg, xs, 32, 128), F32),
            pltpu.VMEM((256, 128), F32),
            pltpu.VMEM((size, 256, 128), BF16),
            pltpu.VMEM((size, 256, 128), BF16),
            pltpu.VMEM((size, 256, 128), BF16),
            pltpu.VMEM((cpg, xs, 48, 128), F32),
            pltpu.VMEM((cpg, xs, 32, 128), F32),
            pltpu.VMEM((cpg, xs // 8, 8, 128), F32),
            pltpu.VMEM((2, cpg, xs // 8, 8, 128), F32),
            pltpu.VMEM((5, cpg, xs, 32, 128), F32),
            pltpu.VMEM((size, cpg, 64, 128), BF16),
            pltpu.VMEM((size, 64, 128), F32),
            pltpu.VMEM((cpg, 40, 8, 128), F32),
            pltpu.VMEM((128, 128), F32),
            pltpu.VMEM((everyone, 8, 128), F32),
            dma((chunks, size)), dma((chunks, size)), dma(()),
            dma((2, size)), dma((2, size)),
            dma((cpg,)), dma((cpg,)),
            dma((size,)), dma((size,)),
            dma((size,)), dma((size,)),
            dma((size,)), dma((size,)),
            dma((2, cpg)), dma((2, cpg)),
            dma((chunks, size)), dma((chunks, size)),
            dma((everyone,)), dma((everyone,)),
        ],
        compiler_params=pltpu.CompilerParams(
            collective_id=0, has_side_effects=True, vmem_limit_bytes=48 * 1024 * 1024
        ),
    )(
        features.reshape(chans, 64, 128), labels.reshape(128, 128), bands,
        tile_filter, wall_filter.T, class_weight,
    )
    return grad.reshape(features.shape), tile_grad, wall_grad.T, class_grad


def solution(mesh):
    return jax.shard_map(
        shards,
        mesh=mesh,
        in_specs=(
            P(None, "col", ("group", "gx"), "gz"),
            P(None, ("group", "gx"), "gz"),
            P(),
            P(),
            P(),
            P(),
            P(),
        ),
        out_specs=(
            P(None, "col", ("group", "gx"), "gz"),
            P("group", None),
            P("group", None),
            P("group", None),
        ),
        check_vma=False,
    )
```

```python
import functools

import jax
import jax.numpy as jnp
from jax import lax
from jax.experimental import pallas as pl
from jax.experimental.pallas import tpu as pltpu
from jax.sharding import PartitionSpec as P

F32 = jnp.float32
BF16 = jnp.bfloat16
MESH = pl.DeviceIdType.MESH


def fold(value):
    total = value[0:8]
    for row in range(8, value.shape[0], 8):
        total = total + value[row : row + 8]
    return total


def rounded(value):
    return value.astype(BF16).astype(F32)


def kernel(
    dims,
    feat, labels, bands, tile_w, wall_w, class_w,
    out, tile_out, wall_out, class_out,
    recv, band_pad, halo_out, halo_in, zfeat, smooth, stage, taps, band_rows, hid, slope,
    part_own, part_out, part_in, err, gwall, gsm, ghalo_out, ghalo_in, zgrad, gout, gstage,
    acc, red, sums,
    a_send, a_recv, own_sem, h_send, h_recv, s_send, s_recv, p_send, p_recv, e_send, e_recv,
    w_send, w_recv, g_send, g_recv, o_send, o_recv, r_send, r_recv,
):
    size, depth, cpg, chunks, volume = dims
    per = cpg // chunks
    xs = 2 * size
    xgroups = xs // 8
    everyone = size * depth * 2
    gx, gz, col = lax.axis_index("gx"), lax.axis_index("gz"), lax.axis_index("col")
    me = (gx * depth + gz) * 2 + col
    other = 1 - col
    right, left = lax.rem(gz + 1, depth), lax.rem(gz + depth - 1, depth)
    chan0 = gx * cpg

    def peer(step):
        return lax.rem(gx + step, size)

    def source(step):
        return lax.rem(gx + size - step, size)

    def coords(step):
        index = lax.rem(me + step, everyone)
        return {
            "gx": index // (2 * depth),
            "gz": lax.rem(index // 2, depth),
            "col": lax.rem(index, 2),
        }

    barrier = pltpu.get_barrier_semaphore()

    @pl.loop(1, everyone)
    def _(step):
        pl.semaphore_signal(barrier, inc=1, device_id=coords(step), device_id_type=MESH)

    pl.semaphore_wait(barrier, everyone - 1)

    def remote(src, dst, send, rec, device):
        return pltpu.make_async_remote_copy(
            src_ref=src, dst_ref=dst, send_sem=send, recv_sem=rec,
            device_id=device, device_id_type=MESH,
        )

    def a_copy(chunk, step):
        return remote(
            feat.at[pl.ds(peer(step) * cpg + chunk * per, per)],
            recv.at[step, pl.ds(chunk * per, per)],
            a_send.at[chunk, step], a_recv.at[chunk, step], {"gx": peer(step)},
        )

    def h_copy(way, step):
        return remote(
            halo_out.at[peer(step)], halo_in.at[way, step],
            h_send.at[way, step], h_recv.at[way, step],
            {"gx": peer(step), "gz": right if way == 0 else left},
        )

    own_copy = pltpu.make_async_copy(feat.at[pl.ds(chan0, cpg)], recv.at[0], own_sem)
    own_copy.start()
    for step in range(1, size):
        a_copy(0, step).start()

    lane = lax.broadcasted_iota(jnp.int32, (8, 128), 1)
    quad = lane // 4

    @pl.loop(0, size)
    def _(group):
        for first in range(0, cpg, 4):
            packed = jnp.zeros((8, 128), F32)
            for c in range(first, min(first + 4, cpg)):
                stage[c] = feat[group * cpg + c].astype(F32)
                for xl in range(2):
                    rows = stage[c, pl.ds(xl, 32, stride=2), :]
                    for t in range(4):
                        m = (c - first) * 8 + xl * 4 + t
                        turned = pltpu.roll(rows[8 * t : 8 * t + 8], (2 + 4 * m) % 128, 1)
                        packed = jnp.where(quad == m, turned, packed)
            halo_out[group, pl.ds(first // 4 * 8, 8), :] = packed

    for way in range(2):
        for step in range(size):
            h_copy(way, step).start()
    for chunk in range(1, chunks):
        for step in range(1, size):
            a_copy(chunk, step).start()

    band_pad[0:8] = jnp.zeros((8, 9), F32)
    band_pad[8:72] = bands[...]
    band_pad[72:80] = jnp.zeros((8, 9), F32)
    for k in range(9):
        band_rows[k] = jnp.broadcast_to(band_pad[pl.ds(32 * col, 48), k : k + 1], (48, 128))

    @pl.loop(0, cpg)
    def _(c):
        for k in range(9):
            taps[c, k] = wall_w[k, chan0 + c] * band_rows[k]
        for x_group in range(0, xs, 8):
            blank = jnp.zeros((8, 8, 128), F32)
            smooth[c, pl.ds(x_group, 8), pl.ds(pl.multiple_of(40 * col, 8), 8), :] = blank
            gwall[c, pl.ds(x_group, 8), pl.ds(pl.multiple_of(40 * col, 8), 8), :] = blank
        for q in range(40):
            acc[c, q] = jnp.zeros((8, 128), F32)

    red[...] = jnp.zeros((128, 128), F32)

    def shifts(value, edge):
        return (
            pltpu.roll(jnp.where(lane >= 126, edge, value), 2, 1),
            pltpu.roll(jnp.where(lane == 127, edge, value), 1, 1),
            value,
            pltpu.roll(jnp.where(lane == 0, edge, value), 127, 1),
            pltpu.roll(jnp.where(lane < 2, edge, value), 126, 1),
        )

    def filtered(field, c, x, flip):
        total = None
        for i in range(5):
            at = lax.rem(x + (4 - i if flip else i) - 2 + xs, xs)
            for j in range(5):
                term = tile_w[chan0 + c, 5 * i + j] * field[4 - j if flip else j, c, at]
                total = term if total is None else total + term
        return total

    def y_copy(ref, index, send, rec):
        src = pl.multiple_of(32 - 24 * col, 8)
        dst = pl.multiple_of(40 * col, 8)
        return remote(
            ref.at[index + (pl.ds(src, 8),)], ref.at[index + (pl.ds(dst, 8),)],
            send, rec, {"col": other},
        )

    def s_copy(c):
        return y_copy(smooth, (c, pl.ds(0, xs)), s_send.at[c], s_recv.at[c])

    own_copy.wait()
    for way in range(2):
        for step in range(size):
            h_copy(way, step).wait_recv()

    def edges_of(ref_left, ref_right):
        return jnp.where(lax.rem(lane, 4) < 2, ref_left, ref_right)

    for chunk in range(chunks):
        for step in range(1, size):
            a_copy(chunk, step).wait_recv()
        for c in range(chunk * per, chunk * per + per):

            @pl.loop(0, size, unroll=2)
            def _(step, c=c):
                s = source(step)
                stage[step] = recv[step, c].astype(F32)
                at = pl.ds(c // 4 * 8, 8)
                packed = edges_of(halo_in[0, step, at, :], halo_in[1, step, at, :])
                for xl in range(2):
                    rows = stage[step, pl.ds(xl, 32, stride=2), :]
                    for t in range(4):
                        m = c % 4 * 8 + xl * 4 + t
                        edge = pltpu.roll(packed, (126 - 4 * m) % 128, 1)
                        moved = shifts(rows[8 * t : 8 * t + 8], edge)
                        for j in range(5):
                            zfeat[j, c, 2 * s + xl, pl.ds(8 * t, 8), :] = moved[j]

            @pl.loop(0, xs, unroll=4)
            def _(x, c=c):
                smooth[c, x, pl.ds(8, 32), :] = rounded(filtered(zfeat, c, x, False))

            s_copy(c).start()

    for c in range(cpg):
        s_copy(c).wait_recv()

    def p_copy(step):
        return remote(
            part_out.at[step], part_in.at[step], p_send.at[step], p_recv.at[step],
            {"gx": peer(step)},
        )

    def scores_at(x):
        def body(c, totals):
            wall = None
            for k in range(9):
                term = taps[c, k, pl.ds(8, 32), :] * smooth[c, x, pl.ds(4 + k, 32), :]
                wall = term if wall is None else wall + term
            sig = jax.nn.sigmoid(wall)
            hidden = wall * sig
            hid[c, x] = hidden
            slope[c, x] = sig * (1.0 + wall * (1.0 - sig))
            return tuple(
                total + class_w[k, chan0 + c] * hidden for k, total in enumerate(totals)
            )

        return lax.fori_loop(
            0, cpg, body, tuple(jnp.zeros((32, 128), F32) for k in range(4)), unroll=min(4, cpg)
        )

    @pl.loop(1, size)
    def _(step):
        for xl in range(2):
            totals = scores_at(2 * peer(step) + xl)
            for k in range(4):
                part_out[step, pl.ds((2 * k + xl) * 32, 32), :] = totals[k].astype(BF16)
        p_copy(step).start()

    for xl in range(2):
        totals = scores_at(2 * gx + xl)
        for k in range(4):
            part_own[pl.ds((2 * k + xl) * 32, 32), :] = totals[k]

    @pl.loop(1, size)
    def _(step):
        p_copy(step).wait_recv()
        part_own[...] = part_own[...] + part_in[step].astype(F32)

    for xl in range(2):
        marks = labels[pl.ds(64 * col + xl, 32, stride=2), :]
        for k in range(4):
            at = pl.ds((2 * k + xl) * 32, 32)
            err[0, at, :] = (part_own[at, :] - jnp.where(marks == k, 1.0, 0.0)).astype(BF16)

    def e_copy(step):
        return remote(
            err.at[0], err.at[step], e_send.at[step], e_recv.at[step], {"gx": peer(step)}
        )

    for step in range(1, size):
        e_copy(step).start()

    def w_copy(step):
        return y_copy(
            gwall, (pl.ds(0, cpg), pl.ds(2 * source(step), 2)), w_send.at[step], w_recv.at[step]
        )

    def wall_grads(step):
        for xl in range(2):
            x = 2 * source(step) + xl
            errors = [err[step, pl.ds((2 * k + xl) * 32, 32), :].astype(F32) for k in range(4)]

            @pl.loop(0, cpg, unroll=min(4, cpg))
            def _(c):
                hidden = hid[c, x]
                grad = None
                for k in range(4):
                    term = class_w[k, chan0 + c] * errors[k]
                    grad = term if grad is None else grad + term
                    acc[c, 34 + k] = acc[c, 34 + k] + fold(errors[k] * hidden)
                gwall[c, x, pl.ds(8, 32), :] = rounded(grad * slope[c, x])

        w_copy(step).start()

    wall_grads(0)

    @pl.loop(1, size)
    def _(step):
        e_copy(step).wait_recv()
        wall_grads(step)

    @pl.loop(0, size)
    def _(step):
        w_copy(step).wait_recv()

    def g_copy(way, c):
        return remote(
            ghalo_out.at[c], ghalo_in.at[way, c], g_send.at[way, c], g_recv.at[way, c],
            {"gz": right if way == 0 else left},
        )

    @pl.loop(0, cpg)
    def _(c):
        def body(x, sums9):
            grad = gwall[c, x, pl.ds(8, 32), :]
            total = None
            news = []
            for k in range(9):
                term = taps[c, k, pl.ds(12 - k, 32), :] * gwall[c, x, pl.ds(12 - k, 32), :]
                total = term if total is None else total + term
                product = grad * band_rows[k, pl.ds(8, 32), :] * smooth[c, x, pl.ds(4 + k, 32), :]
                news.append(sums9[k] + fold(product))
            gsm[c, x] = rounded(total)
            return tuple(news)

        sums9 = lax.fori_loop(0, xs, body, tuple(jnp.zeros((8, 128), F32) for k in range(9)), unroll=2)
        for k in range(9):
            acc[c, 25 + k] = sums9[k]

        @pl.loop(0, xgroups)
        def _(group):
            packed = jnp.zeros((8, 128), F32)
            for m in range(32):
                piece = gsm[c, group * 8 + m // 4, pl.ds(m % 4 * 8, 8), :]
                packed = jnp.where(quad == m, pltpu.roll(piece, (2 + 4 * m) % 128, 1), packed)
            ghalo_out[c, group] = packed

        for way in range(2):
            g_copy(way, c).start()

    def o_copy(chunk, step):
        return remote(
            gout.at[peer(step), pl.ds(chunk * per, per)],
            out.at[pl.ds(chan0 + chunk * per, per)],
            o_send.at[chunk, step], o_recv.at[chunk, step], {"gx": peer(step)},
        )

    @pl.loop(0, chunks)
    def _(chunk):
        @pl.loop(0, per)
        def _(lower):
            c = chunk * per + lower
            for way in range(2):
                g_copy(way, c).wait_recv()

            @pl.loop(0, xgroups)
            def _(group):
                packed = edges_of(ghalo_in[0, c, group], ghalo_in[1, c, group])
                for m in range(32):
                    at = pl.ds(m % 4 * 8, 8)
                    x = group * 8 + m // 4
                    edge = pltpu.roll(packed, (126 - 4 * m) % 128, 1)
                    moved = shifts(gsm[c, x, at, :], edge)
                    for j in range(5):
                        zgrad[j, c, x, at, :] = moved[j]

            @pl.loop(0, size, unroll=2)
            def _(s):
                for xl in range(2):
                    gstage[s, pl.ds(xl, 32, stride=2), :] = filtered(zgrad, c, 2 * s + xl, True)
                gout[s, c] = gstage[s].astype(BF16)

            out[chan0 + c] = gout[gx, c]

        for step in range(1, size):
            o_copy(chunk, step).start()

    row = lax.broadcasted_iota(jnp.int32, (8, 128), 0)

    @pl.loop(0, cpg)
    def _(c):
        def body(x, sums25):
            grad = gsm[c, x]
            news = []
            for i in range(5):
                at = lax.rem(x + i - 2 + xs, xs)
                for j in range(5):
                    news.append(sums25[5 * i + j] + fold(zfeat[j, c, at] * grad))
            return tuple(news)

        sums25 = lax.fori_loop(0, xs, body, tuple(jnp.zeros((8, 128), F32) for q in range(25)), unroll=2)
        for q in range(38):
            value = sums25[q] if q < 25 else acc[c, q]
            red[pl.ds(q, 1), :] = jnp.sum(value, axis=0, keepdims=True)
        line = lax.dot_general(
            jnp.ones((8, 128), F32), red[...], (((1,), (1,)), ((), ())),
            precision=lax.Precision.HIGHEST, preferred_element_type=F32,
        )
        before = jnp.where(c == 0, jnp.zeros((8, 128), F32), sums[me])
        sums[me] = jnp.where(row == c, line, before)

    def r_copy(step):
        return remote(sums.at[me], sums.at[me], r_send.at[step], r_recv.at[step], coords(step))

    @pl.loop(1, everyone)
    def _(step):
        r_copy(step).start()

    @pl.loop(1, everyone)
    def _(step):
        r_copy(step).wait_recv()

    @pl.loop(0, size)
    def _(group):
        total = sums[group * depth * 2]
        for member in range(1, depth * 2):
            total = total + sums[group * depth * 2 + member]
        red[pl.ds(group * cpg, cpg), :] = total[0:cpg] / volume

    turned = red[...].T
    chans = size * cpg
    tile_out[...] = red[0:chans, 0:25]
    wall_out[...] = turned[25:34, 0:chans]
    class_out[...] = turned[34:38, 0:chans]

    for chunk in range(chunks):
        for step in range(1, size):
            o_copy(chunk, step).wait()
            a_copy(chunk, step).wait_send()
    for way in range(2):
        for step in range(size):
            h_copy(way, step).wait_send()
        for c in range(cpg):
            g_copy(way, c).wait_send()
    for c in range(cpg):
        s_copy(c).wait_send()
    for step in range(1, size):
        p_copy(step).wait_send()
        e_copy(step).wait_send()
    for step in range(size):
        w_copy(step).wait_send()

    @pl.loop(1, everyone)
    def _(step):
        r_copy(step).wait_send()


OWN = 32
WIN = OWN + 8
BLOCK = 12
BLOCKS = (WIN - 4) // BLOCK
ROWS = BLOCK * 8
HALF = ROWS // 2
PIECES = ((0, 2), (2, 6), (8, 6), (14, 4), (18, 2))
ARRIVE = ((0, 1), (2,), (3, 4))
WANTED = 38
HIGH = lax.Precision.HIGHEST


def cast_dot(a, b, dims=((1,), (0,))):
    return lax.dot_general(
        a.astype(BF16), b.astype(BF16), (dims, ((), ())), preferred_element_type=F32
    )


def split_dot(a, b):
    a_high, b_high = a.astype(BF16), b.astype(BF16)
    a_low, b_low = (a - a_high.astype(F32)).astype(BF16), (b - b_high.astype(F32)).astype(BF16)
    return cast_dot(a_high, b_high) + (cast_dot(a_high, b_low) + cast_dot(a_low, b_high))


def dot(a, b, dims=((1,), (0,))):
    return lax.dot_general(a, b, (dims, ((), ())), precision=HIGH, preferred_element_type=F32)


def region_kernel(
    dims,
    feat_h, lab_h, index_h, stretch_h, tile_h, wall_h, class_h,
    ghome, sums,
    feat, lab, index, stretch, tile_w, wall_w, class_w,
    turn, send, recv, lab_rows, lab_send, lab_recv, lab_wide, lab_win,
    field, odd, smooth, gwall, gsm, godd, hid, slope, part_out, part_in,
    taps, fore, wide, wide_t, band_tile, wall, wall_acc, acc, gram, params, classes, classes_t,
    gout, mine, red,
    in_sem, f_send, f_recv, l_send, l_recv, p_send, p_recv, g_send, g_recv, r_send, r_recv,
):
    size, depth, volume = dims
    everyone = size * depth * 2
    gx, gz, col = lax.axis_index("gx"), lax.axis_index("gz"), lax.axis_index("col")
    me = (gx * depth + gz) * 2 + col
    right, left = lax.rem(gz + 1, depth), lax.rem(gz + depth - 1, depth)
    zps = OWN // 2
    lane = lax.broadcasted_iota(jnp.int32, (8, 128), 1)
    row = lax.broadcasted_iota(jnp.int32, (8, 128), 0)
    first = lane < 64
    y_lane = lax.rem(lane, 64) // 2
    x_even = lax.rem(lane, 2) == 0

    ins = [
        pltpu.make_async_copy(src, dst, in_sem.at[n])
        for n, (src, dst) in enumerate((
            (feat_h, feat), (lab_h, lab), (index_h, index), (stretch_h, stretch),
            (tile_h, tile_w), (wall_h, wall_w), (class_h, class_w),
        ))
    ]
    for copy in ins:
        copy.start()

    def coords(step):
        place = lax.rem(me + step, everyone)
        return {
            "gx": place // (2 * depth),
            "gz": lax.rem(place // 2, depth),
            "col": lax.rem(place, 2),
        }

    barrier = pltpu.get_barrier_semaphore()

    @pl.loop(1, everyone)
    def _(step):
        pl.semaphore_signal(barrier, inc=1, device_id=coords(step), device_id_type=MESH)

    def remote(src, dst, sent, got, device):
        return pltpu.make_async_remote_copy(
            src_ref=src, dst_ref=dst, send_sem=sent, recv_sem=got,
            device_id=device, device_id_type=MESH,
        )

    def target(sx):
        return lax.rem(gx + sx, size)

    def origin(sx):
        return lax.rem(gx + size - sx, size)

    ins[0].wait()
    for side in range(2):
        for cp in range(8):
            block = feat[pl.ds(side * 16 + 2 * cp, 2)].astype(F32).reshape(128, 128)
            turn[side, pl.ds(cp, 128, stride=8), :] = block.T

        @pl.loop(0, 64, unroll=8)
        def _(zp, side=side):
            at = pl.ds(pl.multiple_of(zp * 16, 16), 16)
            send[side, zp] = turn[side, at, :].astype(BF16)

    ins[1].wait()
    turn[2, 0:128, :] = lab[...].astype(F32).T
    even, uneven = turn[2, pl.ds(0, 64, stride=2), :], turn[2, pl.ds(1, 64, stride=2), :]
    here = jnp.where(col == 0, even, pltpu.roll(even, 64, 1))
    there = jnp.where(col == 0, pltpu.roll(uneven, 64, 1), uneven)
    lab_rows[...] = jnp.where(lax.broadcasted_iota(jnp.int32, (64, 128), 1) < 64, here, there)
    for t in range(size):
        lab_send[t] = lab_rows[pl.ds(zps * t, zps), :].astype(BF16)
    edge_rows = [jnp.zeros((1, 128), F32)] * 16
    for t in range(size):
        edge_rows[2 * t] = lab_rows[pl.ds((zps * t - 1) % 64, 1), :]
        edge_rows[2 * t + 1] = lab_rows[pl.ds((zps * t + zps) % 64, 1), :]
    lab_send[size] = jnp.concatenate(edge_rows, axis=0).astype(BF16)

    pl.semaphore_wait(barrier, everyone - 1)

    def f_spot(piece, t):
        at, count = PIECES[piece]
        return pl.ds(lax.rem(t * zps + at - 2 + 64, 64), count), pl.ds(at, count)

    def f_far(piece, sx, sc):
        t, ct = target(sx), lax.rem(col + sc, 2)
        src, dst = f_spot(piece, t)
        if piece == 0:
            tz = lax.rem(gz + 1 - (t + size - 1) // size, depth)
        elif piece == len(PIECES) - 1:
            tz = lax.rem(gz + depth - (t + 1) // size, depth)
        else:
            tz = gz
        return remote(
            send.at[ct, src], recv.at[gx, col, dst],
            f_send.at[piece, sx, sc], f_recv.at[piece, sx, sc],
            {"gx": t, "gz": tz, "col": ct},
        )

    def f_near(piece):
        src, dst = f_spot(piece, gx)
        return pltpu.make_async_copy(
            send.at[col, src], recv.at[gx, col, dst], f_recv.at[piece, 0, 0]
        )

    def f_wait(piece, sx, sc):
        at, count = PIECES[piece]
        slot = recv.at[origin(sx), lax.rem(col + sc, 2), pl.ds(at, count)]
        return remote(
            slot, slot, f_send.at[piece, sx, sc], f_recv.at[piece, sx, sc],
            {"gx": target(sx), "gz": gz, "col": lax.rem(col + sc, 2)},
        )

    def own_piece(piece, near, far):
        if piece == 0:
            pl.when(gx > 0)(near)
            pl.when(gx == 0)(far)
        elif piece == len(PIECES) - 1:
            pl.when(gx < size - 1)(near)
            pl.when(gx == size - 1)(far)
        else:
            near()

    others = [(sx, sc) for sx in (2, 1, 3, 0) for sc in range(2) if sx or sc]

    def l_mid(sx):
        return remote(
            lab_send.at[target(sx)], lab_recv.at[gx, 0], l_send.at[0, sx], l_recv.at[0, sx],
            {"gx": target(sx)},
        )

    def l_edge(sx):
        return remote(
            lab_send.at[size], lab_recv.at[gx, 1], l_send.at[1, sx], l_recv.at[1, sx],
            {"gx": target(sx)},
        )

    def l_far(sx):
        t = target(sx)
        tz = lax.rem(gz + depth + 1 - 2 * ((t + 1) // size), depth)
        return remote(
            lab_send.at[size], lab_recv.at[gx, 2], l_send.at[2, sx], l_recv.at[2, sx],
            {"gx": t, "gz": tz},
        )

    l_own = [
        pltpu.make_async_copy(lab_send.at[gx], lab_recv.at[gx, 0], l_recv.at[0, 0]),
        pltpu.make_async_copy(lab_send.at[size], lab_recv.at[gx, 1], l_recv.at[1, 0]),
    ]

    for block in range(BLOCKS):
        for piece in ARRIVE[block]:
            for sx, sc in others:
                f_far(piece, sx, sc).start()
            own_piece(
                piece,
                lambda piece=piece: f_near(piece).start(),
                lambda piece=piece: f_far(piece, 0, 0).start(),
            )
        if block == 0:
            for copy in l_own:
                copy.start()
            for sx in range(size):
                if sx:
                    l_mid(sx).start()
                    l_edge(sx).start()
                l_far(sx).start()

    for copy in ins[2:]:
        copy.wait()
    params[...] = jnp.zeros((128, 128), F32)
    params[0:9, 0:32] = wall_w[...]
    params[16:20, 0:32] = class_w[...]
    params[64:96, 0:25] = tile_w[...]
    red[...] = params[...].T

    def pairs(ref, start):
        return ref[pl.ds(start + col * 16, 8, stride=2), :], ref[pl.ds(start + col * 16 + 1, 8, stride=2), :]

    def spread(both, q):
        low, high = (jnp.broadcast_to(rows[:, q : q + 1], (8, 128)) for rows in both)
        return jnp.where(first, low, high)

    tile_pairs, wall_pairs = pairs(params, 64), pairs(red, 0)
    for q in range(25):
        taps[q] = spread(tile_pairs, q)

    levels = stretch.shape[0]
    hot = lax.broadcasted_iota(jnp.int32, (levels, 64), 0) == index[...]
    params[32:41, 0:64] = dot(stretch[...], hot.astype(F32), ((0,), (0,)))
    band_t = params[32:48, 0:64]
    y_row = lax.broadcasted_iota(jnp.int32, (64, 128), 0)
    y_col = lax.rem(lax.broadcasted_iota(jnp.int32, (64, 128), 1), 64) // 2
    square_row = lax.broadcasted_iota(jnp.int32, (128, 128), 0)
    square_lane = lax.broadcasted_iota(jnp.int32, (128, 128), 1)
    k_of_lane = lax.rem(lax.broadcasted_iota(jnp.int32, (16, 128), 1) // 2 + 4, 64)
    k_of_lane = (k_of_lane == lax.broadcasted_iota(jnp.int32, (16, 128), 0)) & (
        lax.rem(lax.broadcasted_iota(jnp.int32, (16, 128), 1), 2) == 0
    )
    placed = dot(band_t, k_of_lane.astype(F32), ((0,), (0,)))
    for yh in range(2):
        ahead = dot(band_t, (y_row == y_col + 32 * yh).astype(F32))
        for k in range(9):
            m = k - 4
            value = spread(wall_pairs, k) * ahead[k : k + 1, :]
            inside = (y_lane + m >= 0) & (y_lane + m < 32)
            fore[k, yh] = jnp.where(inside, value, 0.0)
            across = (y_lane + m >= 32) if yh == 0 else (y_lane + m < 0)
            fore[k, 2 + yh] = jnp.where(across, value, 0.0)
        rows_y = lax.broadcasted_iota(jnp.int32, (128, 64), 0) % 64 // 2 + 32 * yh
        at_y = rows_y == lax.broadcasted_iota(jnp.int32, (128, 64), 1)
        value = dot(at_y.astype(F32), placed)
        shift = lax.rem(square_lane // 2 + 4, 64) - 4 + square_row % 64 // 2
        inner = jnp.where((shift >= 0) & (shift < 32), value, 0.0)
        outer = jnp.where((shift >= 0) & (shift < 32), 0.0, value)
        band_tile[yh] = pltpu.roll(inner, 0, 1, stride=1, stride_axis=0)
        band_tile[2 + yh] = pltpu.roll(outer, 64, 1, stride=1, stride_axis=0)

    @pl.loop(0, 8, unroll=2)
    def _(cp):
        for yh in range(2):
            tile = jnp.zeros((128, 128), F32)
            for k in range(9):
                line = fore[k, yh, pl.ds(cp, 1), :]
                tile = jnp.where(square_row == square_lane + 2 * (k - 4), line, tile)
            wide[cp, 128 * yh : 128 * yh + 128, 128 * yh : 128 * yh + 128] = tile.astype(BF16)
            wide_t[cp, 128 * yh : 128 * yh + 128, 128 * yh : 128 * yh + 128] = tile.T.astype(BF16)
            tile = jnp.zeros((128, 128), F32)
            for k in range(5, 9) if yh == 0 else range(4):
                line = fore[k, 2 + yh, pl.ds(cp, 1), :]
                far = 2 * (k - 4) - 64 if yh == 0 else 2 * (k - 4) + 64
                tile = jnp.where(square_row == square_lane + far, line, tile)
            low, high = 128 - 128 * yh, 128 * yh
            wide[cp, low : low + 128, high : high + 128] = tile.astype(BF16)
            wide_t[cp, high : high + 128, low : low + 128] = tile.T.astype(BF16)

    chan = lax.broadcasted_iota(jnp.int32, (128, 128), 0)
    unit = lax.rem(lax.broadcasted_iota(jnp.int32, (128, 128), 1), 8)
    half_row = lax.broadcasted_iota(jnp.int32, (HALF, 128), 0)
    half_z = lax.broadcasted_iota(jnp.int32, (HALF, 128), 1) // 8
    half_k = lax.rem(half_row, 8) // 2
    same_z = (half_row // 8) * 2 + lax.rem(half_row, 2) == half_z
    classes[...] = jnp.zeros((128, 128), F32)
    for par in range(2):
        rows = dot(params[16:24, :], (chan == col * 16 + 2 * unit + par).astype(F32))
        value = jnp.zeros((HALF, 128), F32)
        for k in range(4):
            value = jnp.where(same_z & (half_k == k), rows[k : k + 1, :], value)
        classes[pl.ds(HALF * par, HALF), :] = value
    classes_t[...] = classes[...].T

    def arrived(block):
        for piece in ARRIVE[block]:
            for sx, sc in others:
                f_wait(piece, sx, sc).wait_recv()
            own_piece(
                piece,
                lambda piece=piece: f_near(piece).wait(),
                lambda piece=piece: f_wait(piece, 0, 0).wait_recv(),
            )
        low, high = PIECES[ARRIVE[block][0]][0], sum(PIECES[ARRIVE[block][-1]])

        @pl.loop(0, 2 * size)
        def _(t):
            for zp in range(low, high):
                pair = recv[t // 2, lax.rem(t, 2), zp].astype(F32)
                field[t, 2 * zp] = pair[0:8]
                field[t, 2 * zp + 1] = pair[8:16]

        between(seen(field), odd, 2 * low, 2 * high)

    def seen(ref):
        return lambda t, z: ref[t, z]

    def seen_rows(ref):
        return lambda t, z: ref[lax.rem(t, 2), spot(z, t // 2), :]

    def between(src, dst, low, high):
        @pl.loop(0, 2 * size)
        def _(t):
            after = lax.rem(t + 2, 2 * size)
            for z in range(low, high):
                dst[t, z] = jnp.where(
                    x_even, pltpu.roll(src(t, z), 127, 1), pltpu.roll(src(after, z), 1, 1)
                )

    def filtered(src, mid, t, low, count, flip, put):
        before, after = lax.rem(t + 2 * size - 2, 2 * size), lax.rem(t + 2, 2 * size)
        totals = [None] * count
        for z in range(count + 4):
            at = low + z - 2
            views = (src(before, at), mid[before, at], src(t, at), mid[t, at], src(after, at))
            for j in range(5):
                if 0 <= z - j < count:
                    for i in range(5):
                        q = 5 * (4 - i) + 4 - j if flip else 5 * i + j
                        term = taps[q] * views[i]
                        old = totals[z - j]
                        totals[z - j] = term if old is None else old + term
            if z >= 4:
                put(z - 4, totals)

    def spot(z, p):
        return pl.ds(pl.multiple_of((z * size + p) * 8, 8), 8)

    def unit_rows(z, count, cp):
        return pl.ds(z * size * 8 + cp, count * size, stride=8)

    def unit_of(ref, z, count, cp):
        at = unit_rows(z, count, cp)
        return jnp.concatenate([ref[0, at, :], ref[1, at, :]], axis=1).astype(BF16)

    def p_copy(block):
        return remote(
            part_out.at[block], part_in.at[block], p_send.at[block], p_recv.at[block],
            {"col": 1 - col},
        )

    def ahead_of(block):
        base = 2 + BLOCK * block

        @pl.loop(0, 2 * size)
        def _(t):
            def put(z, totals):
                smooth[lax.rem(t, 2), spot(base + z, t // 2), :] = rounded(totals[z])

            filtered(seen(field), odd, t, base, BLOCK, False, put)

        @pl.loop(0, 8, unroll=8)
        def _(cp):
            both = jnp.dot(
                unit_of(smooth, base, BLOCK, cp), wide[cp], preferred_element_type=F32
            )
            for yh in range(2):
                wall[yh, unit_rows(0, BLOCK, cp), :] = both[:, 128 * yh : 128 * yh + 128]

        @pl.loop(0, BLOCK)
        def _(z):
            at = pl.ds(pl.multiple_of(8 * z, 8), 8)
            for p in range(size):
                for yh in range(2):
                    value = wall[yh, spot(z, p), :]
                    sig = jax.nn.sigmoid(value)
                    lanes = slice(128 * yh, 128 * yh + 128)
                    hid[block, p, at, lanes] = value * sig
                    slope[block, p, at, lanes] = sig * (1.0 + value * (1.0 - sig))

        left_half = lax.rem(lax.broadcasted_iota(jnp.int32, (HALF, 256), 1), 128) < 64

        @pl.loop(0, size, unroll=size)
        def _(p):
            part = split_dot(classes[0:ROWS, 0:ROWS], hid[block, p])
            part_out[block, p] = jnp.where(left_half, part[0:HALF], part[HALF:ROWS])
            lanes = pl.ds(pl.multiple_of(128 * col, 128), 128)
            for zp in range(BLOCK // 2):
                at = slice(8 * zp, 8 * zp + 8)
                mark = lab_win[p, pl.ds(BLOCK // 2 * block + zp, 1), :]
                mark = jnp.broadcast_to(mark, (8, 128))
                mark = jnp.where(lax.rem(row, 2) == 0, mark, pltpu.roll(mark, 64, 1))
                hit = first & (mark == (row // 2).astype(F32))
                part_out[block, p, at, lanes] = part_out[block, p, at, lanes] - jnp.where(hit, 1.0, 0.0)

        p_copy(block).start()

    def back_of(block):
        base = 2 + BLOCK * block
        p_copy(block).wait_recv()
        left_half = lax.rem(lax.broadcasted_iota(jnp.int32, (HALF, 256), 1), 128) < 64

        @pl.loop(0, size, unroll=size)
        def _(p):
            err = part_out[block, p] + part_in[block, p]
            swapped = jnp.concatenate(
                [pltpu.roll(err[:, 0:128], 64, 1), pltpu.roll(err[:, 128:256], 64, 1)], axis=1
            )
            err = err + swapped
            both = jnp.concatenate(
                [jnp.where(left_half, err, 0.0), jnp.where(left_half, 0.0, err)], axis=0
            )
            grad = split_dot(classes_t[0:ROWS, 0:ROWS], both) * slope[block, p]
            for z in range(BLOCK):
                for yh in range(2):
                    gwall[yh, spot(base + z, p), :] = rounded(
                        grad[8 * z : 8 * z + 8, 128 * yh : 128 * yh + 128]
                    )
            new = cast_dot(both, hid[block, p], ((1,), (1,)))
            gram[block, p] = new

        @pl.loop(0, 8, unroll=8)
        def _(cp):
            both = jnp.dot(
                unit_of(gwall, base, BLOCK, cp), wide_t[cp], preferred_element_type=F32
            )
            for yh in range(2):
                at = unit_rows(base, BLOCK, cp)
                gsm[yh, at, :] = rounded(both[:, 128 * yh : 128 * yh + 128])

        between(seen_rows(gsm), godd, base, base + BLOCK)

    def g_spot(block):
        low = 4 if block == 0 else BLOCK * block
        return low, BLOCK * block + BLOCK - low

    def g_copy(block, step):
        low, count = g_spot(block)
        at, many = (low - 4) // 2, count // 2
        p, yh = target(step // 2), lax.rem(col + step, 2)
        return remote(
            gout.at[2 * p + yh, pl.ds(at, many)],
            ghome.at[col, pl.ds(gx * zps + at, many)],
            g_send.at[block, step], g_recv.at[block, step], {"gx": p, "col": yh},
        )

    def g_near(block):
        low, count = g_spot(block)
        at, many = (low - 4) // 2, count // 2
        return pltpu.make_async_copy(
            gout.at[2 * gx + col, pl.ds(at, many)],
            ghome.at[col, pl.ds(gx * zps + at, many)],
            g_recv.at[block, 0],
        )

    def g_wait(block, step):
        low, count = g_spot(block)
        at, many = (low - 4) // 2, count // 2
        slot = ghome.at[lax.rem(col + step, 2), pl.ds(origin(step // 2) * zps + at, many)]
        return remote(
            slot, slot, g_send.at[block, step], g_recv.at[block, step],
            {"gx": target(step // 2), "col": lax.rem(col + step, 2)},
        )

    def home(block):
        low, count = g_spot(block)

        @pl.loop(0, 2 * size)
        def _(turn_at):
            step = lax.rem(turn_at + 4, 2 * size)
            t = 2 * target(step // 2) + lax.rem(col + step, 2)

            def put(z, totals):
                if z % 2:
                    pair = jnp.concatenate([totals[z - 1], totals[z]], axis=0)
                    gout[t, (low - 4 + z) // 2] = pair.astype(BF16)

            filtered(seen_rows(gsm), godd, t, low, count, True, put)

            @pl.when(step > 0)
            def _():
                g_copy(block, step).start()

            @pl.when(step == 0)
            def _():
                g_near(block).start()

    def labels_in():
        for sx in range(size):
            if sx:
                for slot in range(2):
                    at = lab_recv.at[origin(sx), slot]
                    remote(
                        at, at, l_send.at[slot, sx], l_recv.at[slot, sx], {"gx": target(sx)}
                    ).wait_recv()
            at = lab_recv.at[origin(sx), 2]
            remote(
                at, at, l_send.at[2, sx], l_recv.at[2, sx], {"gx": target(sx), "gz": right}
            ).wait_recv()
        for copy in l_own:
            copy.wait()
        low_edge = 2 - (gx + size - 1) // size
        high_edge = 1 + (gx + 1) // size
        for p in range(size):
            lab_win[p, 1 : 1 + zps, :] = lab_recv[p, 0].astype(F32)
            for slot in range(1, 3):
                lab_wide[p, slot] = lab_recv[p, slot].astype(F32)
            lab_win[p, 0:1, :] = lab_wide[p, low_edge, pl.ds(2 * gx, 1), :]
            lab_win[p, 1 + zps : 2 + zps, :] = lab_wide[p, high_edge, pl.ds(2 * gx + 1, 1), :]

    arrived(0)
    labels_in()
    ahead_of(0)
    arrived(1)
    ahead_of(1)
    back_of(0)
    home(0)
    arrived(2)
    ahead_of(2)
    back_of(1)
    home(1)
    back_of(2)
    home(2)

    def tile_body(it, sums25):
        t, base = it // 4, 4 + 8 * lax.rem(it, 4)
        before, after = lax.rem(t + 2 * size - 2, 2 * size), lax.rem(t + 2, 2 * size)
        grads = [seen_rows(gsm)(t, base + z) for z in range(8)]
        news = list(sums25)
        for z in range(12):
            at = base + z - 2
            views = (
                field[before, at], odd[before, at], field[t, at], odd[t, at], field[after, at]
            )
            for j in range(5):
                if 0 <= z - j < 8:
                    for i in range(5):
                        news[5 * i + j] = news[5 * i + j] + views[i] * grads[z - j]
        return tuple(news)

    sums25 = lax.fori_loop(
        0, 8 * size, tile_body, tuple(jnp.zeros((8, 128), F32) for q in range(25))
    )
    for q in range(25):
        acc[8 * q : 8 * q + 8, :] = sums25[q]

    @pl.loop(0, 8, unroll=8)
    def _(cp):
        grads, fields = unit_of(gwall, 4, OWN, cp), unit_of(smooth, 4, OWN, cp)
        both = cast_dot(grads, fields, ((0,), (0,)))
        for par in range(2):
            wall_acc[par, cp] = jnp.zeros((8, 128), F32)
        for yh in range(2):
            here, far = slice(128 * yh, 128 * yh + 128), slice(128 - 128 * yh, 256 - 128 * yh)
            for g in range(16):
                at = slice(128 * yh + 8 * g, 128 * yh + 8 * g + 8)
                tile = both[at, here] * band_tile[yh, 8 * g : 8 * g + 8, :]
                if g % 8 == (0 if yh else 7):
                    edge = both[at, far] * band_tile[2 + yh, 8 * g : 8 * g + 8, :]
                    tile = tile + pltpu.roll(edge, 64, 1)
                wall_acc[g // 8, cp] = wall_acc[g // 8, cp] + pltpu.roll(tile, (128 - 8 * g) % 128, 1)

    inner_row = lax.rem(lax.broadcasted_iota(jnp.int32, (64, 128), 0), 8)
    halves = lax.broadcasted_iota(jnp.int32, (128, 128), 0) // 64
    parity = lax.rem(lax.broadcasted_iota(jnp.int32, (128, 128), 1), 2)
    lines = dot(acc[...], (halves == parity).astype(F32))
    total = jnp.zeros((8, 128), F32)
    for q in range(25):
        total = jnp.where(lane // 2 == q, lines[8 * q : 8 * q + 8, :], total)

    full_row = lax.broadcasted_iota(jnp.int32, (ROWS, ROWS), 0)
    full_lane = lax.broadcasted_iota(jnp.int32, (ROWS, ROWS), 1)
    row_z = lax.rem(full_row, HALF) // 8 * 2 + lax.rem(full_row, 2)
    matrix = jnp.zeros((ROWS, ROWS), F32)
    for block in range(BLOCKS):
        base = 2 + BLOCK * block
        value = gram[block, 0]
        for p in range(1, size):
            value = value + gram[block, p]
        keep = (row_z == full_lane // 8) & (row_z + base >= 4) & (row_z + base < 4 + OWN)
        matrix = matrix + jnp.where(keep, value, 0.0)
    gather = (
        lax.broadcasted_iota(jnp.int32, (8, ROWS), 0)
        == lax.rem(lax.broadcasted_iota(jnp.int32, (8, ROWS), 1), 8)
    ).astype(F32)
    by_row = dot(gather, matrix, ((1,), (1,)))
    source_row = lax.broadcasted_iota(jnp.int32, (ROWS, 128), 0)
    place = 2 * (34 + lax.rem(source_row, 8) // 2) + source_row // HALF
    place = place == lax.broadcasted_iota(jnp.int32, (ROWS, 128), 1)
    total = total + dot(by_row, place.astype(F32))
    stack = (
        lax.broadcasted_iota(jnp.int32, (8, 64), 0)
        == lax.broadcasted_iota(jnp.int32, (8, 64), 1) // 8
    ).astype(F32)
    for par in range(2):
        value = wall_acc[par].reshape(64, 128)
        for r in range(1, 8):
            value = jnp.where(inner_row == r, pltpu.roll(value, 128 - r, 1), value)
        by_lane = dot(stack, value)
        source = lax.rem(square_row // 2 + 4, 64)
        place = (lax.rem(square_row, 2) == 0) & (source < 9) & (
            square_lane == 2 * (25 + source) + par
        )
        total = total + dot(by_lane, place.astype(F32))
    mine[...] = total

    def r_copy(step):
        return remote(mine, sums.at[me], r_send.at[step], r_recv.at[step], coords(step))

    r_own = pltpu.make_async_copy(mine, sums.at[me], r_recv.at[0])
    r_own.start()

    @pl.loop(1, everyone)
    def _(step):
        r_copy(step).start()

    for block in range(BLOCKS):
        for step in range(1, 2 * size):
            g_wait(block, step).wait_recv()
        g_near(block).wait()

    def r_wait(step):
        place = lax.rem(me + everyone - step, everyone)
        return remote(
            sums.at[place], sums.at[place], r_send.at[step], r_recv.at[step], coords(step)
        )

    @pl.loop(1, everyone)
    def _(step):
        r_wait(step).wait_recv()

    r_own.wait()
    for piece in range(len(PIECES)):
        for sx, sc in others:
            f_far(piece, sx, sc).wait_send()
    pl.when(gx == 0)(lambda: f_far(0, 0, 0).wait_send())
    pl.when(gx == size - 1)(lambda: f_far(len(PIECES) - 1, 0, 0).wait_send())
    for sx in range(size):
        if sx:
            l_mid(sx).wait_send()
            l_edge(sx).wait_send()
        l_far(sx).wait_send()
    for block in range(BLOCKS):
        p_copy(block).wait_send()
        for step in range(1, 2 * size):
            g_copy(block, step).wait_send()

    @pl.loop(1, everyone)
    def _(step):
        r_copy(step).wait_send()


def last_kernel(volume, home, sums, out, tile_out, wall_out, class_out, turn, red):
    side = pl.program_id(0)
    members = sums.shape[0] // 2

    @pl.loop(0, 64, unroll=8)
    def _(zp):
        at = pl.ds(pl.multiple_of(zp * 16, 16), 16)
        turn[at, :] = home[0, zp].astype(F32)

    for cp in range(8):
        block = turn[pl.ds(cp, 128, stride=8), :].T
        out[pl.ds(2 * cp, 2)] = block.reshape(2, 64, 128).astype(BF16)

    @pl.when(side == 0)
    def _():
        spot = lax.broadcasted_iota(jnp.int32, (128, 128), 0)
        want = 2 * lax.broadcasted_iota(jnp.int32, (128, 128), 1)
        red[...] = jnp.zeros((128, 128), F32)
        for half in range(2):
            total = sums[half]
            for member in range(1, members):
                total = total + sums[2 * member + half]
            total = total / volume
            for par in range(2):
                red[pl.ds(half * 16 + par, 8, stride=2), :] = dot(
                    total, (spot == want + par).astype(F32)
                )
        turned = red[...].T
        tile_out[...] = red[0:32, 0:25]
        wall_out[...] = turned[25:34, 0:32]
        class_out[...] = turned[34:38, 0:32]


def regional(
    size, depth, volume,
    features, labels, grid_index, stretch, tile_filter, wall_filter, class_weight,
):
    chans = features.shape[0]
    levels = stretch.shape[0]
    everyone = size * depth * 2
    dma = pltpu.SemaphoreType.DMA
    far = pl.BlockSpec(memory_space=pl.ANY)
    wide = pltpu.VMEM((2 * size, WIN, 8, 128), F32)
    rows = pltpu.VMEM((2, WIN * size * 8, 128), F32)
    block = pltpu.VMEM((BLOCKS, size, ROWS, 256), F32)
    half = pltpu.VMEM((BLOCKS, size, HALF, 256), F32)
    home, sums = pl.pallas_call(
        functools.partial(region_kernel, (size, depth, volume)),
        out_shape=(
            jax.ShapeDtypeStruct((2, 64, 16, 128), BF16),
            jax.ShapeDtypeStruct((everyone, 8, 128), F32),
        ),
        in_specs=[far] * 7,
        out_specs=(far, far),
        scratch_shapes=[
            pltpu.VMEM((chans, 64, 128), BF16),
            pltpu.VMEM((128, 128), jnp.int32),
            pltpu.VMEM((1, 64), jnp.int32),
            pltpu.VMEM((levels, 9), F32),
            pltpu.VMEM((chans, 25), F32),
            pltpu.VMEM((9, chans), F32),
            pltpu.VMEM((4, chans), F32),
            pltpu.VMEM((3, 1024, 128), F32),
            pltpu.VMEM((2, 64, 16, 128), BF16),
            pltpu.VMEM((size, 2, WIN // 2, 16, 128), BF16),
            pltpu.VMEM((64, 128), F32),
            pltpu.VMEM((size + 1, 16, 128), BF16),
            pltpu.VMEM((size, 3, 16, 128), BF16),
            pltpu.VMEM((size, 3, 16, 128), F32),
            pltpu.VMEM((size, 24, 128), F32),
            wide, wide, rows, rows, rows, wide,
            block, block, half, half,
            pltpu.VMEM((25, 8, 128), F32),
            pltpu.VMEM((9, 4, 8, 128), F32),
            pltpu.VMEM((8, 256, 256), BF16),
            pltpu.VMEM((8, 256, 256), BF16),
            pltpu.VMEM((4, 128, 128), F32),
            pltpu.VMEM((2, ROWS * size, 128), F32),
            pltpu.VMEM((2, 8, 8, 128), F32),
            pltpu.VMEM((25 * 8, 128), F32),
            pltpu.VMEM((BLOCKS, size, ROWS, ROWS), F32),
            pltpu.VMEM((128, 128), F32),
            pltpu.VMEM((128, 128), F32),
            pltpu.VMEM((128, 128), F32),
            pltpu.VMEM((2 * size, OWN // 2, 16, 128), BF16),
            pltpu.VMEM((8, 128), F32),
            pltpu.VMEM((128, 128), F32),
            dma((7,)),
            dma((len(PIECES), size, 2)), dma((len(PIECES), size, 2)),
            dma((3, size)), dma((3, size)),
            dma((BLOCKS,)), dma((BLOCKS,)),
            dma((BLOCKS, 2 * size)), dma((BLOCKS, 2 * size)),
            dma((everyone,)), dma((everyone,)),
        ],
        compiler_params=pltpu.CompilerParams(
            collective_id=0, has_side_effects=True, vmem_limit_bytes=63 * 1024 * 1024
        ),
    )(
        features.reshape(chans, 64, 128), labels.reshape(128, 128), grid_index.reshape(1, 64),
        stretch, tile_filter, wall_filter.T, class_weight,
    )
    def whole(*shape):
        return pl.BlockSpec(shape, lambda side: (0,) * len(shape))

    grad, tile_grad, wall_grad, class_grad = pl.pallas_call(
        functools.partial(last_kernel, volume),
        grid=(2,),
        out_shape=(
            jax.ShapeDtypeStruct((chans, 64, 128), BF16),
            jax.ShapeDtypeStruct((chans, 25), F32),
            jax.ShapeDtypeStruct((9, chans), F32),
            jax.ShapeDtypeStruct((4, chans), F32),
        ),
        in_specs=[
            pl.BlockSpec((1, 64, 16, 128), lambda side: (side, 0, 0, 0)),
            whole(everyone, 8, 128),
        ],
        out_specs=(
            pl.BlockSpec((chans // 2, 64, 128), lambda side: (side, 0, 0)),
            whole(chans, 25), whole(9, chans), whole(4, chans),
        ),
        scratch_shapes=[pltpu.VMEM((1024, 128), F32), pltpu.VMEM((128, 128), F32)],
    )(home, sums)
    return grad.reshape(features.shape), tile_grad, wall_grad.T, class_grad


def shards(features, labels, grid_index, stretch, tile_filter, wall_filter, class_weight):
    chans, rows, cells_x, cells_z = features.shape
    size, depth = lax.axis_size("gx"), lax.axis_size("gz")
    volume = labels.shape[0] * cells_x * size * cells_z * depth
    cpg = chans // size
    if 128 // size == OWN:
        return regional(
            size, depth, volume,
            features, labels, grid_index, stretch, tile_filter, wall_filter, class_weight,
        )
    chunks = min(4, cpg)
    per_dest = max(cpg // 4, 1) * 8
    xs = 2 * size
    everyone = size * depth * 2
    onehot = (grid_index[:, None] == jnp.arange(stretch.shape[0], dtype=jnp.int32)).astype(F32)
    bands = jnp.dot(onehot, stretch, precision=lax.Precision.HIGHEST)
    dma = pltpu.SemaphoreType.DMA
    vmem = pl.BlockSpec(memory_space=pltpu.VMEM)
    smem = pl.BlockSpec(memory_space=pltpu.SMEM)
    grad, tile_grad, wall_grad, class_grad = pl.pallas_call(
        functools.partial(kernel, (size, depth, cpg, chunks, volume)),
        out_shape=(
            jax.ShapeDtypeStruct((chans, 64, 128), BF16),
            jax.ShapeDtypeStruct((chans, 25), F32),
            jax.ShapeDtypeStruct((9, chans), F32),
            jax.ShapeDtypeStruct((4, chans), F32),
        ),
        in_specs=[vmem, vmem, vmem, smem, smem, smem],
        out_specs=(vmem, vmem, vmem, vmem),
        scratch_shapes=[
            pltpu.VMEM((size, cpg, 64, 128), BF16),
            pltpu.VMEM((80, 9), F32),
            pltpu.VMEM((size, per_dest, 128), F32),
            pltpu.VMEM((2, size, per_dest, 128), F32),
            pltpu.VMEM((5, cpg, xs, 32, 128), F32),
            pltpu.VMEM((cpg, xs, 48, 128), F32),
            pltpu.VMEM((max(cpg, size), 64, 128), F32),
            pltpu.VMEM((cpg, 9, 48, 128), F32),
            pltpu.VMEM((9, 48, 128), F32),
            pltpu.VMEM((cpg, xs, 32, 128), F32),
            pltpu.VMEM((cpg, xs, 32, 128), F32),
            pltpu.VMEM((256, 128), F32),
            pltpu.VMEM((size, 256, 128), BF16),
            pltpu.VMEM((size, 256, 128), BF16),
            pltpu.VMEM((size, 256, 128), BF16),
            pltpu.VMEM((cpg, xs, 48, 128), F32),
            pltpu.VMEM((cpg, xs, 32, 128), F32),
            pltpu.VMEM((cpg, xs // 8, 8, 128), F32),
            pltpu.VMEM((2, cpg, xs // 8, 8, 128), F32),
            pltpu.VMEM((5, cpg, xs, 32, 128), F32),
            pltpu.VMEM((size, cpg, 64, 128), BF16),
            pltpu.VMEM((size, 64, 128), F32),
            pltpu.VMEM((cpg, 40, 8, 128), F32),
            pltpu.VMEM((128, 128), F32),
            pltpu.VMEM((everyone, 8, 128), F32),
            dma((chunks, size)), dma((chunks, size)), dma(()),
            dma((2, size)), dma((2, size)),
            dma((cpg,)), dma((cpg,)),
            dma((size,)), dma((size,)),
            dma((size,)), dma((size,)),
            dma((size,)), dma((size,)),
            dma((2, cpg)), dma((2, cpg)),
            dma((chunks, size)), dma((chunks, size)),
            dma((everyone,)), dma((everyone,)),
        ],
        compiler_params=pltpu.CompilerParams(
            collective_id=0, has_side_effects=True, vmem_limit_bytes=48 * 1024 * 1024
        ),
    )(
        features.reshape(chans, 64, 128), labels.reshape(128, 128), bands,
        tile_filter, wall_filter.T, class_weight,
    )
    return grad.reshape(features.shape), tile_grad, wall_grad.T, class_grad


def solution(mesh):
    return jax.shard_map(
        shards,
        mesh=mesh,
        in_specs=(
            P(None, "col", ("group", "gx"), "gz"),
            P(None, ("group", "gx"), "gz"),
            P(),
            P(),
            P(),
            P(),
            P(),
        ),
        out_specs=(
            P(None, "col", ("group", "gx"), "gz"),
            P("group", None),
            P("group", None),
            P("group", None),
        ),
        check_vma=False,
    )
```

```python
import functools

import jax
import jax.numpy as jnp
from jax import lax
from jax.experimental import pallas as pl
from jax.experimental.pallas import tpu as pltpu
from jax.sharding import PartitionSpec as P

F32 = jnp.float32
BF16 = jnp.bfloat16
MESH = pl.DeviceIdType.MESH


def fold(value):
    total = value[0:8]
    for row in range(8, value.shape[0], 8):
        total = total + value[row : row + 8]
    return total


def rounded(value):
    return value.astype(BF16).astype(F32)


def kernel(
    dims,
    feat, labels, bands, tile_w, wall_w, class_w,
    out, tile_out, wall_out, class_out,
    recv, band_pad, halo_out, halo_in, zfeat, smooth, stage, taps, band_rows, hid, slope,
    part_own, part_out, part_in, err, gwall, gsm, ghalo_out, ghalo_in, zgrad, gout, gstage,
    acc, red, sums,
    a_send, a_recv, own_sem, h_send, h_recv, s_send, s_recv, p_send, p_recv, e_send, e_recv,
    w_send, w_recv, g_send, g_recv, o_send, o_recv, r_send, r_recv,
):
    size, depth, cpg, chunks, volume = dims
    per = cpg // chunks
    xs = 2 * size
    xgroups = xs // 8
    everyone = size * depth * 2
    gx, gz, col = lax.axis_index("gx"), lax.axis_index("gz"), lax.axis_index("col")
    me = (gx * depth + gz) * 2 + col
    other = 1 - col
    right, left = lax.rem(gz + 1, depth), lax.rem(gz + depth - 1, depth)
    chan0 = gx * cpg

    def peer(step):
        return lax.rem(gx + step, size)

    def source(step):
        return lax.rem(gx + size - step, size)

    def coords(step):
        index = lax.rem(me + step, everyone)
        return {
            "gx": index // (2 * depth),
            "gz": lax.rem(index // 2, depth),
            "col": lax.rem(index, 2),
        }

    barrier = pltpu.get_barrier_semaphore()

    @pl.loop(1, everyone)
    def _(step):
        pl.semaphore_signal(barrier, inc=1, device_id=coords(step), device_id_type=MESH)

    pl.semaphore_wait(barrier, everyone - 1)

    def remote(src, dst, send, rec, device):
        return pltpu.make_async_remote_copy(
            src_ref=src, dst_ref=dst, send_sem=send, recv_sem=rec,
            device_id=device, device_id_type=MESH,
        )

    def a_copy(chunk, step):
        return remote(
            feat.at[pl.ds(peer(step) * cpg + chunk * per, per)],
            recv.at[step, pl.ds(chunk * per, per)],
            a_send.at[chunk, step], a_recv.at[chunk, step], {"gx": peer(step)},
        )

    def h_copy(way, step):
        return remote(
            halo_out.at[peer(step)], halo_in.at[way, step],
            h_send.at[way, step], h_recv.at[way, step],
            {"gx": peer(step), "gz": right if way == 0 else left},
        )

    own_copy = pltpu.make_async_copy(feat.at[pl.ds(chan0, cpg)], recv.at[0], own_sem)
    own_copy.start()
    for step in range(1, size):
        a_copy(0, step).start()

    lane = lax.broadcasted_iota(jnp.int32, (8, 128), 1)
    quad = lane // 4

    @pl.loop(0, size)
    def _(group):
        for first in range(0, cpg, 4):
            packed = jnp.zeros((8, 128), F32)
            for c in range(first, min(first + 4, cpg)):
                stage[c] = feat[group * cpg + c].astype(F32)
                for xl in range(2):
                    rows = stage[c, pl.ds(xl, 32, stride=2), :]
                    for t in range(4):
                        m = (c - first) * 8 + xl * 4 + t
                        turned = pltpu.roll(rows[8 * t : 8 * t + 8], (2 + 4 * m) % 128, 1)
                        packed = jnp.where(quad == m, turned, packed)
            halo_out[group, pl.ds(first // 4 * 8, 8), :] = packed

    for way in range(2):
        for step in range(size):
            h_copy(way, step).start()
    for chunk in range(1, chunks):
        for step in range(1, size):
            a_copy(chunk, step).start()

    band_pad[0:8] = jnp.zeros((8, 9), F32)
    band_pad[8:72] = bands[...]
    band_pad[72:80] = jnp.zeros((8, 9), F32)
    for k in range(9):
        band_rows[k] = jnp.broadcast_to(band_pad[pl.ds(32 * col, 48), k : k + 1], (48, 128))

    @pl.loop(0, cpg)
    def _(c):
        for k in range(9):
            taps[c, k] = wall_w[k, chan0 + c] * band_rows[k]
        for x_group in range(0, xs, 8):
            blank = jnp.zeros((8, 8, 128), F32)
            smooth[c, pl.ds(x_group, 8), pl.ds(pl.multiple_of(40 * col, 8), 8), :] = blank
            gwall[c, pl.ds(x_group, 8), pl.ds(pl.multiple_of(40 * col, 8), 8), :] = blank
        for q in range(40):
            acc[c, q] = jnp.zeros((8, 128), F32)

    red[...] = jnp.zeros((128, 128), F32)

    def shifts(value, edge):
        return (
            pltpu.roll(jnp.where(lane >= 126, edge, value), 2, 1),
            pltpu.roll(jnp.where(lane == 127, edge, value), 1, 1),
            value,
            pltpu.roll(jnp.where(lane == 0, edge, value), 127, 1),
            pltpu.roll(jnp.where(lane < 2, edge, value), 126, 1),
        )

    def filtered(field, c, x, flip):
        total = None
        for i in range(5):
            at = lax.rem(x + (4 - i if flip else i) - 2 + xs, xs)
            for j in range(5):
                term = tile_w[chan0 + c, 5 * i + j] * field[4 - j if flip else j, c, at]
                total = term if total is None else total + term
        return total

    def y_copy(ref, index, send, rec):
        src = pl.multiple_of(32 - 24 * col, 8)
        dst = pl.multiple_of(40 * col, 8)
        return remote(
            ref.at[index + (pl.ds(src, 8),)], ref.at[index + (pl.ds(dst, 8),)],
            send, rec, {"col": other},
        )

    def s_copy(c):
        return y_copy(smooth, (c, pl.ds(0, xs)), s_send.at[c], s_recv.at[c])

    own_copy.wait()
    for way in range(2):
        for step in range(size):
            h_copy(way, step).wait_recv()

    def edges_of(ref_left, ref_right):
        return jnp.where(lax.rem(lane, 4) < 2, ref_left, ref_right)

    for chunk in range(chunks):
        for step in range(1, size):
            a_copy(chunk, step).wait_recv()
        for c in range(chunk * per, chunk * per + per):

            @pl.loop(0, size, unroll=2)
            def _(step, c=c):
                s = source(step)
                stage[step] = recv[step, c].astype(F32)
                at = pl.ds(c // 4 * 8, 8)
                packed = edges_of(halo_in[0, step, at, :], halo_in[1, step, at, :])
                for xl in range(2):
                    rows = stage[step, pl.ds(xl, 32, stride=2), :]
                    for t in range(4):
                        m = c % 4 * 8 + xl * 4 + t
                        edge = pltpu.roll(packed, (126 - 4 * m) % 128, 1)
                        moved = shifts(rows[8 * t : 8 * t + 8], edge)
                        for j in range(5):
                            zfeat[j, c, 2 * s + xl, pl.ds(8 * t, 8), :] = moved[j]

            @pl.loop(0, xs, unroll=4)
            def _(x, c=c):
                smooth[c, x, pl.ds(8, 32), :] = rounded(filtered(zfeat, c, x, False))

            s_copy(c).start()

    for c in range(cpg):
        s_copy(c).wait_recv()

    def p_copy(step):
        return remote(
            part_out.at[step], part_in.at[step], p_send.at[step], p_recv.at[step],
            {"gx": peer(step)},
        )

    def scores_at(x):
        def body(c, totals):
            wall = None
            for k in range(9):
                term = taps[c, k, pl.ds(8, 32), :] * smooth[c, x, pl.ds(4 + k, 32), :]
                wall = term if wall is None else wall + term
            sig = jax.nn.sigmoid(wall)
            hidden = wall * sig
            hid[c, x] = hidden
            slope[c, x] = sig * (1.0 + wall * (1.0 - sig))
            return tuple(
                total + class_w[k, chan0 + c] * hidden for k, total in enumerate(totals)
            )

        return lax.fori_loop(
            0, cpg, body, tuple(jnp.zeros((32, 128), F32) for k in range(4)), unroll=min(4, cpg)
        )

    @pl.loop(1, size)
    def _(step):
        for xl in range(2):
            totals = scores_at(2 * peer(step) + xl)
            for k in range(4):
                part_out[step, pl.ds((2 * k + xl) * 32, 32), :] = totals[k].astype(BF16)
        p_copy(step).start()

    for xl in range(2):
        totals = scores_at(2 * gx + xl)
        for k in range(4):
            part_own[pl.ds((2 * k + xl) * 32, 32), :] = totals[k]

    @pl.loop(1, size)
    def _(step):
        p_copy(step).wait_recv()
        part_own[...] = part_own[...] + part_in[step].astype(F32)

    for xl in range(2):
        marks = labels[pl.ds(64 * col + xl, 32, stride=2), :]
        for k in range(4):
            at = pl.ds((2 * k + xl) * 32, 32)
            err[0, at, :] = (part_own[at, :] - jnp.where(marks == k, 1.0, 0.0)).astype(BF16)

    def e_copy(step):
        return remote(
            err.at[0], err.at[step], e_send.at[step], e_recv.at[step], {"gx": peer(step)}
        )

    for step in range(1, size):
        e_copy(step).start()

    def w_copy(step):
        return y_copy(
            gwall, (pl.ds(0, cpg), pl.ds(2 * source(step), 2)), w_send.at[step], w_recv.at[step]
        )

    def wall_grads(step):
        for xl in range(2):
            x = 2 * source(step) + xl
            errors = [err[step, pl.ds((2 * k + xl) * 32, 32), :].astype(F32) for k in range(4)]

            @pl.loop(0, cpg, unroll=min(4, cpg))
            def _(c):
                hidden = hid[c, x]
                grad = None
                for k in range(4):
                    term = class_w[k, chan0 + c] * errors[k]
                    grad = term if grad is None else grad + term
                    acc[c, 34 + k] = acc[c, 34 + k] + fold(errors[k] * hidden)
                gwall[c, x, pl.ds(8, 32), :] = rounded(grad * slope[c, x])

        w_copy(step).start()

    wall_grads(0)

    @pl.loop(1, size)
    def _(step):
        e_copy(step).wait_recv()
        wall_grads(step)

    @pl.loop(0, size)
    def _(step):
        w_copy(step).wait_recv()

    def g_copy(way, c):
        return remote(
            ghalo_out.at[c], ghalo_in.at[way, c], g_send.at[way, c], g_recv.at[way, c],
            {"gz": right if way == 0 else left},
        )

    @pl.loop(0, cpg)
    def _(c):
        def body(x, sums9):
            grad = gwall[c, x, pl.ds(8, 32), :]
            total = None
            news = []
            for k in range(9):
                term = taps[c, k, pl.ds(12 - k, 32), :] * gwall[c, x, pl.ds(12 - k, 32), :]
                total = term if total is None else total + term
                product = grad * band_rows[k, pl.ds(8, 32), :] * smooth[c, x, pl.ds(4 + k, 32), :]
                news.append(sums9[k] + fold(product))
            gsm[c, x] = rounded(total)
            return tuple(news)

        sums9 = lax.fori_loop(0, xs, body, tuple(jnp.zeros((8, 128), F32) for k in range(9)), unroll=2)
        for k in range(9):
            acc[c, 25 + k] = sums9[k]

        @pl.loop(0, xgroups)
        def _(group):
            packed = jnp.zeros((8, 128), F32)
            for m in range(32):
                piece = gsm[c, group * 8 + m // 4, pl.ds(m % 4 * 8, 8), :]
                packed = jnp.where(quad == m, pltpu.roll(piece, (2 + 4 * m) % 128, 1), packed)
            ghalo_out[c, group] = packed

        for way in range(2):
            g_copy(way, c).start()

    def o_copy(chunk, step):
        return remote(
            gout.at[peer(step), pl.ds(chunk * per, per)],
            out.at[pl.ds(chan0 + chunk * per, per)],
            o_send.at[chunk, step], o_recv.at[chunk, step], {"gx": peer(step)},
        )

    @pl.loop(0, chunks)
    def _(chunk):
        @pl.loop(0, per)
        def _(lower):
            c = chunk * per + lower
            for way in range(2):
                g_copy(way, c).wait_recv()

            @pl.loop(0, xgroups)
            def _(group):
                packed = edges_of(ghalo_in[0, c, group], ghalo_in[1, c, group])
                for m in range(32):
                    at = pl.ds(m % 4 * 8, 8)
                    x = group * 8 + m // 4
                    edge = pltpu.roll(packed, (126 - 4 * m) % 128, 1)
                    moved = shifts(gsm[c, x, at, :], edge)
                    for j in range(5):
                        zgrad[j, c, x, at, :] = moved[j]

            @pl.loop(0, size, unroll=2)
            def _(s):
                for xl in range(2):
                    gstage[s, pl.ds(xl, 32, stride=2), :] = filtered(zgrad, c, 2 * s + xl, True)
                gout[s, c] = gstage[s].astype(BF16)

            out[chan0 + c] = gout[gx, c]

        for step in range(1, size):
            o_copy(chunk, step).start()

    row = lax.broadcasted_iota(jnp.int32, (8, 128), 0)

    @pl.loop(0, cpg)
    def _(c):
        def body(x, sums25):
            grad = gsm[c, x]
            news = []
            for i in range(5):
                at = lax.rem(x + i - 2 + xs, xs)
                for j in range(5):
                    news.append(sums25[5 * i + j] + fold(zfeat[j, c, at] * grad))
            return tuple(news)

        sums25 = lax.fori_loop(0, xs, body, tuple(jnp.zeros((8, 128), F32) for q in range(25)), unroll=2)
        for q in range(38):
            value = sums25[q] if q < 25 else acc[c, q]
            red[pl.ds(q, 1), :] = jnp.sum(value, axis=0, keepdims=True)
        line = lax.dot_general(
            jnp.ones((8, 128), F32), red[...], (((1,), (1,)), ((), ())),
            precision=lax.Precision.HIGHEST, preferred_element_type=F32,
        )
        before = jnp.where(c == 0, jnp.zeros((8, 128), F32), sums[me])
        sums[me] = jnp.where(row == c, line, before)

    def r_copy(step):
        return remote(sums.at[me], sums.at[me], r_send.at[step], r_recv.at[step], coords(step))

    @pl.loop(1, everyone)
    def _(step):
        r_copy(step).start()

    @pl.loop(1, everyone)
    def _(step):
        r_copy(step).wait_recv()

    @pl.loop(0, size)
    def _(group):
        total = sums[group * depth * 2]
        for member in range(1, depth * 2):
            total = total + sums[group * depth * 2 + member]
        red[pl.ds(group * cpg, cpg), :] = total[0:cpg] / volume

    turned = red[...].T
    chans = size * cpg
    tile_out[...] = red[0:chans, 0:25]
    wall_out[...] = turned[25:34, 0:chans]
    class_out[...] = turned[34:38, 0:chans]

    for chunk in range(chunks):
        for step in range(1, size):
            o_copy(chunk, step).wait()
            a_copy(chunk, step).wait_send()
    for way in range(2):
        for step in range(size):
            h_copy(way, step).wait_send()
        for c in range(cpg):
            g_copy(way, c).wait_send()
    for c in range(cpg):
        s_copy(c).wait_send()
    for step in range(1, size):
        p_copy(step).wait_send()
        e_copy(step).wait_send()
    for step in range(size):
        w_copy(step).wait_send()

    @pl.loop(1, everyone)
    def _(step):
        r_copy(step).wait_send()


OWN = 32
WIN = OWN + 8
BLOCK = 12
BLOCKS = (WIN - 4) // BLOCK
ROWS = BLOCK * 8
HALF = ROWS // 2
PIECES = ((0, 8), (8, 6), (14, 6))
RETURNS = ((0, 4), (4, 6), (10, 6))
WANTED = 38
HIGH = lax.Precision.HIGHEST


def cast_dot(a, b, dims=((1,), (0,))):
    return lax.dot_general(
        a.astype(BF16), b.astype(BF16), (dims, ((), ())), preferred_element_type=F32
    )


def split_dot(a, b):
    a_high, b_high = a.astype(BF16), b.astype(BF16)
    a_low, b_low = (a - a_high.astype(F32)).astype(BF16), (b - b_high.astype(F32)).astype(BF16)
    return cast_dot(a_high, b_high) + (cast_dot(a_high, b_low) + cast_dot(a_low, b_high))


def dot(a, b, dims=((1,), (0,))):
    return lax.dot_general(a, b, (dims, ((), ())), precision=HIGH, preferred_element_type=F32)


def region_kernel(
    dims,
    feat_h, lab_h, index_h, stretch_h, tile_h, wall_h, class_h,
    ghome, sums,
    feat, lab, index, stretch, tile_w, wall_w, class_w,
    turn, send, recv, lab_rows, lab_send, lab_recv, lab_wide, lab_win,
    field, odd, smooth, gwall, gsm, godd, hid, slope, part_out, part_in,
    taps, fore, wide, wide_t, band_tile, wall, wall_acc, acc, gram, params, classes, classes_t,
    gout, mine, red,
    in_sem, own_sem, f_send, f_recv, l_send, l_recv, p_send, p_recv, g_send, g_recv, r_send, r_recv,
):
    size, depth, volume = dims
    everyone = size * depth * 2
    gx, gz, col = lax.axis_index("gx"), lax.axis_index("gz"), lax.axis_index("col")
    me = (gx * depth + gz) * 2 + col
    right, left = lax.rem(gz + 1, depth), lax.rem(gz + depth - 1, depth)
    zps = OWN // 2
    lane = lax.broadcasted_iota(jnp.int32, (8, 128), 1)
    row = lax.broadcasted_iota(jnp.int32, (8, 128), 0)
    first = lane < 64
    y_lane = lax.rem(lane, 64) // 2
    x_even = lax.rem(lane, 2) == 0

    ins = [
        pltpu.make_async_copy(src, dst, in_sem.at[n])
        for n, (src, dst) in enumerate((
            (feat_h.at[pl.ds(0, 16)], feat.at[pl.ds(0, 16)]),
            (feat_h.at[pl.ds(16, 16)], feat.at[pl.ds(16, 16)]),
            (lab_h, lab), (index_h, index), (stretch_h, stretch),
            (tile_h, tile_w), (wall_h, wall_w), (class_h, class_w),
        ))
    ]
    for copy in ins:
        copy.start()

    gx_at = [lax.rem(gx + n, size) for n in range(size)]
    gz_at = [lax.rem(gz + n, depth) for n in range(depth)]
    col_at = [col, 1 - col]
    steps = [
        (sx, sz, sc)
        for sx in range(size) for sz in range(depth) for sc in range(2) if sx or sz or sc
    ]

    def coords(sx, sz, sc):
        return {"gx": gx_at[sx], "gz": gz_at[sz], "col": col_at[sc]}

    barrier = pltpu.get_barrier_semaphore()
    for step in steps:
        pl.semaphore_signal(barrier, inc=1, device_id=coords(*step), device_id_type=MESH)

    def remote(src, dst, sent, got, device):
        return pltpu.make_async_remote_copy(
            src_ref=src, dst_ref=dst, send_sem=sent, recv_sem=got,
            device_id=device, device_id_type=MESH,
        )

    def target(sx):
        return gx_at[sx] if isinstance(sx, int) else lax.rem(gx + sx, size)

    def origin(sx):
        return gx_at[-sx % size]

    def turned_features(side):
        ins[side].wait()
        for cp in range(8):
            block = feat[pl.ds(side * 16 + 2 * cp, 2)].astype(F32).reshape(128, 128)
            turn[side, pl.ds(cp, 128, stride=8), :] = block.T

        @pl.loop(0, 64, unroll=8)
        def _(zp):
            at = pl.ds(pl.multiple_of(zp * 16, 16), 16)
            send[side, zp] = turn[side, at, :].astype(BF16)

    last = len(PIECES) - 1

    def f_copy(piece, sx, ct, part, way):
        t, sc = target(sx), col_at[ct] if isinstance(ct, int) else 0
        at, count = part
        return remote(
            send.at[ct, pl.ds(lax.rem(t * zps + at - 2 + 64, 64), count)],
            recv.at[gx, col, pl.ds(at, count)],
            f_send.at[piece, sx, sc], f_recv.at[piece, sx, sc],
            {"gx": t, "gz": gz_at[way % depth], "col": ct},
        )

    def edge_part(piece):
        at, count = PIECES[piece]
        return ((at, 2), (at + 2, count - 2)) if piece == 0 else (
            (at + count - 2, 2), (at, count - 2)
        )

    def f_start(piece, sx, ct):
        t = target(sx)
        if 0 < piece < last:
            f_copy(piece, sx, ct, PIECES[piece], 0).start()
            return
        end, way = (0, 1) if piece == 0 else (size - 1, -1)
        far, near = edge_part(piece)

        @pl.when(t != end)
        def _():
            f_copy(piece, sx, ct, PIECES[piece], 0).start()

        @pl.when(t == end)
        def _():
            f_copy(piece, sx, ct, near, 0).start()
            f_copy(piece, sx, ct, far, way).start()

    def f_own(piece, part):
        at, count = part
        return pltpu.make_async_copy(
            send.at[col, pl.ds(lax.rem(gx * zps + at - 2 + 64, 64), count)],
            recv.at[gx, col, pl.ds(at, count)], own_sem.at[piece],
        )

    def own_piece(piece, whole_one, near_one, far_one):
        if 0 < piece < last:
            whole_one(f_own(piece, PIECES[piece]))
            return
        end, way = (0, 1) if piece == 0 else (size - 1, -1)
        far, near = edge_part(piece)

        @pl.when(gx != end)
        def _():
            whole_one(f_own(piece, PIECES[piece]))

        @pl.when(gx == end)
        def _():
            near_one(f_own(piece, near))
            far_one(f_copy(piece, 0, col, far, way))

    def begin(copy):
        copy.start()

    def f_send_all(piece, ct):
        for sx in (2, 1, 3):
            f_start(piece, sx, ct)

        @pl.when(col != ct)
        def _():
            f_start(piece, 0, ct)

        @pl.when(col == ct)
        def _():
            own_piece(piece, begin, begin, begin)

    others = [(sx, sc) for sx in (2, 1, 3, 0) for sc in range(2) if sx or sc]

    def f_wait(piece, sx, sc):
        slot = recv.at[origin(sx), col_at[sc], pl.ds(*PIECES[piece])]
        return remote(
            slot, slot, f_send.at[piece, sx, sc], f_recv.at[piece, sx, sc],
            {"gx": target(sx), "gz": gz, "col": col_at[sc]},
        )

    turned_features(0)
    pl.semaphore_wait(barrier, everyone - 1)
    f_send_all(0, 0)
    turned_features(1)
    f_send_all(0, 1)

    ins[2].wait()
    turn[2, 0:128, :] = lab[...].astype(F32).T
    even, uneven = turn[2, pl.ds(0, 64, stride=2), :], turn[2, pl.ds(1, 64, stride=2), :]
    here = jnp.where(col == 0, even, pltpu.roll(even, 64, 1))
    there = jnp.where(col == 0, pltpu.roll(uneven, 64, 1), uneven)
    lab_rows[...] = jnp.where(lax.broadcasted_iota(jnp.int32, (64, 128), 1) < 64, here, there)
    edge_rows = [jnp.zeros((1, 128), F32)] * 16
    for t in range(size):
        edge_rows[2 * t] = lab_rows[pl.ds((zps * t - 1) % 64, 1), :]
        edge_rows[2 * t + 1] = lab_rows[pl.ds((zps * t + zps) % 64, 1), :]
    edge_rows = jnp.concatenate(edge_rows, axis=0).astype(BF16)
    for t in range(size):
        lab_send[t, 0] = lab_rows[pl.ds(zps * t, zps), :].astype(BF16)
        lab_send[t, 1] = edge_rows

    def l_copy(sx):
        return remote(
            lab_send.at[target(sx)], lab_recv.at[gx, pl.ds(0, 2)],
            l_send.at[0, sx], l_recv.at[0, sx], {"gx": target(sx)},
        )

    def l_far(sx, way):
        return remote(
            lab_send.at[target(sx), 1], lab_recv.at[gx, 2], l_send.at[1, sx], l_recv.at[1, sx],
            {"gx": target(sx), "gz": gz_at[way % depth]},
        )

    l_own = pltpu.make_async_copy(lab_send.at[gx], lab_recv.at[gx, pl.ds(0, 2)], own_sem.at[3])
    l_own.start()

    def at_ends(sx, act):
        @pl.when(target(sx) == 0)
        def _():
            act(l_far(sx, 1))

        @pl.when(target(sx) == size - 1)
        def _():
            act(l_far(sx, -1))

    for sx in range(size):
        if sx:
            l_copy(sx).start()
        at_ends(sx, begin)
    for piece in range(1, len(PIECES)):
        for ct in range(2):
            f_send_all(piece, ct)

    for copy in ins[3:]:
        copy.wait()
    params[...] = jnp.zeros((128, 128), F32)
    params[0:9, 0:32] = wall_w[...]
    params[16:20, 0:32] = class_w[...]
    params[64:96, 0:25] = tile_w[...]
    red[...] = params[...].T

    def pairs(ref, start):
        return ref[pl.ds(start + col * 16, 8, stride=2), :], ref[pl.ds(start + col * 16 + 1, 8, stride=2), :]

    def spread(both, q):
        low, high = (jnp.broadcast_to(rows[:, q : q + 1], (8, 128)) for rows in both)
        return jnp.where(first, low, high)

    tile_pairs, wall_pairs = pairs(params, 64), pairs(red, 0)
    for q in range(25):
        taps[q] = spread(tile_pairs, q)

    levels = stretch.shape[0]
    hot = lax.broadcasted_iota(jnp.int32, (levels, 64), 0) == index[...]
    params[32:41, 0:64] = dot(stretch[...], hot.astype(F32), ((0,), (0,)))
    band_t = params[32:48, 0:64]
    y_row = lax.broadcasted_iota(jnp.int32, (64, 128), 0)
    y_col = lax.rem(lax.broadcasted_iota(jnp.int32, (64, 128), 1), 64) // 2
    square_row = lax.broadcasted_iota(jnp.int32, (128, 128), 0)
    square_lane = lax.broadcasted_iota(jnp.int32, (128, 128), 1)
    k_of_lane = lax.rem(lax.broadcasted_iota(jnp.int32, (16, 128), 1) // 2 + 4, 64)
    k_of_lane = (k_of_lane == lax.broadcasted_iota(jnp.int32, (16, 128), 0)) & (
        lax.rem(lax.broadcasted_iota(jnp.int32, (16, 128), 1), 2) == 0
    )
    placed = dot(band_t, k_of_lane.astype(F32), ((0,), (0,)))
    for yh in range(2):
        ahead = dot(band_t, (y_row == y_col + 32 * yh).astype(F32))
        for k in range(9):
            m = k - 4
            value = spread(wall_pairs, k) * ahead[k : k + 1, :]
            inside = (y_lane + m >= 0) & (y_lane + m < 32)
            fore[k, yh] = jnp.where(inside, value, 0.0)
            across = (y_lane + m >= 32) if yh == 0 else (y_lane + m < 0)
            fore[k, 2 + yh] = jnp.where(across, value, 0.0)
        rows_y = lax.broadcasted_iota(jnp.int32, (128, 64), 0) % 64 // 2 + 32 * yh
        at_y = rows_y == lax.broadcasted_iota(jnp.int32, (128, 64), 1)
        value = dot(at_y.astype(F32), placed)
        shift = lax.rem(square_lane // 2 + 4, 64) - 4 + square_row % 64 // 2
        inner = jnp.where((shift >= 0) & (shift < 32), value, 0.0)
        outer = jnp.where((shift >= 0) & (shift < 32), 0.0, value)
        band_tile[yh] = pltpu.roll(inner, 0, 1, stride=1, stride_axis=0)
        band_tile[2 + yh] = pltpu.roll(outer, 64, 1, stride=1, stride_axis=0)

    @pl.loop(0, 8, unroll=2)
    def _(cp):
        for yh in range(2):
            tile = jnp.zeros((128, 128), F32)
            for k in range(9):
                line = fore[k, yh, pl.ds(cp, 1), :]
                tile = jnp.where(square_row == square_lane + 2 * (k - 4), line, tile)
            wide[cp, 128 * yh : 128 * yh + 128, 128 * yh : 128 * yh + 128] = tile.astype(BF16)
            wide_t[cp, 128 * yh : 128 * yh + 128, 128 * yh : 128 * yh + 128] = tile.T.astype(BF16)
            tile = jnp.zeros((128, 128), F32)
            for k in range(5, 9) if yh == 0 else range(4):
                line = fore[k, 2 + yh, pl.ds(cp, 1), :]
                far = 2 * (k - 4) - 64 if yh == 0 else 2 * (k - 4) + 64
                tile = jnp.where(square_row == square_lane + far, line, tile)
            low, high = 128 - 128 * yh, 128 * yh
            wide[cp, low : low + 128, high : high + 128] = tile.astype(BF16)
            wide_t[cp, high : high + 128, low : low + 128] = tile.T.astype(BF16)

    chan = lax.broadcasted_iota(jnp.int32, (128, 128), 0)
    unit = lax.rem(lax.broadcasted_iota(jnp.int32, (128, 128), 1), 8)
    half_row = lax.broadcasted_iota(jnp.int32, (HALF, 128), 0)
    half_z = lax.broadcasted_iota(jnp.int32, (HALF, 128), 1) // 8
    half_k = lax.rem(half_row, 8) // 2
    same_z = (half_row // 8) * 2 + lax.rem(half_row, 2) == half_z
    classes[...] = jnp.zeros((128, 128), F32)
    for par in range(2):
        rows = dot(params[16:24, :], (chan == col * 16 + 2 * unit + par).astype(F32))
        value = jnp.zeros((HALF, 128), F32)
        for k in range(4):
            value = jnp.where(same_z & (half_k == k), rows[k : k + 1, :], value)
        classes[pl.ds(HALF * par, HALF), :] = value
    classes_t[...] = classes[...].T

    def arrived(block):
        for sx, sc in others:
            f_wait(block, sx, sc).wait_recv()
        own_piece(
            block, lambda copy: copy.wait(), lambda copy: copy.wait(), lambda copy: copy.wait_recv()
        )
        low, high = PIECES[block][0], sum(PIECES[block])

        @pl.loop(0, 2 * size)
        def _(t):
            for zp in range(low, high):
                pair = recv[t // 2, lax.rem(t, 2), zp].astype(F32)
                field[t, 2 * zp] = pair[0:8]
                field[t, 2 * zp + 1] = pair[8:16]

        between(seen(field), odd, 2 * low, 2 * high)

    def seen(ref):
        return lambda t, z: ref[t, z]

    def seen_rows(ref):
        return lambda t, z: ref[lax.rem(t, 2), spot(z, t // 2), :]

    def between(src, dst, low, high):
        @pl.loop(0, 2 * size)
        def _(t):
            after = lax.rem(t + 2, 2 * size)
            for z in range(low, high):
                dst[t, z] = jnp.where(
                    x_even, pltpu.roll(src(t, z), 127, 1), pltpu.roll(src(after, z), 1, 1)
                )

    def filtered(src, mid, t, low, count, flip, put):
        before, after = lax.rem(t + 2 * size - 2, 2 * size), lax.rem(t + 2, 2 * size)
        totals = [None] * count
        for z in range(count + 4):
            at = low + z - 2
            views = (src(before, at), mid[before, at], src(t, at), mid[t, at], src(after, at))
            for j in range(5):
                if 0 <= z - j < count:
                    for i in range(5):
                        q = 5 * (4 - i) + 4 - j if flip else 5 * i + j
                        term = taps[q] * views[i]
                        old = totals[z - j]
                        totals[z - j] = term if old is None else old + term
            if z >= 4:
                put(z - 4, totals)

    def spot(z, p):
        return pl.ds(pl.multiple_of((z * size + p) * 8, 8), 8)

    def unit_rows(z, count, cp):
        return pl.ds(z * size * 8 + cp, count * size, stride=8)

    def unit_of(ref, z, count, cp):
        at = unit_rows(z, count, cp)
        return jnp.concatenate([ref[0, at, :], ref[1, at, :]], axis=1).astype(BF16)

    def p_copy(block):
        return remote(
            part_out.at[block], part_in.at[block], p_send.at[block], p_recv.at[block],
            {"col": 1 - col},
        )

    def ahead_of(block):
        base = 2 + BLOCK * block

        @pl.loop(0, 2 * size)
        def _(t):
            def put(z, totals):
                smooth[lax.rem(t, 2), spot(base + z, t // 2), :] = rounded(totals[z])

            filtered(seen(field), odd, t, base, BLOCK, False, put)

        @pl.loop(0, 8, unroll=8)
        def _(cp):
            both = jnp.dot(
                unit_of(smooth, base, BLOCK, cp), wide[cp], preferred_element_type=F32
            )
            for yh in range(2):
                wall[yh, unit_rows(0, BLOCK, cp), :] = both[:, 128 * yh : 128 * yh + 128]

        @pl.loop(0, BLOCK)
        def _(z):
            at = pl.ds(pl.multiple_of(8 * z, 8), 8)
            for p in range(size):
                for yh in range(2):
                    value = wall[yh, spot(z, p), :]
                    sig = jax.nn.sigmoid(value)
                    lanes = slice(128 * yh, 128 * yh + 128)
                    hid[block, p, at, lanes] = value * sig
                    slope[block, p, at, lanes] = sig * (1.0 + value * (1.0 - sig))

        left_half = lax.rem(lax.broadcasted_iota(jnp.int32, (HALF, 256), 1), 128) < 64

        @pl.loop(0, size, unroll=size)
        def _(p):
            part = split_dot(classes[0:ROWS, 0:ROWS], hid[block, p])
            part_out[block, p] = jnp.where(left_half, part[0:HALF], part[HALF:ROWS])
            lanes = pl.ds(pl.multiple_of(128 * col, 128), 128)
            for zp in range(BLOCK // 2):
                at = slice(8 * zp, 8 * zp + 8)
                mark = lab_win[p, pl.ds(BLOCK // 2 * block + zp, 1), :]
                mark = jnp.broadcast_to(mark, (8, 128))
                mark = jnp.where(lax.rem(row, 2) == 0, mark, pltpu.roll(mark, 64, 1))
                hit = first & (mark == (row // 2).astype(F32))
                part_out[block, p, at, lanes] = part_out[block, p, at, lanes] - jnp.where(hit, 1.0, 0.0)

        p_copy(block).start()

    def back_of(block):
        base = 2 + BLOCK * block
        p_copy(block).wait_recv()
        left_half = lax.rem(lax.broadcasted_iota(jnp.int32, (HALF, 256), 1), 128) < 64

        @pl.loop(0, size, unroll=size)
        def _(p):
            err = part_out[block, p] + part_in[block, p]
            swapped = jnp.concatenate(
                [pltpu.roll(err[:, 0:128], 64, 1), pltpu.roll(err[:, 128:256], 64, 1)], axis=1
            )
            err = err + swapped
            both = jnp.concatenate(
                [jnp.where(left_half, err, 0.0), jnp.where(left_half, 0.0, err)], axis=0
            )
            grad = split_dot(classes_t[0:ROWS, 0:ROWS], both) * slope[block, p]
            for z in range(BLOCK):
                for yh in range(2):
                    gwall[yh, spot(base + z, p), :] = rounded(
                        grad[8 * z : 8 * z + 8, 128 * yh : 128 * yh + 128]
                    )
            new = cast_dot(both, hid[block, p], ((1,), (1,)))
            gram[block, p] = new

        @pl.loop(0, 8, unroll=8)
        def _(cp):
            both = jnp.dot(
                unit_of(gwall, base, BLOCK, cp), wide_t[cp], preferred_element_type=F32
            )
            for yh in range(2):
                at = unit_rows(base, BLOCK, cp)
                gsm[yh, at, :] = rounded(both[:, 128 * yh : 128 * yh + 128])

        between(seen_rows(gsm), godd, base, base + BLOCK)

    def g_spot(block):
        low = 4 if block == 0 else BLOCK * block
        return low, BLOCK * block + BLOCK - low

    def g_copy(back, step):
        at, many = RETURNS[back]
        p, yh = target(step // 2), lax.rem(col + step, 2)
        return remote(
            gout.at[2 * p + yh, pl.ds(at, many)],
            ghome.at[col, pl.ds(gx * zps + at, many)],
            g_send.at[back, step], g_recv.at[back, step], {"gx": p, "col": yh},
        )

    def g_near(back):
        at, many = RETURNS[back]
        return pltpu.make_async_copy(
            gout.at[2 * gx + col, pl.ds(at, many)],
            ghome.at[col, pl.ds(gx * zps + at, many)],
            g_recv.at[back, 0],
        )

    def g_wait(back, step):
        at, many = RETURNS[back]
        slot = ghome.at[col_at[step % 2], pl.ds(origin(step // 2) * zps + at, many)]
        return remote(
            slot, slot, g_send.at[back, step], g_recv.at[back, step],
            {"gx": target(step // 2), "col": col_at[step % 2]},
        )

    def home(block):
        low, count = g_spot(block)

        @pl.loop(0, 2 * size)
        def _(turn_at):
            step = lax.rem(turn_at + 4, 2 * size)
            t = 2 * target(step // 2) + lax.rem(col + step, 2)

            def put(z, totals):
                if z % 2:
                    pair = jnp.concatenate([totals[z - 1], totals[z]], axis=0)
                    gout[t, (low - 4 + z) // 2] = pair.astype(BF16)

            filtered(seen_rows(gsm), godd, t, low, count, True, put)

            @pl.when(step > 0)
            def _():
                g_copy(block, step).start()

            @pl.when(step == 0)
            def _():
                g_near(block).start()

    def labels_in():
        at_end = (gx == 0) | (gx == size - 1)
        for sx in range(size):
            if sx:
                at = lab_recv.at[origin(sx), pl.ds(0, 2)]
                remote(
                    at, at, l_send.at[0, sx], l_recv.at[0, sx], {"gx": target(sx)}
                ).wait_recv()

            @pl.when(at_end)
            def _(sx=sx):
                at = lab_recv.at[origin(sx), 2]
                remote(
                    at, at, l_send.at[1, sx], l_recv.at[1, sx], {"gx": target(sx), "gz": right}
                ).wait_recv()
                lab_wide[origin(sx), 2] = lab_recv[origin(sx), 2].astype(F32)

        l_own.wait()
        low_edge = 2 - (gx + size - 1) // size
        high_edge = 1 + (gx + 1) // size
        for p in range(size):
            lab_win[p, 1 : 1 + zps, :] = lab_recv[p, 0].astype(F32)
            lab_wide[p, 1] = lab_recv[p, 1].astype(F32)
            lab_win[p, 0:1, :] = lab_wide[p, low_edge, pl.ds(2 * gx, 1), :]
            lab_win[p, 1 + zps : 2 + zps, :] = lab_wide[p, high_edge, pl.ds(2 * gx + 1, 1), :]

    arrived(0)
    labels_in()
    ahead_of(0)
    back_of(0)
    home(0)
    arrived(1)
    ahead_of(1)
    arrived(2)
    ahead_of(2)
    back_of(1)
    home(1)
    back_of(2)
    home(2)

    def tile_body(it, sums25):
        t, base = it // 4, 4 + 8 * lax.rem(it, 4)
        before, after = lax.rem(t + 2 * size - 2, 2 * size), lax.rem(t + 2, 2 * size)
        grads = [seen_rows(gsm)(t, base + z) for z in range(8)]
        news = list(sums25)
        for z in range(12):
            at = base + z - 2
            views = (
                field[before, at], odd[before, at], field[t, at], odd[t, at], field[after, at]
            )
            for j in range(5):
                if 0 <= z - j < 8:
                    for i in range(5):
                        news[5 * i + j] = news[5 * i + j] + views[i] * grads[z - j]
        return tuple(news)

    sums25 = lax.fori_loop(
        0, 8 * size, tile_body, tuple(jnp.zeros((8, 128), F32) for q in range(25))
    )
    for q in range(25):
        acc[8 * q : 8 * q + 8, :] = sums25[q]

    @pl.loop(0, 8, unroll=8)
    def _(cp):
        grads, fields = unit_of(gwall, 4, OWN, cp), unit_of(smooth, 4, OWN, cp)
        both = cast_dot(grads, fields, ((0,), (0,)))
        for par in range(2):
            wall_acc[par, cp] = jnp.zeros((8, 128), F32)
        for yh in range(2):
            here, far = slice(128 * yh, 128 * yh + 128), slice(128 - 128 * yh, 256 - 128 * yh)
            for g in range(16):
                at = slice(128 * yh + 8 * g, 128 * yh + 8 * g + 8)
                tile = both[at, here] * band_tile[yh, 8 * g : 8 * g + 8, :]
                if g % 8 == (0 if yh else 7):
                    edge = both[at, far] * band_tile[2 + yh, 8 * g : 8 * g + 8, :]
                    tile = tile + pltpu.roll(edge, 64, 1)
                wall_acc[g // 8, cp] = wall_acc[g // 8, cp] + pltpu.roll(tile, (128 - 8 * g) % 128, 1)

    inner_row = lax.rem(lax.broadcasted_iota(jnp.int32, (64, 128), 0), 8)
    halves = lax.broadcasted_iota(jnp.int32, (128, 128), 0) // 64
    parity = lax.rem(lax.broadcasted_iota(jnp.int32, (128, 128), 1), 2)
    lines = dot(acc[...], (halves == parity).astype(F32))
    total = jnp.zeros((8, 128), F32)
    for q in range(25):
        total = jnp.where(lane // 2 == q, lines[8 * q : 8 * q + 8, :], total)

    full_row = lax.broadcasted_iota(jnp.int32, (ROWS, ROWS), 0)
    full_lane = lax.broadcasted_iota(jnp.int32, (ROWS, ROWS), 1)
    row_z = lax.rem(full_row, HALF) // 8 * 2 + lax.rem(full_row, 2)
    matrix = jnp.zeros((ROWS, ROWS), F32)
    for block in range(BLOCKS):
        base = 2 + BLOCK * block
        value = gram[block, 0]
        for p in range(1, size):
            value = value + gram[block, p]
        keep = (row_z == full_lane // 8) & (row_z + base >= 4) & (row_z + base < 4 + OWN)
        matrix = matrix + jnp.where(keep, value, 0.0)
    gather = (
        lax.broadcasted_iota(jnp.int32, (8, ROWS), 0)
        == lax.rem(lax.broadcasted_iota(jnp.int32, (8, ROWS), 1), 8)
    ).astype(F32)
    by_row = dot(gather, matrix, ((1,), (1,)))
    source_row = lax.broadcasted_iota(jnp.int32, (ROWS, 128), 0)
    place = 2 * (34 + lax.rem(source_row, 8) // 2) + source_row // HALF
    place = place == lax.broadcasted_iota(jnp.int32, (ROWS, 128), 1)
    total = total + dot(by_row, place.astype(F32))
    stack = (
        lax.broadcasted_iota(jnp.int32, (8, 64), 0)
        == lax.broadcasted_iota(jnp.int32, (8, 64), 1) // 8
    ).astype(F32)
    for par in range(2):
        value = wall_acc[par].reshape(64, 128)
        for r in range(1, 8):
            value = jnp.where(inner_row == r, pltpu.roll(value, 128 - r, 1), value)
        by_lane = dot(stack, value)
        source = lax.rem(square_row // 2 + 4, 64)
        place = (lax.rem(square_row, 2) == 0) & (source < 9) & (
            square_lane == 2 * (25 + source) + par
        )
        total = total + dot(by_lane, place.astype(F32))
    mine[...] = total

    def r_copy(n):
        return remote(mine, sums.at[me], r_send.at[n + 1], r_recv.at[n + 1], coords(*steps[n]))

    r_own = pltpu.make_async_copy(mine, sums.at[me], r_recv.at[0])
    r_own.start()

    for n in range(len(steps)):
        r_copy(n).start()

    for back in range(BLOCKS):
        for step in range(1, 2 * size):
            g_wait(back, step).wait_recv()
        g_near(back).wait()

    for n, (sx, sz, sc) in enumerate(steps):
        place = (origin(sx) * depth + gz_at[-sz % depth]) * 2 + col_at[sc]
        remote(
            sums.at[place], sums.at[place], r_send.at[n + 1], r_recv.at[n + 1], coords(sx, sz, sc)
        ).wait_recv()
    r_own.wait()
    for piece in range(len(PIECES)):
        for sx, sc in others:
            f_wait(piece, sx, sc).wait_send()
    pl.when(gx == 0)(lambda: f_copy(0, 0, col, edge_part(0)[0], 1).wait_send())
    pl.when(gx == size - 1)(lambda: f_copy(last, 0, col, edge_part(last)[0], -1).wait_send())
    for sx in range(size):
        if sx:
            l_copy(sx).wait_send()
        at_ends(sx, lambda copy: copy.wait_send())
    for block in range(BLOCKS):
        p_copy(block).wait_send()
    for back in range(BLOCKS):
        for step in range(1, 2 * size):
            g_copy(back, step).wait_send()

    for n in range(len(steps)):
        r_copy(n).wait_send()


def last_kernel(volume, home, sums, out, tile_out, wall_out, class_out, turn, red):
    side = pl.program_id(0)
    members = sums.shape[0] // 2

    @pl.loop(0, 64, unroll=8)
    def _(zp):
        at = pl.ds(pl.multiple_of(zp * 16, 16), 16)
        turn[at, :] = home[0, zp].astype(F32)

    for cp in range(8):
        block = turn[pl.ds(cp, 128, stride=8), :].T
        out[pl.ds(2 * cp, 2)] = block.reshape(2, 64, 128).astype(BF16)

    @pl.when(side == 0)
    def _():
        spot = lax.broadcasted_iota(jnp.int32, (128, 128), 0)
        want = 2 * lax.broadcasted_iota(jnp.int32, (128, 128), 1)
        red[...] = jnp.zeros((128, 128), F32)
        for half in range(2):
            total = sums[half]
            for member in range(1, members):
                total = total + sums[2 * member + half]
            total = total / volume
            for par in range(2):
                red[pl.ds(half * 16 + par, 8, stride=2), :] = dot(
                    total, (spot == want + par).astype(F32)
                )
        turned = red[...].T
        tile_out[...] = red[0:32, 0:25]
        wall_out[...] = turned[25:34, 0:32]
        class_out[...] = turned[34:38, 0:32]


def regional(
    size, depth, volume,
    features, labels, grid_index, stretch, tile_filter, wall_filter, class_weight,
):
    chans = features.shape[0]
    levels = stretch.shape[0]
    everyone = size * depth * 2
    dma = pltpu.SemaphoreType.DMA
    far = pl.BlockSpec(memory_space=pl.ANY)
    wide = pltpu.VMEM((2 * size, WIN, 8, 128), F32)
    rows = pltpu.VMEM((2, WIN * size * 8, 128), F32)
    block = pltpu.VMEM((BLOCKS, size, ROWS, 256), F32)
    half = pltpu.VMEM((BLOCKS, size, HALF, 256), F32)
    home, sums = pl.pallas_call(
        functools.partial(region_kernel, (size, depth, volume)),
        out_shape=(
            jax.ShapeDtypeStruct((2, 64, 16, 128), BF16),
            jax.ShapeDtypeStruct((everyone, 8, 128), F32),
        ),
        in_specs=[far] * 7,
        out_specs=(far, far),
        scratch_shapes=[
            pltpu.VMEM((chans, 64, 128), BF16),
            pltpu.VMEM((128, 128), jnp.int32),
            pltpu.VMEM((1, 64), jnp.int32),
            pltpu.VMEM((levels, 9), F32),
            pltpu.VMEM((chans, 25), F32),
            pltpu.VMEM((9, chans), F32),
            pltpu.VMEM((4, chans), F32),
            pltpu.VMEM((3, 1024, 128), F32),
            pltpu.VMEM((2, 64, 16, 128), BF16),
            pltpu.VMEM((size, 2, WIN // 2, 16, 128), BF16),
            pltpu.VMEM((64, 128), F32),
            pltpu.VMEM((size, 2, 16, 128), BF16),
            pltpu.VMEM((size, 3, 16, 128), BF16),
            pltpu.VMEM((size, 3, 16, 128), F32),
            pltpu.VMEM((size, 24, 128), F32),
            wide, wide, rows, rows, rows, wide,
            block, block, half, half,
            pltpu.VMEM((25, 8, 128), F32),
            pltpu.VMEM((9, 4, 8, 128), F32),
            pltpu.VMEM((8, 256, 256), BF16),
            pltpu.VMEM((8, 256, 256), BF16),
            pltpu.VMEM((4, 128, 128), F32),
            pltpu.VMEM((2, ROWS * size, 128), F32),
            pltpu.VMEM((2, 8, 8, 128), F32),
            pltpu.VMEM((25 * 8, 128), F32),
            pltpu.VMEM((BLOCKS, size, ROWS, ROWS), F32),
            pltpu.VMEM((128, 128), F32),
            pltpu.VMEM((128, 128), F32),
            pltpu.VMEM((128, 128), F32),
            pltpu.VMEM((2 * size, OWN // 2, 16, 128), BF16),
            pltpu.VMEM((8, 128), F32),
            pltpu.VMEM((128, 128), F32),
            dma((8,)), dma((4,)),
            dma((len(PIECES), size, 2)), dma((len(PIECES), size, 2)),
            dma((2, size)), dma((2, size)),
            dma((BLOCKS,)), dma((BLOCKS,)),
            dma((BLOCKS, 2 * size)), dma((BLOCKS, 2 * size)),
            dma((everyone,)), dma((everyone,)),
        ],
        compiler_params=pltpu.CompilerParams(
            collective_id=0, has_side_effects=True, vmem_limit_bytes=63 * 1024 * 1024
        ),
    )(
        features.reshape(chans, 64, 128), labels.reshape(128, 128), grid_index.reshape(1, 64),
        stretch, tile_filter, wall_filter.T, class_weight,
    )
    def whole(*shape):
        return pl.BlockSpec(shape, lambda side: (0,) * len(shape))

    grad, tile_grad, wall_grad, class_grad = pl.pallas_call(
        functools.partial(last_kernel, volume),
        grid=(2,),
        out_shape=(
            jax.ShapeDtypeStruct((chans, 64, 128), BF16),
            jax.ShapeDtypeStruct((chans, 25), F32),
            jax.ShapeDtypeStruct((9, chans), F32),
            jax.ShapeDtypeStruct((4, chans), F32),
        ),
        in_specs=[
            pl.BlockSpec((1, 64, 16, 128), lambda side: (side, 0, 0, 0)),
            whole(everyone, 8, 128),
        ],
        out_specs=(
            pl.BlockSpec((chans // 2, 64, 128), lambda side: (side, 0, 0)),
            whole(chans, 25), whole(9, chans), whole(4, chans),
        ),
        scratch_shapes=[pltpu.VMEM((1024, 128), F32), pltpu.VMEM((128, 128), F32)],
    )(home, sums)
    return grad.reshape(features.shape), tile_grad, wall_grad.T, class_grad


def shards(features, labels, grid_index, stretch, tile_filter, wall_filter, class_weight):
    chans, rows, cells_x, cells_z = features.shape
    size, depth = lax.axis_size("gx"), lax.axis_size("gz")
    volume = labels.shape[0] * cells_x * size * cells_z * depth
    cpg = chans // size
    if 128 // size == OWN:
        return regional(
            size, depth, volume,
            features, labels, grid_index, stretch, tile_filter, wall_filter, class_weight,
        )
    chunks = min(4, cpg)
    per_dest = max(cpg // 4, 1) * 8
    xs = 2 * size
    everyone = size * depth * 2
    onehot = (grid_index[:, None] == jnp.arange(stretch.shape[0], dtype=jnp.int32)).astype(F32)
    bands = jnp.dot(onehot, stretch, precision=lax.Precision.HIGHEST)
    dma = pltpu.SemaphoreType.DMA
    vmem = pl.BlockSpec(memory_space=pltpu.VMEM)
    smem = pl.BlockSpec(memory_space=pltpu.SMEM)
    grad, tile_grad, wall_grad, class_grad = pl.pallas_call(
        functools.partial(kernel, (size, depth, cpg, chunks, volume)),
        out_shape=(
            jax.ShapeDtypeStruct((chans, 64, 128), BF16),
            jax.ShapeDtypeStruct((chans, 25), F32),
            jax.ShapeDtypeStruct((9, chans), F32),
            jax.ShapeDtypeStruct((4, chans), F32),
        ),
        in_specs=[vmem, vmem, vmem, smem, smem, smem],
        out_specs=(vmem, vmem, vmem, vmem),
        scratch_shapes=[
            pltpu.VMEM((size, cpg, 64, 128), BF16),
            pltpu.VMEM((80, 9), F32),
            pltpu.VMEM((size, per_dest, 128), F32),
            pltpu.VMEM((2, size, per_dest, 128), F32),
            pltpu.VMEM((5, cpg, xs, 32, 128), F32),
            pltpu.VMEM((cpg, xs, 48, 128), F32),
            pltpu.VMEM((max(cpg, size), 64, 128), F32),
            pltpu.VMEM((cpg, 9, 48, 128), F32),
            pltpu.VMEM((9, 48, 128), F32),
            pltpu.VMEM((cpg, xs, 32, 128), F32),
            pltpu.VMEM((cpg, xs, 32, 128), F32),
            pltpu.VMEM((256, 128), F32),
            pltpu.VMEM((size, 256, 128), BF16),
            pltpu.VMEM((size, 256, 128), BF16),
            pltpu.VMEM((size, 256, 128), BF16),
            pltpu.VMEM((cpg, xs, 48, 128), F32),
            pltpu.VMEM((cpg, xs, 32, 128), F32),
            pltpu.VMEM((cpg, xs // 8, 8, 128), F32),
            pltpu.VMEM((2, cpg, xs // 8, 8, 128), F32),
            pltpu.VMEM((5, cpg, xs, 32, 128), F32),
            pltpu.VMEM((size, cpg, 64, 128), BF16),
            pltpu.VMEM((size, 64, 128), F32),
            pltpu.VMEM((cpg, 40, 8, 128), F32),
            pltpu.VMEM((128, 128), F32),
            pltpu.VMEM((everyone, 8, 128), F32),
            dma((chunks, size)), dma((chunks, size)), dma(()),
            dma((2, size)), dma((2, size)),
            dma((cpg,)), dma((cpg,)),
            dma((size,)), dma((size,)),
            dma((size,)), dma((size,)),
            dma((size,)), dma((size,)),
            dma((2, cpg)), dma((2, cpg)),
            dma((chunks, size)), dma((chunks, size)),
            dma((everyone,)), dma((everyone,)),
        ],
        compiler_params=pltpu.CompilerParams(
            collective_id=0, has_side_effects=True, vmem_limit_bytes=48 * 1024 * 1024
        ),
    )(
        features.reshape(chans, 64, 128), labels.reshape(128, 128), bands,
        tile_filter, wall_filter.T, class_weight,
    )
    return grad.reshape(features.shape), tile_grad, wall_grad.T, class_grad


def solution(mesh):
    return jax.shard_map(
        shards,
        mesh=mesh,
        in_specs=(
            P(None, "col", ("group", "gx"), "gz"),
            P(None, ("group", "gx"), "gz"),
            P(),
            P(),
            P(),
            P(),
            P(),
        ),
        out_specs=(
            P(None, "col", ("group", "gx"), "gz"),
            P("group", None),
            P("group", None),
            P("group", None),
        ),
        check_vma=False,
    )
```

```python
import functools

import jax
import jax.numpy as jnp
from jax import lax
from jax.experimental import pallas as pl
from jax.experimental.pallas import tpu as pltpu
from jax.sharding import PartitionSpec as P

F32 = jnp.float32
BF16 = jnp.bfloat16
MESH = pl.DeviceIdType.MESH


def fold(value):
    total = value[0:8]
    for row in range(8, value.shape[0], 8):
        total = total + value[row : row + 8]
    return total


def rounded(value):
    return value.astype(BF16).astype(F32)


def kernel(
    dims,
    feat, labels, bands, tile_w, wall_w, class_w,
    out, tile_out, wall_out, class_out,
    recv, band_pad, halo_out, halo_in, zfeat, smooth, stage, taps, band_rows, hid, slope,
    part_own, part_out, part_in, err, gwall, gsm, ghalo_out, ghalo_in, zgrad, gout, gstage,
    acc, red, sums,
    a_send, a_recv, own_sem, h_send, h_recv, s_send, s_recv, p_send, p_recv, e_send, e_recv,
    w_send, w_recv, g_send, g_recv, o_send, o_recv, r_send, r_recv,
):
    size, depth, cpg, chunks, volume = dims
    per = cpg // chunks
    xs = 2 * size
    xgroups = xs // 8
    everyone = size * depth * 2
    gx, gz, col = lax.axis_index("gx"), lax.axis_index("gz"), lax.axis_index("col")
    me = (gx * depth + gz) * 2 + col
    other = 1 - col
    right, left = lax.rem(gz + 1, depth), lax.rem(gz + depth - 1, depth)
    chan0 = gx * cpg

    def peer(step):
        return lax.rem(gx + step, size)

    def source(step):
        return lax.rem(gx + size - step, size)

    def coords(step):
        index = lax.rem(me + step, everyone)
        return {
            "gx": index // (2 * depth),
            "gz": lax.rem(index // 2, depth),
            "col": lax.rem(index, 2),
        }

    barrier = pltpu.get_barrier_semaphore()

    @pl.loop(1, everyone)
    def _(step):
        pl.semaphore_signal(barrier, inc=1, device_id=coords(step), device_id_type=MESH)

    pl.semaphore_wait(barrier, everyone - 1)

    def remote(src, dst, send, rec, device):
        return pltpu.make_async_remote_copy(
            src_ref=src, dst_ref=dst, send_sem=send, recv_sem=rec,
            device_id=device, device_id_type=MESH,
        )

    def a_copy(chunk, step):
        return remote(
            feat.at[pl.ds(peer(step) * cpg + chunk * per, per)],
            recv.at[step, pl.ds(chunk * per, per)],
            a_send.at[chunk, step], a_recv.at[chunk, step], {"gx": peer(step)},
        )

    def h_copy(way, step):
        return remote(
            halo_out.at[peer(step)], halo_in.at[way, step],
            h_send.at[way, step], h_recv.at[way, step],
            {"gx": peer(step), "gz": right if way == 0 else left},
        )

    own_copy = pltpu.make_async_copy(feat.at[pl.ds(chan0, cpg)], recv.at[0], own_sem)
    own_copy.start()
    for step in range(1, size):
        a_copy(0, step).start()

    lane = lax.broadcasted_iota(jnp.int32, (8, 128), 1)
    quad = lane // 4

    @pl.loop(0, size)
    def _(group):
        for first in range(0, cpg, 4):
            packed = jnp.zeros((8, 128), F32)
            for c in range(first, min(first + 4, cpg)):
                stage[c] = feat[group * cpg + c].astype(F32)
                for xl in range(2):
                    rows = stage[c, pl.ds(xl, 32, stride=2), :]
                    for t in range(4):
                        m = (c - first) * 8 + xl * 4 + t
                        turned = pltpu.roll(rows[8 * t : 8 * t + 8], (2 + 4 * m) % 128, 1)
                        packed = jnp.where(quad == m, turned, packed)
            halo_out[group, pl.ds(first // 4 * 8, 8), :] = packed

    for way in range(2):
        for step in range(size):
            h_copy(way, step).start()
    for chunk in range(1, chunks):
        for step in range(1, size):
            a_copy(chunk, step).start()

    band_pad[0:8] = jnp.zeros((8, 9), F32)
    band_pad[8:72] = bands[...]
    band_pad[72:80] = jnp.zeros((8, 9), F32)
    for k in range(9):
        band_rows[k] = jnp.broadcast_to(band_pad[pl.ds(32 * col, 48), k : k + 1], (48, 128))

    @pl.loop(0, cpg)
    def _(c):
        for k in range(9):
            taps[c, k] = wall_w[k, chan0 + c] * band_rows[k]
        for x_group in range(0, xs, 8):
            blank = jnp.zeros((8, 8, 128), F32)
            smooth[c, pl.ds(x_group, 8), pl.ds(pl.multiple_of(40 * col, 8), 8), :] = blank
            gwall[c, pl.ds(x_group, 8), pl.ds(pl.multiple_of(40 * col, 8), 8), :] = blank
        for q in range(40):
            acc[c, q] = jnp.zeros((8, 128), F32)

    red[...] = jnp.zeros((128, 128), F32)

    def shifts(value, edge):
        return (
            pltpu.roll(jnp.where(lane >= 126, edge, value), 2, 1),
            pltpu.roll(jnp.where(lane == 127, edge, value), 1, 1),
            value,
            pltpu.roll(jnp.where(lane == 0, edge, value), 127, 1),
            pltpu.roll(jnp.where(lane < 2, edge, value), 126, 1),
        )

    def filtered(field, c, x, flip):
        total = None
        for i in range(5):
            at = lax.rem(x + (4 - i if flip else i) - 2 + xs, xs)
            for j in range(5):
                term = tile_w[chan0 + c, 5 * i + j] * field[4 - j if flip else j, c, at]
                total = term if total is None else total + term
        return total

    def y_copy(ref, index, send, rec):
        src = pl.multiple_of(32 - 24 * col, 8)
        dst = pl.multiple_of(40 * col, 8)
        return remote(
            ref.at[index + (pl.ds(src, 8),)], ref.at[index + (pl.ds(dst, 8),)],
            send, rec, {"col": other},
        )

    def s_copy(c):
        return y_copy(smooth, (c, pl.ds(0, xs)), s_send.at[c], s_recv.at[c])

    own_copy.wait()
    for way in range(2):
        for step in range(size):
            h_copy(way, step).wait_recv()

    def edges_of(ref_left, ref_right):
        return jnp.where(lax.rem(lane, 4) < 2, ref_left, ref_right)

    for chunk in range(chunks):
        for step in range(1, size):
            a_copy(chunk, step).wait_recv()
        for c in range(chunk * per, chunk * per + per):

            @pl.loop(0, size, unroll=2)
            def _(step, c=c):
                s = source(step)
                stage[step] = recv[step, c].astype(F32)
                at = pl.ds(c // 4 * 8, 8)
                packed = edges_of(halo_in[0, step, at, :], halo_in[1, step, at, :])
                for xl in range(2):
                    rows = stage[step, pl.ds(xl, 32, stride=2), :]
                    for t in range(4):
                        m = c % 4 * 8 + xl * 4 + t
                        edge = pltpu.roll(packed, (126 - 4 * m) % 128, 1)
                        moved = shifts(rows[8 * t : 8 * t + 8], edge)
                        for j in range(5):
                            zfeat[j, c, 2 * s + xl, pl.ds(8 * t, 8), :] = moved[j]

            @pl.loop(0, xs, unroll=4)
            def _(x, c=c):
                smooth[c, x, pl.ds(8, 32), :] = rounded(filtered(zfeat, c, x, False))

            s_copy(c).start()

    for c in range(cpg):
        s_copy(c).wait_recv()

    def p_copy(step):
        return remote(
            part_out.at[step], part_in.at[step], p_send.at[step], p_recv.at[step],
            {"gx": peer(step)},
        )

    def scores_at(x):
        def body(c, totals):
            wall = None
            for k in range(9):
                term = taps[c, k, pl.ds(8, 32), :] * smooth[c, x, pl.ds(4 + k, 32), :]
                wall = term if wall is None else wall + term
            sig = jax.nn.sigmoid(wall)
            hidden = wall * sig
            hid[c, x] = hidden
            slope[c, x] = sig * (1.0 + wall * (1.0 - sig))
            return tuple(
                total + class_w[k, chan0 + c] * hidden for k, total in enumerate(totals)
            )

        return lax.fori_loop(
            0, cpg, body, tuple(jnp.zeros((32, 128), F32) for k in range(4)), unroll=min(4, cpg)
        )

    @pl.loop(1, size)
    def _(step):
        for xl in range(2):
            totals = scores_at(2 * peer(step) + xl)
            for k in range(4):
                part_out[step, pl.ds((2 * k + xl) * 32, 32), :] = totals[k].astype(BF16)
        p_copy(step).start()

    for xl in range(2):
        totals = scores_at(2 * gx + xl)
        for k in range(4):
            part_own[pl.ds((2 * k + xl) * 32, 32), :] = totals[k]

    @pl.loop(1, size)
    def _(step):
        p_copy(step).wait_recv()
        part_own[...] = part_own[...] + part_in[step].astype(F32)

    for xl in range(2):
        marks = labels[pl.ds(64 * col + xl, 32, stride=2), :]
        for k in range(4):
            at = pl.ds((2 * k + xl) * 32, 32)
            err[0, at, :] = (part_own[at, :] - jnp.where(marks == k, 1.0, 0.0)).astype(BF16)

    def e_copy(step):
        return remote(
            err.at[0], err.at[step], e_send.at[step], e_recv.at[step], {"gx": peer(step)}
        )

    for step in range(1, size):
        e_copy(step).start()

    def w_copy(step):
        return y_copy(
            gwall, (pl.ds(0, cpg), pl.ds(2 * source(step), 2)), w_send.at[step], w_recv.at[step]
        )

    def wall_grads(step):
        for xl in range(2):
            x = 2 * source(step) + xl
            errors = [err[step, pl.ds((2 * k + xl) * 32, 32), :].astype(F32) for k in range(4)]

            @pl.loop(0, cpg, unroll=min(4, cpg))
            def _(c):
                hidden = hid[c, x]
                grad = None
                for k in range(4):
                    term = class_w[k, chan0 + c] * errors[k]
                    grad = term if grad is None else grad + term
                    acc[c, 34 + k] = acc[c, 34 + k] + fold(errors[k] * hidden)
                gwall[c, x, pl.ds(8, 32), :] = rounded(grad * slope[c, x])

        w_copy(step).start()

    wall_grads(0)

    @pl.loop(1, size)
    def _(step):
        e_copy(step).wait_recv()
        wall_grads(step)

    @pl.loop(0, size)
    def _(step):
        w_copy(step).wait_recv()

    def g_copy(way, c):
        return remote(
            ghalo_out.at[c], ghalo_in.at[way, c], g_send.at[way, c], g_recv.at[way, c],
            {"gz": right if way == 0 else left},
        )

    @pl.loop(0, cpg)
    def _(c):
        def body(x, sums9):
            grad = gwall[c, x, pl.ds(8, 32), :]
            total = None
            news = []
            for k in range(9):
                term = taps[c, k, pl.ds(12 - k, 32), :] * gwall[c, x, pl.ds(12 - k, 32), :]
                total = term if total is None else total + term
                product = grad * band_rows[k, pl.ds(8, 32), :] * smooth[c, x, pl.ds(4 + k, 32), :]
                news.append(sums9[k] + fold(product))
            gsm[c, x] = rounded(total)
            return tuple(news)

        sums9 = lax.fori_loop(0, xs, body, tuple(jnp.zeros((8, 128), F32) for k in range(9)), unroll=2)
        for k in range(9):
            acc[c, 25 + k] = sums9[k]

        @pl.loop(0, xgroups)
        def _(group):
            packed = jnp.zeros((8, 128), F32)
            for m in range(32):
                piece = gsm[c, group * 8 + m // 4, pl.ds(m % 4 * 8, 8), :]
                packed = jnp.where(quad == m, pltpu.roll(piece, (2 + 4 * m) % 128, 1), packed)
            ghalo_out[c, group] = packed

        for way in range(2):
            g_copy(way, c).start()

    def o_copy(chunk, step):
        return remote(
            gout.at[peer(step), pl.ds(chunk * per, per)],
            out.at[pl.ds(chan0 + chunk * per, per)],
            o_send.at[chunk, step], o_recv.at[chunk, step], {"gx": peer(step)},
        )

    @pl.loop(0, chunks)
    def _(chunk):
        @pl.loop(0, per)
        def _(lower):
            c = chunk * per + lower
            for way in range(2):
                g_copy(way, c).wait_recv()

            @pl.loop(0, xgroups)
            def _(group):
                packed = edges_of(ghalo_in[0, c, group], ghalo_in[1, c, group])
                for m in range(32):
                    at = pl.ds(m % 4 * 8, 8)
                    x = group * 8 + m // 4
                    edge = pltpu.roll(packed, (126 - 4 * m) % 128, 1)
                    moved = shifts(gsm[c, x, at, :], edge)
                    for j in range(5):
                        zgrad[j, c, x, at, :] = moved[j]

            @pl.loop(0, size, unroll=2)
            def _(s):
                for xl in range(2):
                    gstage[s, pl.ds(xl, 32, stride=2), :] = filtered(zgrad, c, 2 * s + xl, True)
                gout[s, c] = gstage[s].astype(BF16)

            out[chan0 + c] = gout[gx, c]

        for step in range(1, size):
            o_copy(chunk, step).start()

    row = lax.broadcasted_iota(jnp.int32, (8, 128), 0)

    @pl.loop(0, cpg)
    def _(c):
        def body(x, sums25):
            grad = gsm[c, x]
            news = []
            for i in range(5):
                at = lax.rem(x + i - 2 + xs, xs)
                for j in range(5):
                    news.append(sums25[5 * i + j] + fold(zfeat[j, c, at] * grad))
            return tuple(news)

        sums25 = lax.fori_loop(0, xs, body, tuple(jnp.zeros((8, 128), F32) for q in range(25)), unroll=2)
        for q in range(38):
            value = sums25[q] if q < 25 else acc[c, q]
            red[pl.ds(q, 1), :] = jnp.sum(value, axis=0, keepdims=True)
        line = lax.dot_general(
            jnp.ones((8, 128), F32), red[...], (((1,), (1,)), ((), ())),
            precision=lax.Precision.HIGHEST, preferred_element_type=F32,
        )
        before = jnp.where(c == 0, jnp.zeros((8, 128), F32), sums[me])
        sums[me] = jnp.where(row == c, line, before)

    def r_copy(step):
        return remote(sums.at[me], sums.at[me], r_send.at[step], r_recv.at[step], coords(step))

    @pl.loop(1, everyone)
    def _(step):
        r_copy(step).start()

    @pl.loop(1, everyone)
    def _(step):
        r_copy(step).wait_recv()

    @pl.loop(0, size)
    def _(group):
        total = sums[group * depth * 2]
        for member in range(1, depth * 2):
            total = total + sums[group * depth * 2 + member]
        red[pl.ds(group * cpg, cpg), :] = total[0:cpg] / volume

    turned = red[...].T
    chans = size * cpg
    tile_out[...] = red[0:chans, 0:25]
    wall_out[...] = turned[25:34, 0:chans]
    class_out[...] = turned[34:38, 0:chans]

    for chunk in range(chunks):
        for step in range(1, size):
            o_copy(chunk, step).wait()
            a_copy(chunk, step).wait_send()
    for way in range(2):
        for step in range(size):
            h_copy(way, step).wait_send()
        for c in range(cpg):
            g_copy(way, c).wait_send()
    for c in range(cpg):
        s_copy(c).wait_send()
    for step in range(1, size):
        p_copy(step).wait_send()
        e_copy(step).wait_send()
    for step in range(size):
        w_copy(step).wait_send()

    @pl.loop(1, everyone)
    def _(step):
        r_copy(step).wait_send()


OWN = 32
WIN = OWN + 8
BLOCK = 12
BLOCKS = (WIN - 4) // BLOCK
ROWS = BLOCK * 8
HALF = ROWS // 2
PIECES = ((0, 8), (8, 6), (14, 6))
RETURNS = ((0, 4), (4, 6), (10, 6))
WANTED = 38
HIGH = lax.Precision.HIGHEST


def cast_dot(a, b, dims=((1,), (0,))):
    return lax.dot_general(
        a.astype(BF16), b.astype(BF16), (dims, ((), ())), preferred_element_type=F32
    )


def split_dot(a, b):
    a_high, b_high = a.astype(BF16), b.astype(BF16)
    a_low, b_low = (a - a_high.astype(F32)).astype(BF16), (b - b_high.astype(F32)).astype(BF16)
    return cast_dot(a_high, b_high) + (cast_dot(a_high, b_low) + cast_dot(a_low, b_high))


def dot(a, b, dims=((1,), (0,))):
    return lax.dot_general(a, b, (dims, ((), ())), precision=HIGH, preferred_element_type=F32)


def region_kernel(
    dims,
    feat_h, lab_h, index_h, stretch_h, tile_h, wall_h, class_h,
    ghome, sums,
    feat, lab, index, stretch, tile_w, wall_w, class_w,
    turn, send, recv, lab_rows, lab_send, lab_recv, lab_wide, lab_win,
    field, odd, smooth, gwall, gsm, godd, hid, slope, part_out, part_in,
    taps, fore, wide, wide_t, band_tile, wall, wall_acc, acc, gram, params, classes, classes_t,
    gout, mine, red,
    in_sem, own_sem, f_send, f_recv, l_send, l_recv, p_send, p_recv, g_send, g_recv, r_send, r_recv,
):
    size, depth, volume = dims
    everyone = size * depth * 2
    gx, gz, col = lax.axis_index("gx"), lax.axis_index("gz"), lax.axis_index("col")
    me = (gx * depth + gz) * 2 + col
    right, left = lax.rem(gz + 1, depth), lax.rem(gz + depth - 1, depth)
    zps = OWN // 2
    lane = lax.broadcasted_iota(jnp.int32, (8, 128), 1)
    row = lax.broadcasted_iota(jnp.int32, (8, 128), 0)
    first = lane < 64
    y_lane = lax.rem(lane, 64) // 2
    x_even = lax.rem(lane, 2) == 0

    ins = [
        pltpu.make_async_copy(src, dst, in_sem.at[n])
        for n, (src, dst) in enumerate((
            (feat_h.at[pl.ds(0, 16)], feat.at[pl.ds(0, 16)]),
            (feat_h.at[pl.ds(16, 16)], feat.at[pl.ds(16, 16)]),
            (lab_h, lab), (index_h, index), (stretch_h, stretch),
            (tile_h, tile_w), (wall_h, wall_w), (class_h, class_w),
        ))
    ]
    for copy in ins:
        copy.start()

    gx_at = [lax.rem(gx + n, size) for n in range(size)]
    gz_at = [lax.rem(gz + n, depth) for n in range(depth)]
    col_at = [col, 1 - col]
    steps = [
        (sx, sz, sc)
        for sx in range(size) for sz in range(depth) for sc in range(2) if sx or sz or sc
    ]

    def coords(sx, sz, sc):
        return {"gx": gx_at[sx], "gz": gz_at[sz], "col": col_at[sc]}

    barrier = pltpu.get_barrier_semaphore()
    for step in steps:
        pl.semaphore_signal(barrier, inc=1, device_id=coords(*step), device_id_type=MESH)

    def remote(src, dst, sent, got, device):
        return pltpu.make_async_remote_copy(
            src_ref=src, dst_ref=dst, send_sem=sent, recv_sem=got,
            device_id=device, device_id_type=MESH,
        )

    def target(sx):
        return gx_at[sx] if isinstance(sx, int) else lax.rem(gx + sx, size)

    def origin(sx):
        return gx_at[-sx % size]

    def turned_features(side):
        ins[side].wait()
        for cp in range(8):
            block = feat[pl.ds(side * 16 + 2 * cp, 2)].astype(F32).reshape(128, 128)
            turn[side, pl.ds(cp, 128, stride=8), :] = block.T

        @pl.loop(0, 64, unroll=8)
        def _(zp):
            at = pl.ds(pl.multiple_of(zp * 16, 16), 16)
            send[side, zp] = turn[side, at, :].astype(BF16)

    last = len(PIECES) - 1

    def f_copy(piece, sx, ct, part, way):
        t, sc = target(sx), col_at[ct] if isinstance(ct, int) else 0
        at, count = part
        return remote(
            send.at[ct, pl.ds(lax.rem(t * zps + at - 2 + 64, 64), count)],
            recv.at[gx, col, pl.ds(at, count)],
            f_send.at[piece, sx, sc], f_recv.at[piece, sx, sc],
            {"gx": t, "gz": gz_at[way % depth], "col": ct},
        )

    def edge_part(piece):
        at, count = PIECES[piece]
        return ((at, 2), (at + 2, count - 2)) if piece == 0 else (
            (at + count - 2, 2), (at, count - 2)
        )

    def f_start(piece, sx, ct):
        t = target(sx)
        if 0 < piece < last:
            f_copy(piece, sx, ct, PIECES[piece], 0).start()
            return
        end, way = (0, 1) if piece == 0 else (size - 1, -1)
        far, near = edge_part(piece)

        @pl.when(t != end)
        def _():
            f_copy(piece, sx, ct, PIECES[piece], 0).start()

        @pl.when(t == end)
        def _():
            f_copy(piece, sx, ct, near, 0).start()
            f_copy(piece, sx, ct, far, way).start()

    def f_own(piece, part):
        at, count = part
        return pltpu.make_async_copy(
            send.at[col, pl.ds(lax.rem(gx * zps + at - 2 + 64, 64), count)],
            recv.at[gx, col, pl.ds(at, count)], own_sem.at[piece],
        )

    def own_piece(piece, whole_one, near_one, far_one):
        if 0 < piece < last:
            whole_one(f_own(piece, PIECES[piece]))
            return
        end, way = (0, 1) if piece == 0 else (size - 1, -1)
        far, near = edge_part(piece)

        @pl.when(gx != end)
        def _():
            whole_one(f_own(piece, PIECES[piece]))

        @pl.when(gx == end)
        def _():
            near_one(f_own(piece, near))
            far_one(f_copy(piece, 0, col, far, way))

    def begin(copy):
        copy.start()

    def f_send_all(piece, ct):
        for sx in (2, 1, 3):
            f_start(piece, sx, ct)

        @pl.when(col != ct)
        def _():
            f_start(piece, 0, ct)

        @pl.when(col == ct)
        def _():
            own_piece(piece, begin, begin, begin)

    others = [(sx, sc) for sx in (2, 1, 3, 0) for sc in range(2) if sx or sc]

    def f_wait(piece, sx, sc):
        slot = recv.at[origin(sx), col_at[sc], pl.ds(*PIECES[piece])]
        return remote(
            slot, slot, f_send.at[piece, sx, sc], f_recv.at[piece, sx, sc],
            {"gx": target(sx), "gz": gz, "col": col_at[sc]},
        )

    turned_features(0)
    pl.semaphore_wait(barrier, everyone - 1)
    f_send_all(0, 0)
    turned_features(1)
    f_send_all(0, 1)

    ins[2].wait()
    turn[2, 0:128, :] = lab[...].astype(F32).T
    even, uneven = turn[2, pl.ds(0, 64, stride=2), :], turn[2, pl.ds(1, 64, stride=2), :]
    here = jnp.where(col == 0, even, pltpu.roll(even, 64, 1))
    there = jnp.where(col == 0, pltpu.roll(uneven, 64, 1), uneven)
    lab_rows[...] = jnp.where(lax.broadcasted_iota(jnp.int32, (64, 128), 1) < 64, here, there)
    edge_rows = [jnp.zeros((1, 128), F32)] * 16
    for t in range(size):
        edge_rows[2 * t] = lab_rows[pl.ds((zps * t - 1) % 64, 1), :]
        edge_rows[2 * t + 1] = lab_rows[pl.ds((zps * t + zps) % 64, 1), :]
    edge_rows = jnp.concatenate(edge_rows, axis=0).astype(BF16)
    for t in range(size):
        lab_send[t, 0] = lab_rows[pl.ds(zps * t, zps), :].astype(BF16)
        lab_send[t, 1] = edge_rows

    def l_copy(sx):
        return remote(
            lab_send.at[target(sx)], lab_recv.at[gx, pl.ds(0, 2)],
            l_send.at[0, sx], l_recv.at[0, sx], {"gx": target(sx)},
        )

    def l_far(sx, way):
        return remote(
            lab_send.at[target(sx), 1], lab_recv.at[gx, 2], l_send.at[1, sx], l_recv.at[1, sx],
            {"gx": target(sx), "gz": gz_at[way % depth]},
        )

    l_own = pltpu.make_async_copy(lab_send.at[gx], lab_recv.at[gx, pl.ds(0, 2)], own_sem.at[3])
    l_own.start()

    def at_ends(sx, act):
        @pl.when(target(sx) == 0)
        def _():
            act(l_far(sx, 1))

        @pl.when(target(sx) == size - 1)
        def _():
            act(l_far(sx, -1))

    for sx in range(size):
        if sx:
            l_copy(sx).start()
        at_ends(sx, begin)

    for copy in ins[3:]:
        copy.wait()
    params[...] = jnp.zeros((128, 128), F32)
    params[0:9, 0:32] = wall_w[...]
    params[16:20, 0:32] = class_w[...]
    params[64:96, 0:25] = tile_w[...]
    red[...] = params[...].T

    def pairs(ref, start):
        return ref[pl.ds(start + col * 16, 8, stride=2), :], ref[pl.ds(start + col * 16 + 1, 8, stride=2), :]

    def spread(both, q):
        low, high = (jnp.broadcast_to(rows[:, q : q + 1], (8, 128)) for rows in both)
        return jnp.where(first, low, high)

    tile_pairs, wall_pairs = pairs(params, 64), pairs(red, 0)
    for q in range(25):
        taps[q] = spread(tile_pairs, q)

    levels = stretch.shape[0]
    hot = lax.broadcasted_iota(jnp.int32, (levels, 64), 0) == index[...]
    params[32:41, 0:64] = dot(stretch[...], hot.astype(F32), ((0,), (0,)))
    band_t = params[32:48, 0:64]
    y_row = lax.broadcasted_iota(jnp.int32, (64, 128), 0)
    y_col = lax.rem(lax.broadcasted_iota(jnp.int32, (64, 128), 1), 64) // 2
    square_row = lax.broadcasted_iota(jnp.int32, (128, 128), 0)
    square_lane = lax.broadcasted_iota(jnp.int32, (128, 128), 1)
    k_of_lane = lax.rem(lax.broadcasted_iota(jnp.int32, (16, 128), 1) // 2 + 4, 64)
    k_of_lane = (k_of_lane == lax.broadcasted_iota(jnp.int32, (16, 128), 0)) & (
        lax.rem(lax.broadcasted_iota(jnp.int32, (16, 128), 1), 2) == 0
    )
    placed = dot(band_t, k_of_lane.astype(F32), ((0,), (0,)))
    for yh in range(2):
        ahead = dot(band_t, (y_row == y_col + 32 * yh).astype(F32))
        for k in range(9):
            m = k - 4
            value = spread(wall_pairs, k) * ahead[k : k + 1, :]
            inside = (y_lane + m >= 0) & (y_lane + m < 32)
            fore[k, yh] = jnp.where(inside, value, 0.0)
            across = (y_lane + m >= 32) if yh == 0 else (y_lane + m < 0)
            fore[k, 2 + yh] = jnp.where(across, value, 0.0)
        rows_y = lax.broadcasted_iota(jnp.int32, (128, 64), 0) % 64 // 2 + 32 * yh
        at_y = rows_y == lax.broadcasted_iota(jnp.int32, (128, 64), 1)
        value = dot(at_y.astype(F32), placed)
        shift = lax.rem(square_lane // 2 + 4, 64) - 4 + square_row % 64 // 2
        inner = jnp.where((shift >= 0) & (shift < 32), value, 0.0)
        outer = jnp.where((shift >= 0) & (shift < 32), 0.0, value)
        band_tile[yh] = pltpu.roll(inner, 0, 1, stride=1, stride_axis=0)
        band_tile[2 + yh] = pltpu.roll(outer, 64, 1, stride=1, stride_axis=0)

    @pl.loop(0, 8, unroll=2)
    def _(cp):
        for yh in range(2):
            tile = jnp.zeros((128, 128), F32)
            for k in range(9):
                line = fore[k, yh, pl.ds(cp, 1), :]
                tile = jnp.where(square_row == square_lane + 2 * (k - 4), line, tile)
            wide[cp, 128 * yh : 128 * yh + 128, 128 * yh : 128 * yh + 128] = tile.astype(BF16)
            wide_t[cp, 128 * yh : 128 * yh + 128, 128 * yh : 128 * yh + 128] = tile.T.astype(BF16)
            tile = jnp.zeros((128, 128), F32)
            for k in range(5, 9) if yh == 0 else range(4):
                line = fore[k, 2 + yh, pl.ds(cp, 1), :]
                far = 2 * (k - 4) - 64 if yh == 0 else 2 * (k - 4) + 64
                tile = jnp.where(square_row == square_lane + far, line, tile)
            low, high = 128 - 128 * yh, 128 * yh
            wide[cp, low : low + 128, high : high + 128] = tile.astype(BF16)
            wide_t[cp, high : high + 128, low : low + 128] = tile.T.astype(BF16)

    chan = lax.broadcasted_iota(jnp.int32, (128, 128), 0)
    unit = lax.rem(lax.broadcasted_iota(jnp.int32, (128, 128), 1), 8)
    half_row = lax.broadcasted_iota(jnp.int32, (HALF, 128), 0)
    half_z = lax.broadcasted_iota(jnp.int32, (HALF, 128), 1) // 8
    half_k = lax.rem(half_row, 8) // 2
    same_z = (half_row // 8) * 2 + lax.rem(half_row, 2) == half_z
    classes[...] = jnp.zeros((128, 128), F32)
    for par in range(2):
        rows = dot(params[16:24, :], (chan == col * 16 + 2 * unit + par).astype(F32))
        value = jnp.zeros((HALF, 128), F32)
        for k in range(4):
            value = jnp.where(same_z & (half_k == k), rows[k : k + 1, :], value)
        classes[pl.ds(HALF * par, HALF), :] = value
    classes_t[...] = classes[...].T

    def arrived(block):
        for sx, sc in others:
            f_wait(block, sx, sc).wait_recv()
        own_piece(
            block, lambda copy: copy.wait(), lambda copy: copy.wait(), lambda copy: copy.wait_recv()
        )
        low, high = PIECES[block][0], sum(PIECES[block])

        @pl.loop(0, 2 * size)
        def _(t):
            for zp in range(low, high):
                pair = recv[t // 2, lax.rem(t, 2), zp].astype(F32)
                field[t, 2 * zp] = pair[0:8]
                field[t, 2 * zp + 1] = pair[8:16]

        between(seen(field), odd, 2 * low, 2 * high)

    def seen(ref):
        return lambda t, z: ref[t, z]

    def seen_rows(ref):
        return lambda t, z: ref[lax.rem(t, 2), spot(z, t // 2), :]

    def between(src, dst, low, high):
        @pl.loop(0, 2 * size)
        def _(t):
            after = lax.rem(t + 2, 2 * size)
            for z in range(low, high):
                dst[t, z] = jnp.where(
                    x_even, pltpu.roll(src(t, z), 127, 1), pltpu.roll(src(after, z), 1, 1)
                )

    def filtered(src, mid, t, low, count, flip, put):
        before, after = lax.rem(t + 2 * size - 2, 2 * size), lax.rem(t + 2, 2 * size)
        totals = [None] * count
        for z in range(count + 4):
            at = low + z - 2
            views = (src(before, at), mid[before, at], src(t, at), mid[t, at], src(after, at))
            for j in range(5):
                if 0 <= z - j < count:
                    for i in range(5):
                        q = 5 * (4 - i) + 4 - j if flip else 5 * i + j
                        term = taps[q] * views[i]
                        old = totals[z - j]
                        totals[z - j] = term if old is None else old + term
            if z >= 4:
                put(z - 4, totals)

    def spot(z, p):
        return pl.ds(pl.multiple_of((z * size + p) * 8, 8), 8)

    def unit_rows(z, count, cp):
        return pl.ds(z * size * 8 + cp, count * size, stride=8)

    def unit_of(ref, z, count, cp):
        at = unit_rows(z, count, cp)
        return jnp.concatenate([ref[0, at, :], ref[1, at, :]], axis=1).astype(BF16)

    def p_copy(block):
        return remote(
            part_out.at[block], part_in.at[block], p_send.at[block], p_recv.at[block],
            {"col": 1 - col},
        )

    def ahead_of(block):
        base = 2 + BLOCK * block

        @pl.loop(0, 2 * size)
        def _(t):
            def put(z, totals):
                smooth[lax.rem(t, 2), spot(base + z, t // 2), :] = rounded(totals[z])

            filtered(seen(field), odd, t, base, BLOCK, False, put)

        @pl.loop(0, 8, unroll=8)
        def _(cp):
            both = jnp.dot(
                unit_of(smooth, base, BLOCK, cp), wide[cp], preferred_element_type=F32
            )
            for yh in range(2):
                wall[yh, unit_rows(0, BLOCK, cp), :] = both[:, 128 * yh : 128 * yh + 128]

        @pl.loop(0, BLOCK)
        def _(z):
            at = pl.ds(pl.multiple_of(8 * z, 8), 8)
            for p in range(size):
                for yh in range(2):
                    value = wall[yh, spot(z, p), :]
                    sig = jax.nn.sigmoid(value)
                    lanes = slice(128 * yh, 128 * yh + 128)
                    hid[block, p, at, lanes] = value * sig
                    slope[block, p, at, lanes] = sig * (1.0 + value * (1.0 - sig))

        left_half = lax.rem(lax.broadcasted_iota(jnp.int32, (HALF, 256), 1), 128) < 64

        @pl.loop(0, size, unroll=size)
        def _(p):
            part = split_dot(classes[0:ROWS, 0:ROWS], hid[block, p])
            part_out[block, p] = jnp.where(left_half, part[0:HALF], part[HALF:ROWS])
            lanes = pl.ds(pl.multiple_of(128 * col, 128), 128)
            for zp in range(BLOCK // 2):
                at = slice(8 * zp, 8 * zp + 8)
                mark = lab_win[p, pl.ds(BLOCK // 2 * block + zp, 1), :]
                mark = jnp.broadcast_to(mark, (8, 128))
                mark = jnp.where(lax.rem(row, 2) == 0, mark, pltpu.roll(mark, 64, 1))
                hit = first & (mark == (row // 2).astype(F32))
                part_out[block, p, at, lanes] = part_out[block, p, at, lanes] - jnp.where(hit, 1.0, 0.0)

        p_copy(block).start()

    def back_of(block):
        base = 2 + BLOCK * block
        p_copy(block).wait_recv()
        left_half = lax.rem(lax.broadcasted_iota(jnp.int32, (HALF, 256), 1), 128) < 64

        @pl.loop(0, size, unroll=size)
        def _(p):
            err = part_out[block, p] + part_in[block, p]
            swapped = jnp.concatenate(
                [pltpu.roll(err[:, 0:128], 64, 1), pltpu.roll(err[:, 128:256], 64, 1)], axis=1
            )
            err = err + swapped
            both = jnp.concatenate(
                [jnp.where(left_half, err, 0.0), jnp.where(left_half, 0.0, err)], axis=0
            )
            grad = split_dot(classes_t[0:ROWS, 0:ROWS], both) * slope[block, p]
            for z in range(BLOCK):
                for yh in range(2):
                    gwall[yh, spot(base + z, p), :] = rounded(
                        grad[8 * z : 8 * z + 8, 128 * yh : 128 * yh + 128]
                    )
            new = cast_dot(both, hid[block, p], ((1,), (1,)))
            gram[block, p] = new

        @pl.loop(0, 8, unroll=8)
        def _(cp):
            both = jnp.dot(
                unit_of(gwall, base, BLOCK, cp), wide_t[cp], preferred_element_type=F32
            )
            for yh in range(2):
                at = unit_rows(base, BLOCK, cp)
                gsm[yh, at, :] = rounded(both[:, 128 * yh : 128 * yh + 128])

        between(seen_rows(gsm), godd, base, base + BLOCK)

    def g_spot(block):
        low = 4 if block == 0 else BLOCK * block
        return low, BLOCK * block + BLOCK - low

    def g_copy(back, step):
        at, many = RETURNS[back]
        p, yh = target(step // 2), lax.rem(col + step, 2)
        return remote(
            gout.at[2 * p + yh, pl.ds(at, many)],
            ghome.at[col, pl.ds(gx * zps + at, many)],
            g_send.at[back, step], g_recv.at[back, step], {"gx": p, "col": yh},
        )

    def g_near(back):
        at, many = RETURNS[back]
        return pltpu.make_async_copy(
            gout.at[2 * gx + col, pl.ds(at, many)],
            ghome.at[col, pl.ds(gx * zps + at, many)],
            g_recv.at[back, 0],
        )

    def g_wait(back, step):
        at, many = RETURNS[back]
        slot = ghome.at[col_at[step % 2], pl.ds(origin(step // 2) * zps + at, many)]
        return remote(
            slot, slot, g_send.at[back, step], g_recv.at[back, step],
            {"gx": target(step // 2), "col": col_at[step % 2]},
        )

    def home(block):
        low, count = g_spot(block)

        @pl.loop(0, 2 * size)
        def _(turn_at):
            step = lax.rem(turn_at + 4, 2 * size)
            t = 2 * target(step // 2) + lax.rem(col + step, 2)

            def put(z, totals):
                if z % 2:
                    pair = jnp.concatenate([totals[z - 1], totals[z]], axis=0)
                    gout[t, (low - 4 + z) // 2] = pair.astype(BF16)

            filtered(seen_rows(gsm), godd, t, low, count, True, put)

            @pl.when(step > 0)
            def _():
                g_copy(block, step).start()

            @pl.when(step == 0)
            def _():
                g_near(block).start()

    def labels_in():
        at_end = (gx == 0) | (gx == size - 1)
        for sx in range(size):
            if sx:
                at = lab_recv.at[origin(sx), pl.ds(0, 2)]
                remote(
                    at, at, l_send.at[0, sx], l_recv.at[0, sx], {"gx": target(sx)}
                ).wait_recv()

            @pl.when(at_end)
            def _(sx=sx):
                at = lab_recv.at[origin(sx), 2]
                remote(
                    at, at, l_send.at[1, sx], l_recv.at[1, sx], {"gx": target(sx), "gz": right}
                ).wait_recv()
                lab_wide[origin(sx), 2] = lab_recv[origin(sx), 2].astype(F32)

        l_own.wait()
        low_edge = 2 - (gx + size - 1) // size
        high_edge = 1 + (gx + 1) // size
        for p in range(size):
            lab_win[p, 1 : 1 + zps, :] = lab_recv[p, 0].astype(F32)
            lab_wide[p, 1] = lab_recv[p, 1].astype(F32)
            lab_win[p, 0:1, :] = lab_wide[p, low_edge, pl.ds(2 * gx, 1), :]
            lab_win[p, 1 + zps : 2 + zps, :] = lab_wide[p, high_edge, pl.ds(2 * gx + 1, 1), :]

    def next_piece(piece):
        for sx, sc in others:
            f_wait(piece - 1, sx, sc).wait_send()
        for ct in range(2):
            f_send_all(piece, ct)

    next_piece(1)
    arrived(0)
    labels_in()
    ahead_of(0)
    next_piece(2)
    arrived(1)
    ahead_of(1)
    back_of(0)
    home(0)
    arrived(2)
    ahead_of(2)
    back_of(1)
    home(1)
    back_of(2)
    home(2)

    def tile_body(it, sums25):
        t, base = it // 4, 4 + 8 * lax.rem(it, 4)
        before, after = lax.rem(t + 2 * size - 2, 2 * size), lax.rem(t + 2, 2 * size)
        grads = [seen_rows(gsm)(t, base + z) for z in range(8)]
        news = list(sums25)
        for z in range(12):
            at = base + z - 2
            views = (
                field[before, at], odd[before, at], field[t, at], odd[t, at], field[after, at]
            )
            for j in range(5):
                if 0 <= z - j < 8:
                    for i in range(5):
                        news[5 * i + j] = news[5 * i + j] + views[i] * grads[z - j]
        return tuple(news)

    sums25 = lax.fori_loop(
        0, 8 * size, tile_body, tuple(jnp.zeros((8, 128), F32) for q in range(25))
    )
    for q in range(25):
        acc[8 * q : 8 * q + 8, :] = sums25[q]

    @pl.loop(0, 8, unroll=8)
    def _(cp):
        grads, fields = unit_of(gwall, 4, OWN, cp), unit_of(smooth, 4, OWN, cp)
        both = cast_dot(grads, fields, ((0,), (0,)))
        for par in range(2):
            wall_acc[par, cp] = jnp.zeros((8, 128), F32)
        for yh in range(2):
            here, far = slice(128 * yh, 128 * yh + 128), slice(128 - 128 * yh, 256 - 128 * yh)
            for g in range(16):
                at = slice(128 * yh + 8 * g, 128 * yh + 8 * g + 8)
                tile = both[at, here] * band_tile[yh, 8 * g : 8 * g + 8, :]
                if g % 8 == (0 if yh else 7):
                    edge = both[at, far] * band_tile[2 + yh, 8 * g : 8 * g + 8, :]
                    tile = tile + pltpu.roll(edge, 64, 1)
                wall_acc[g // 8, cp] = wall_acc[g // 8, cp] + pltpu.roll(tile, (128 - 8 * g) % 128, 1)

    inner_row = lax.rem(lax.broadcasted_iota(jnp.int32, (64, 128), 0), 8)
    halves = lax.broadcasted_iota(jnp.int32, (128, 128), 0) // 64
    parity = lax.rem(lax.broadcasted_iota(jnp.int32, (128, 128), 1), 2)
    lines = dot(acc[...], (halves == parity).astype(F32))
    total = jnp.zeros((8, 128), F32)
    for q in range(25):
        total = jnp.where(lane // 2 == q, lines[8 * q : 8 * q + 8, :], total)

    full_row = lax.broadcasted_iota(jnp.int32, (ROWS, ROWS), 0)
    full_lane = lax.broadcasted_iota(jnp.int32, (ROWS, ROWS), 1)
    row_z = lax.rem(full_row, HALF) // 8 * 2 + lax.rem(full_row, 2)
    matrix = jnp.zeros((ROWS, ROWS), F32)
    for block in range(BLOCKS):
        base = 2 + BLOCK * block
        value = gram[block, 0]
        for p in range(1, size):
            value = value + gram[block, p]
        keep = (row_z == full_lane // 8) & (row_z + base >= 4) & (row_z + base < 4 + OWN)
        matrix = matrix + jnp.where(keep, value, 0.0)
    gather = (
        lax.broadcasted_iota(jnp.int32, (8, ROWS), 0)
        == lax.rem(lax.broadcasted_iota(jnp.int32, (8, ROWS), 1), 8)
    ).astype(F32)
    by_row = dot(gather, matrix, ((1,), (1,)))
    source_row = lax.broadcasted_iota(jnp.int32, (ROWS, 128), 0)
    place = 2 * (34 + lax.rem(source_row, 8) // 2) + source_row // HALF
    place = place == lax.broadcasted_iota(jnp.int32, (ROWS, 128), 1)
    total = total + dot(by_row, place.astype(F32))
    stack = (
        lax.broadcasted_iota(jnp.int32, (8, 64), 0)
        == lax.broadcasted_iota(jnp.int32, (8, 64), 1) // 8
    ).astype(F32)
    for par in range(2):
        value = wall_acc[par].reshape(64, 128)
        for r in range(1, 8):
            value = jnp.where(inner_row == r, pltpu.roll(value, 128 - r, 1), value)
        by_lane = dot(stack, value)
        source = lax.rem(square_row // 2 + 4, 64)
        place = (lax.rem(square_row, 2) == 0) & (source < 9) & (
            square_lane == 2 * (25 + source) + par
        )
        total = total + dot(by_lane, place.astype(F32))
    mine[...] = total

    def r_copy(n):
        return remote(mine, sums.at[me], r_send.at[n + 1], r_recv.at[n + 1], coords(*steps[n]))

    r_own = pltpu.make_async_copy(mine, sums.at[me], r_recv.at[0])
    r_own.start()

    for n in range(len(steps)):
        r_copy(n).start()

    for back in range(BLOCKS):
        for step in range(1, 2 * size):
            g_wait(back, step).wait_recv()
        g_near(back).wait()

    for n, (sx, sz, sc) in enumerate(steps):
        place = (origin(sx) * depth + gz_at[-sz % depth]) * 2 + col_at[sc]
        remote(
            sums.at[place], sums.at[place], r_send.at[n + 1], r_recv.at[n + 1], coords(sx, sz, sc)
        ).wait_recv()
    r_own.wait()
    for piece in (2,):
        for sx, sc in others:
            f_wait(piece, sx, sc).wait_send()
    pl.when(gx == 0)(lambda: f_copy(0, 0, col, edge_part(0)[0], 1).wait_send())
    pl.when(gx == size - 1)(lambda: f_copy(last, 0, col, edge_part(last)[0], -1).wait_send())
    for sx in range(size):
        if sx:
            l_copy(sx).wait_send()
        at_ends(sx, lambda copy: copy.wait_send())
    for block in range(BLOCKS):
        p_copy(block).wait_send()
    for back in range(BLOCKS):
        for step in range(1, 2 * size):
            g_copy(back, step).wait_send()

    for n in range(len(steps)):
        r_copy(n).wait_send()


def last_kernel(volume, home, sums, out, tile_out, wall_out, class_out, turn, red):
    members = sums.shape[0] // 2

    for side in range(2):
        @pl.loop(0, 64, unroll=8)
        def _(zp, side=side):
            at = pl.ds(pl.multiple_of(side * 1024 + zp * 16, 16), 16)
            turn[at, :] = home[side, zp].astype(F32)

    for cp in range(16):
        block = turn[pl.ds(cp // 8 * 1024 + cp % 8, 128, stride=8), :].T
        out[pl.ds(2 * cp, 2)] = block.reshape(2, 64, 128).astype(BF16)

    spot = lax.broadcasted_iota(jnp.int32, (128, 128), 0)
    want = 2 * lax.broadcasted_iota(jnp.int32, (128, 128), 1)
    red[...] = jnp.zeros((128, 128), F32)
    for half in range(2):
        total = sums[half]
        for member in range(1, members):
            total = total + sums[2 * member + half]
        total = total / volume
        for par in range(2):
            red[pl.ds(half * 16 + par, 8, stride=2), :] = dot(
                total, (spot == want + par).astype(F32)
            )
    turned = red[...].T
    tile_out[...] = red[0:32, 0:25]
    wall_out[...] = turned[25:34, 0:32]
    class_out[...] = turned[34:38, 0:32]


def regional(
    size, depth, volume,
    features, labels, grid_index, stretch, tile_filter, wall_filter, class_weight,
):
    chans = features.shape[0]
    levels = stretch.shape[0]
    everyone = size * depth * 2
    dma = pltpu.SemaphoreType.DMA
    far = pl.BlockSpec(memory_space=pl.ANY)
    wide = pltpu.VMEM((2 * size, WIN, 8, 128), F32)
    rows = pltpu.VMEM((2, WIN * size * 8, 128), F32)
    block = pltpu.VMEM((BLOCKS, size, ROWS, 256), F32)
    half = pltpu.VMEM((BLOCKS, size, HALF, 256), F32)
    home, sums = pl.pallas_call(
        functools.partial(region_kernel, (size, depth, volume)),
        out_shape=(
            jax.ShapeDtypeStruct((2, 64, 16, 128), BF16),
            jax.ShapeDtypeStruct((everyone, 8, 128), F32),
        ),
        in_specs=[far] * 7,
        out_specs=(far, far),
        scratch_shapes=[
            pltpu.VMEM((chans, 64, 128), BF16),
            pltpu.VMEM((128, 128), jnp.int32),
            pltpu.VMEM((1, 64), jnp.int32),
            pltpu.VMEM((levels, 9), F32),
            pltpu.VMEM((chans, 25), F32),
            pltpu.VMEM((9, chans), F32),
            pltpu.VMEM((4, chans), F32),
            pltpu.VMEM((3, 1024, 128), F32),
            pltpu.VMEM((2, 64, 16, 128), BF16),
            pltpu.VMEM((size, 2, WIN // 2, 16, 128), BF16),
            pltpu.VMEM((64, 128), F32),
            pltpu.VMEM((size, 2, 16, 128), BF16),
            pltpu.VMEM((size, 3, 16, 128), BF16),
            pltpu.VMEM((size, 3, 16, 128), F32),
            pltpu.VMEM((size, 24, 128), F32),
            wide, wide, rows, rows, rows, wide,
            block, block, half, half,
            pltpu.VMEM((25, 8, 128), F32),
            pltpu.VMEM((9, 4, 8, 128), F32),
            pltpu.VMEM((8, 256, 256), BF16),
            pltpu.VMEM((8, 256, 256), BF16),
            pltpu.VMEM((4, 128, 128), F32),
            pltpu.VMEM((2, ROWS * size, 128), F32),
            pltpu.VMEM((2, 8, 8, 128), F32),
            pltpu.VMEM((25 * 8, 128), F32),
            pltpu.VMEM((BLOCKS, size, ROWS, ROWS), F32),
            pltpu.VMEM((128, 128), F32),
            pltpu.VMEM((128, 128), F32),
            pltpu.VMEM((128, 128), F32),
            pltpu.VMEM((2 * size, OWN // 2, 16, 128), BF16),
            pltpu.VMEM((8, 128), F32),
            pltpu.VMEM((128, 128), F32),
            dma((8,)), dma((4,)),
            dma((len(PIECES), size, 2)), dma((len(PIECES), size, 2)),
            dma((2, size)), dma((2, size)),
            dma((BLOCKS,)), dma((BLOCKS,)),
            dma((BLOCKS, 2 * size)), dma((BLOCKS, 2 * size)),
            dma((everyone,)), dma((everyone,)),
        ],
        compiler_params=pltpu.CompilerParams(
            collective_id=0, has_side_effects=True, vmem_limit_bytes=63 * 1024 * 1024
        ),
    )(
        features.reshape(chans, 64, 128), labels.reshape(128, 128), grid_index.reshape(1, 64),
        stretch, tile_filter, wall_filter.T, class_weight,
    )
    def whole(*shape):
        return pl.BlockSpec(shape, lambda: (0,) * len(shape))

    grad, tile_grad, wall_grad, class_grad = pl.pallas_call(
        functools.partial(last_kernel, volume),
        out_shape=(
            jax.ShapeDtypeStruct((chans, 64, 128), BF16),
            jax.ShapeDtypeStruct((chans, 25), F32),
            jax.ShapeDtypeStruct((9, chans), F32),
            jax.ShapeDtypeStruct((4, chans), F32),
        ),
        in_specs=[
            whole(2, 64, 16, 128),
            whole(everyone, 8, 128),
        ],
        out_specs=(
            whole(chans, 64, 128),
            whole(chans, 25), whole(9, chans), whole(4, chans),
        ),
        scratch_shapes=[pltpu.VMEM((2048, 128), F32), pltpu.VMEM((128, 128), F32)],
    )(home, sums)
    return grad.reshape(features.shape), tile_grad, wall_grad.T, class_grad


def shards(features, labels, grid_index, stretch, tile_filter, wall_filter, class_weight):
    chans, rows, cells_x, cells_z = features.shape
    size, depth = lax.axis_size("gx"), lax.axis_size("gz")
    volume = labels.shape[0] * cells_x * size * cells_z * depth
    cpg = chans // size
    if 128 // size == OWN:
        return regional(
            size, depth, volume,
            features, labels, grid_index, stretch, tile_filter, wall_filter, class_weight,
        )
    chunks = min(4, cpg)
    per_dest = max(cpg // 4, 1) * 8
    xs = 2 * size
    everyone = size * depth * 2
    onehot = (grid_index[:, None] == jnp.arange(stretch.shape[0], dtype=jnp.int32)).astype(F32)
    bands = jnp.dot(onehot, stretch, precision=lax.Precision.HIGHEST)
    dma = pltpu.SemaphoreType.DMA
    vmem = pl.BlockSpec(memory_space=pltpu.VMEM)
    smem = pl.BlockSpec(memory_space=pltpu.SMEM)
    grad, tile_grad, wall_grad, class_grad = pl.pallas_call(
        functools.partial(kernel, (size, depth, cpg, chunks, volume)),
        out_shape=(
            jax.ShapeDtypeStruct((chans, 64, 128), BF16),
            jax.ShapeDtypeStruct((chans, 25), F32),
            jax.ShapeDtypeStruct((9, chans), F32),
            jax.ShapeDtypeStruct((4, chans), F32),
        ),
        in_specs=[vmem, vmem, vmem, smem, smem, smem],
        out_specs=(vmem, vmem, vmem, vmem),
        scratch_shapes=[
            pltpu.VMEM((size, cpg, 64, 128), BF16),
            pltpu.VMEM((80, 9), F32),
            pltpu.VMEM((size, per_dest, 128), F32),
            pltpu.VMEM((2, size, per_dest, 128), F32),
            pltpu.VMEM((5, cpg, xs, 32, 128), F32),
            pltpu.VMEM((cpg, xs, 48, 128), F32),
            pltpu.VMEM((max(cpg, size), 64, 128), F32),
            pltpu.VMEM((cpg, 9, 48, 128), F32),
            pltpu.VMEM((9, 48, 128), F32),
            pltpu.VMEM((cpg, xs, 32, 128), F32),
            pltpu.VMEM((cpg, xs, 32, 128), F32),
            pltpu.VMEM((256, 128), F32),
            pltpu.VMEM((size, 256, 128), BF16),
            pltpu.VMEM((size, 256, 128), BF16),
            pltpu.VMEM((size, 256, 128), BF16),
            pltpu.VMEM((cpg, xs, 48, 128), F32),
            pltpu.VMEM((cpg, xs, 32, 128), F32),
            pltpu.VMEM((cpg, xs // 8, 8, 128), F32),
            pltpu.VMEM((2, cpg, xs // 8, 8, 128), F32),
            pltpu.VMEM((5, cpg, xs, 32, 128), F32),
            pltpu.VMEM((size, cpg, 64, 128), BF16),
            pltpu.VMEM((size, 64, 128), F32),
            pltpu.VMEM((cpg, 40, 8, 128), F32),
            pltpu.VMEM((128, 128), F32),
            pltpu.VMEM((everyone, 8, 128), F32),
            dma((chunks, size)), dma((chunks, size)), dma(()),
            dma((2, size)), dma((2, size)),
            dma((cpg,)), dma((cpg,)),
            dma((size,)), dma((size,)),
            dma((size,)), dma((size,)),
            dma((size,)), dma((size,)),
            dma((2, cpg)), dma((2, cpg)),
            dma((chunks, size)), dma((chunks, size)),
            dma((everyone,)), dma((everyone,)),
        ],
        compiler_params=pltpu.CompilerParams(
            collective_id=0, has_side_effects=True, vmem_limit_bytes=48 * 1024 * 1024
        ),
    )(
        features.reshape(chans, 64, 128), labels.reshape(128, 128), bands,
        tile_filter, wall_filter.T, class_weight,
    )
    return grad.reshape(features.shape), tile_grad, wall_grad.T, class_grad


def solution(mesh):
    return jax.shard_map(
        shards,
        mesh=mesh,
        in_specs=(
            P(None, "col", ("group", "gx"), "gz"),
            P(None, ("group", "gx"), "gz"),
            P(),
            P(),
            P(),
            P(),
            P(),
        ),
        out_specs=(
            P(None, "col", ("group", "gx"), "gz"),
            P("group", None),
            P("group", None),
            P("group", None),
        ),
        check_vma=False,
    )
```

```python
import functools

import jax
import jax.numpy as jnp
from jax import lax
from jax.experimental import pallas as pl
from jax.experimental.pallas import tpu as pltpu
from jax.sharding import PartitionSpec as P

F32 = jnp.float32
BF16 = jnp.bfloat16
MESH = pl.DeviceIdType.MESH


def fold(value):
    total = value[0:8]
    for row in range(8, value.shape[0], 8):
        total = total + value[row : row + 8]
    return total


def rounded(value):
    return value.astype(BF16).astype(F32)


def kernel(
    dims,
    feat, labels, bands, tile_w, wall_w, class_w,
    out, tile_out, wall_out, class_out,
    recv, band_pad, halo_out, halo_in, zfeat, smooth, stage, taps, band_rows, hid, slope,
    part_own, part_out, part_in, err, gwall, gsm, ghalo_out, ghalo_in, zgrad, gout, gstage,
    acc, red, sums,
    a_send, a_recv, own_sem, h_send, h_recv, s_send, s_recv, p_send, p_recv, e_send, e_recv,
    w_send, w_recv, g_send, g_recv, o_send, o_recv, r_send, r_recv,
):
    size, depth, cpg, chunks, volume = dims
    per = cpg // chunks
    xs = 2 * size
    xgroups = xs // 8
    everyone = size * depth * 2
    gx, gz, col = lax.axis_index("gx"), lax.axis_index("gz"), lax.axis_index("col")
    me = (gx * depth + gz) * 2 + col
    other = 1 - col
    right, left = lax.rem(gz + 1, depth), lax.rem(gz + depth - 1, depth)
    chan0 = gx * cpg

    def peer(step):
        return lax.rem(gx + step, size)

    def source(step):
        return lax.rem(gx + size - step, size)

    def coords(step):
        index = lax.rem(me + step, everyone)
        return {
            "gx": index // (2 * depth),
            "gz": lax.rem(index // 2, depth),
            "col": lax.rem(index, 2),
        }

    barrier = pltpu.get_barrier_semaphore()

    @pl.loop(1, everyone)
    def _(step):
        pl.semaphore_signal(barrier, inc=1, device_id=coords(step), device_id_type=MESH)

    pl.semaphore_wait(barrier, everyone - 1)

    def remote(src, dst, send, rec, device):
        return pltpu.make_async_remote_copy(
            src_ref=src, dst_ref=dst, send_sem=send, recv_sem=rec,
            device_id=device, device_id_type=MESH,
        )

    def a_copy(chunk, step):
        return remote(
            feat.at[pl.ds(peer(step) * cpg + chunk * per, per)],
            recv.at[step, pl.ds(chunk * per, per)],
            a_send.at[chunk, step], a_recv.at[chunk, step], {"gx": peer(step)},
        )

    def h_copy(way, step):
        return remote(
            halo_out.at[peer(step)], halo_in.at[way, step],
            h_send.at[way, step], h_recv.at[way, step],
            {"gx": peer(step), "gz": right if way == 0 else left},
        )

    own_copy = pltpu.make_async_copy(feat.at[pl.ds(chan0, cpg)], recv.at[0], own_sem)
    own_copy.start()
    for step in range(1, size):
        a_copy(0, step).start()

    lane = lax.broadcasted_iota(jnp.int32, (8, 128), 1)
    quad = lane // 4

    @pl.loop(0, size)
    def _(group):
        for first in range(0, cpg, 4):
            packed = jnp.zeros((8, 128), F32)
            for c in range(first, min(first + 4, cpg)):
                stage[c] = feat[group * cpg + c].astype(F32)
                for xl in range(2):
                    rows = stage[c, pl.ds(xl, 32, stride=2), :]
                    for t in range(4):
                        m = (c - first) * 8 + xl * 4 + t
                        turned = pltpu.roll(rows[8 * t : 8 * t + 8], (2 + 4 * m) % 128, 1)
                        packed = jnp.where(quad == m, turned, packed)
            halo_out[group, pl.ds(first // 4 * 8, 8), :] = packed

    for way in range(2):
        for step in range(size):
            h_copy(way, step).start()
    for chunk in range(1, chunks):
        for step in range(1, size):
            a_copy(chunk, step).start()

    band_pad[0:8] = jnp.zeros((8, 9), F32)
    band_pad[8:72] = bands[...]
    band_pad[72:80] = jnp.zeros((8, 9), F32)
    for k in range(9):
        band_rows[k] = jnp.broadcast_to(band_pad[pl.ds(32 * col, 48), k : k + 1], (48, 128))

    @pl.loop(0, cpg)
    def _(c):
        for k in range(9):
            taps[c, k] = wall_w[k, chan0 + c] * band_rows[k]
        for x_group in range(0, xs, 8):
            blank = jnp.zeros((8, 8, 128), F32)
            smooth[c, pl.ds(x_group, 8), pl.ds(pl.multiple_of(40 * col, 8), 8), :] = blank
            gwall[c, pl.ds(x_group, 8), pl.ds(pl.multiple_of(40 * col, 8), 8), :] = blank
        for q in range(40):
            acc[c, q] = jnp.zeros((8, 128), F32)

    red[...] = jnp.zeros((128, 128), F32)

    def shifts(value, edge):
        return (
            pltpu.roll(jnp.where(lane >= 126, edge, value), 2, 1),
            pltpu.roll(jnp.where(lane == 127, edge, value), 1, 1),
            value,
            pltpu.roll(jnp.where(lane == 0, edge, value), 127, 1),
            pltpu.roll(jnp.where(lane < 2, edge, value), 126, 1),
        )

    def filtered(field, c, x, flip):
        total = None
        for i in range(5):
            at = lax.rem(x + (4 - i if flip else i) - 2 + xs, xs)
            for j in range(5):
                term = tile_w[chan0 + c, 5 * i + j] * field[4 - j if flip else j, c, at]
                total = term if total is None else total + term
        return total

    def y_copy(ref, index, send, rec):
        src = pl.multiple_of(32 - 24 * col, 8)
        dst = pl.multiple_of(40 * col, 8)
        return remote(
            ref.at[index + (pl.ds(src, 8),)], ref.at[index + (pl.ds(dst, 8),)],
            send, rec, {"col": other},
        )

    def s_copy(c):
        return y_copy(smooth, (c, pl.ds(0, xs)), s_send.at[c], s_recv.at[c])

    own_copy.wait()
    for way in range(2):
        for step in range(size):
            h_copy(way, step).wait_recv()

    def edges_of(ref_left, ref_right):
        return jnp.where(lax.rem(lane, 4) < 2, ref_left, ref_right)

    for chunk in range(chunks):
        for step in range(1, size):
            a_copy(chunk, step).wait_recv()
        for c in range(chunk * per, chunk * per + per):

            @pl.loop(0, size, unroll=2)
            def _(step, c=c):
                s = source(step)
                stage[step] = recv[step, c].astype(F32)
                at = pl.ds(c // 4 * 8, 8)
                packed = edges_of(halo_in[0, step, at, :], halo_in[1, step, at, :])
                for xl in range(2):
                    rows = stage[step, pl.ds(xl, 32, stride=2), :]
                    for t in range(4):
                        m = c % 4 * 8 + xl * 4 + t
                        edge = pltpu.roll(packed, (126 - 4 * m) % 128, 1)
                        moved = shifts(rows[8 * t : 8 * t + 8], edge)
                        for j in range(5):
                            zfeat[j, c, 2 * s + xl, pl.ds(8 * t, 8), :] = moved[j]

            @pl.loop(0, xs, unroll=4)
            def _(x, c=c):
                smooth[c, x, pl.ds(8, 32), :] = rounded(filtered(zfeat, c, x, False))

            s_copy(c).start()

    for c in range(cpg):
        s_copy(c).wait_recv()

    def p_copy(step):
        return remote(
            part_out.at[step], part_in.at[step], p_send.at[step], p_recv.at[step],
            {"gx": peer(step)},
        )

    def scores_at(x):
        def body(c, totals):
            wall = None
            for k in range(9):
                term = taps[c, k, pl.ds(8, 32), :] * smooth[c, x, pl.ds(4 + k, 32), :]
                wall = term if wall is None else wall + term
            sig = jax.nn.sigmoid(wall)
            hidden = wall * sig
            hid[c, x] = hidden
            slope[c, x] = sig * (1.0 + wall * (1.0 - sig))
            return tuple(
                total + class_w[k, chan0 + c] * hidden for k, total in enumerate(totals)
            )

        return lax.fori_loop(
            0, cpg, body, tuple(jnp.zeros((32, 128), F32) for k in range(4)), unroll=min(4, cpg)
        )

    @pl.loop(1, size)
    def _(step):
        for xl in range(2):
            totals = scores_at(2 * peer(step) + xl)
            for k in range(4):
                part_out[step, pl.ds((2 * k + xl) * 32, 32), :] = totals[k].astype(BF16)
        p_copy(step).start()

    for xl in range(2):
        totals = scores_at(2 * gx + xl)
        for k in range(4):
            part_own[pl.ds((2 * k + xl) * 32, 32), :] = totals[k]

    @pl.loop(1, size)
    def _(step):
        p_copy(step).wait_recv()
        part_own[...] = part_own[...] + part_in[step].astype(F32)

    for xl in range(2):
        marks = labels[pl.ds(64 * col + xl, 32, stride=2), :]
        for k in range(4):
            at = pl.ds((2 * k + xl) * 32, 32)
            err[0, at, :] = (part_own[at, :] - jnp.where(marks == k, 1.0, 0.0)).astype(BF16)

    def e_copy(step):
        return remote(
            err.at[0], err.at[step], e_send.at[step], e_recv.at[step], {"gx": peer(step)}
        )

    for step in range(1, size):
        e_copy(step).start()

    def w_copy(step):
        return y_copy(
            gwall, (pl.ds(0, cpg), pl.ds(2 * source(step), 2)), w_send.at[step], w_recv.at[step]
        )

    def wall_grads(step):
        for xl in range(2):
            x = 2 * source(step) + xl
            errors = [err[step, pl.ds((2 * k + xl) * 32, 32), :].astype(F32) for k in range(4)]

            @pl.loop(0, cpg, unroll=min(4, cpg))
            def _(c):
                hidden = hid[c, x]
                grad = None
                for k in range(4):
                    term = class_w[k, chan0 + c] * errors[k]
                    grad = term if grad is None else grad + term
                    acc[c, 34 + k] = acc[c, 34 + k] + fold(errors[k] * hidden)
                gwall[c, x, pl.ds(8, 32), :] = rounded(grad * slope[c, x])

        w_copy(step).start()

    wall_grads(0)

    @pl.loop(1, size)
    def _(step):
        e_copy(step).wait_recv()
        wall_grads(step)

    @pl.loop(0, size)
    def _(step):
        w_copy(step).wait_recv()

    def g_copy(way, c):
        return remote(
            ghalo_out.at[c], ghalo_in.at[way, c], g_send.at[way, c], g_recv.at[way, c],
            {"gz": right if way == 0 else left},
        )

    @pl.loop(0, cpg)
    def _(c):
        def body(x, sums9):
            grad = gwall[c, x, pl.ds(8, 32), :]
            total = None
            news = []
            for k in range(9):
                term = taps[c, k, pl.ds(12 - k, 32), :] * gwall[c, x, pl.ds(12 - k, 32), :]
                total = term if total is None else total + term
                product = grad * band_rows[k, pl.ds(8, 32), :] * smooth[c, x, pl.ds(4 + k, 32), :]
                news.append(sums9[k] + fold(product))
            gsm[c, x] = rounded(total)
            return tuple(news)

        sums9 = lax.fori_loop(0, xs, body, tuple(jnp.zeros((8, 128), F32) for k in range(9)), unroll=2)
        for k in range(9):
            acc[c, 25 + k] = sums9[k]

        @pl.loop(0, xgroups)
        def _(group):
            packed = jnp.zeros((8, 128), F32)
            for m in range(32):
                piece = gsm[c, group * 8 + m // 4, pl.ds(m % 4 * 8, 8), :]
                packed = jnp.where(quad == m, pltpu.roll(piece, (2 + 4 * m) % 128, 1), packed)
            ghalo_out[c, group] = packed

        for way in range(2):
            g_copy(way, c).start()

    def o_copy(chunk, step):
        return remote(
            gout.at[peer(step), pl.ds(chunk * per, per)],
            out.at[pl.ds(chan0 + chunk * per, per)],
            o_send.at[chunk, step], o_recv.at[chunk, step], {"gx": peer(step)},
        )

    @pl.loop(0, chunks)
    def _(chunk):
        @pl.loop(0, per)
        def _(lower):
            c = chunk * per + lower
            for way in range(2):
                g_copy(way, c).wait_recv()

            @pl.loop(0, xgroups)
            def _(group):
                packed = edges_of(ghalo_in[0, c, group], ghalo_in[1, c, group])
                for m in range(32):
                    at = pl.ds(m % 4 * 8, 8)
                    x = group * 8 + m // 4
                    edge = pltpu.roll(packed, (126 - 4 * m) % 128, 1)
                    moved = shifts(gsm[c, x, at, :], edge)
                    for j in range(5):
                        zgrad[j, c, x, at, :] = moved[j]

            @pl.loop(0, size, unroll=2)
            def _(s):
                for xl in range(2):
                    gstage[s, pl.ds(xl, 32, stride=2), :] = filtered(zgrad, c, 2 * s + xl, True)
                gout[s, c] = gstage[s].astype(BF16)

            out[chan0 + c] = gout[gx, c]

        for step in range(1, size):
            o_copy(chunk, step).start()

    row = lax.broadcasted_iota(jnp.int32, (8, 128), 0)

    @pl.loop(0, cpg)
    def _(c):
        def body(x, sums25):
            grad = gsm[c, x]
            news = []
            for i in range(5):
                at = lax.rem(x + i - 2 + xs, xs)
                for j in range(5):
                    news.append(sums25[5 * i + j] + fold(zfeat[j, c, at] * grad))
            return tuple(news)

        sums25 = lax.fori_loop(0, xs, body, tuple(jnp.zeros((8, 128), F32) for q in range(25)), unroll=2)
        for q in range(38):
            value = sums25[q] if q < 25 else acc[c, q]
            red[pl.ds(q, 1), :] = jnp.sum(value, axis=0, keepdims=True)
        line = lax.dot_general(
            jnp.ones((8, 128), F32), red[...], (((1,), (1,)), ((), ())),
            precision=lax.Precision.HIGHEST, preferred_element_type=F32,
        )
        before = jnp.where(c == 0, jnp.zeros((8, 128), F32), sums[me])
        sums[me] = jnp.where(row == c, line, before)

    def r_copy(step):
        return remote(sums.at[me], sums.at[me], r_send.at[step], r_recv.at[step], coords(step))

    @pl.loop(1, everyone)
    def _(step):
        r_copy(step).start()

    @pl.loop(1, everyone)
    def _(step):
        r_copy(step).wait_recv()

    @pl.loop(0, size)
    def _(group):
        total = sums[group * depth * 2]
        for member in range(1, depth * 2):
            total = total + sums[group * depth * 2 + member]
        red[pl.ds(group * cpg, cpg), :] = total[0:cpg] / volume

    turned = red[...].T
    chans = size * cpg
    tile_out[...] = red[0:chans, 0:25]
    wall_out[...] = turned[25:34, 0:chans]
    class_out[...] = turned[34:38, 0:chans]

    for chunk in range(chunks):
        for step in range(1, size):
            o_copy(chunk, step).wait()
            a_copy(chunk, step).wait_send()
    for way in range(2):
        for step in range(size):
            h_copy(way, step).wait_send()
        for c in range(cpg):
            g_copy(way, c).wait_send()
    for c in range(cpg):
        s_copy(c).wait_send()
    for step in range(1, size):
        p_copy(step).wait_send()
        e_copy(step).wait_send()
    for step in range(size):
        w_copy(step).wait_send()

    @pl.loop(1, everyone)
    def _(step):
        r_copy(step).wait_send()


OWN = 32
WIN = OWN + 8
BLOCK = 12
BLOCKS = (WIN - 4) // BLOCK
ROWS = BLOCK * 8
HALF = ROWS // 2
PIECES = ((0, 8), (8, 6), (14, 6))
RETURNS = ((0, 4), (4, 6), (10, 6))
WANTED = 38
HIGH = lax.Precision.HIGHEST


def cast_dot(a, b, dims=((1,), (0,))):
    return lax.dot_general(
        a.astype(BF16), b.astype(BF16), (dims, ((), ())), preferred_element_type=F32
    )


def split_dot(a, b):
    a_high, b_high = a.astype(BF16), b.astype(BF16)
    a_low, b_low = (a - a_high.astype(F32)).astype(BF16), (b - b_high.astype(F32)).astype(BF16)
    return cast_dot(a_high, b_high) + (cast_dot(a_high, b_low) + cast_dot(a_low, b_high))


def dot(a, b, dims=((1,), (0,))):
    return lax.dot_general(a, b, (dims, ((), ())), precision=HIGH, preferred_element_type=F32)


def region_kernel(
    dims,
    feat_h, lab_h, index_h, stretch_h, tile_h, wall_h, class_h,
    ghome, sums,
    feat, lab, index, stretch, tile_w, wall_w, class_w,
    turn, send, recv, lab_rows, lab_send, lab_recv, lab_wide, lab_win,
    field, odd, smooth, gwall, gsm, godd, hid, slope, part_out, part_in,
    taps, fore, wide, wide_t, band_tile, wall, wall_acc, acc, gram, params, classes, classes_t,
    gout, mine, red,
    in_sem, own_sem, f_send, f_recv, l_send, l_recv, p_send, p_recv, g_send, g_recv, r_send, r_recv,
):
    size, depth, volume = dims
    everyone = size * depth * 2
    gx, gz, col = lax.axis_index("gx"), lax.axis_index("gz"), lax.axis_index("col")
    me = (gx * depth + gz) * 2 + col
    right, left = lax.rem(gz + 1, depth), lax.rem(gz + depth - 1, depth)
    zps = OWN // 2
    lane = lax.broadcasted_iota(jnp.int32, (8, 128), 1)
    row = lax.broadcasted_iota(jnp.int32, (8, 128), 0)
    first = lane < 64
    y_lane = lax.rem(lane, 64) // 2
    x_even = lax.rem(lane, 2) == 0

    ins = [
        pltpu.make_async_copy(src, dst, in_sem.at[n])
        for n, (src, dst) in enumerate((
            (feat_h.at[pl.ds(0, 16)], feat.at[pl.ds(0, 16)]),
            (feat_h.at[pl.ds(16, 16)], feat.at[pl.ds(16, 16)]),
            (lab_h, lab), (index_h, index), (stretch_h, stretch),
            (tile_h, tile_w), (wall_h, wall_w), (class_h, class_w),
        ))
    ]
    for copy in ins:
        copy.start()

    gx_at = [lax.rem(gx + n, size) for n in range(size)]
    gz_at = [lax.rem(gz + n, depth) for n in range(depth)]
    col_at = [col, 1 - col]
    steps = [
        (sx, sz, sc)
        for sx in range(size) for sz in range(depth) for sc in range(2) if sx or sz or sc
    ]

    def coords(sx, sz, sc):
        return {"gx": gx_at[sx], "gz": gz_at[sz], "col": col_at[sc]}

    barrier = pltpu.get_barrier_semaphore()
    for step in steps:
        pl.semaphore_signal(barrier, inc=1, device_id=coords(*step), device_id_type=MESH)

    def remote(src, dst, sent, got, device):
        return pltpu.make_async_remote_copy(
            src_ref=src, dst_ref=dst, send_sem=sent, recv_sem=got,
            device_id=device, device_id_type=MESH,
        )

    def target(sx):
        return gx_at[sx] if isinstance(sx, int) else lax.rem(gx + sx, size)

    def origin(sx):
        return gx_at[-sx % size]

    def turned_features(side):
        ins[side].wait()
        for cp in range(8):
            block = feat[pl.ds(side * 16 + 2 * cp, 2)].astype(F32).reshape(128, 128)
            turn[side, pl.ds(cp, 128, stride=8), :] = block.T

        @pl.loop(0, 64, unroll=8)
        def _(zp):
            at = pl.ds(pl.multiple_of(zp * 16, 16), 16)
            send[side, zp] = turn[side, at, :].astype(BF16)

    last = len(PIECES) - 1

    def f_copy(piece, sx, ct, part, way):
        t, sc = target(sx), col_at[ct] if isinstance(ct, int) else 0
        at, count = part
        return remote(
            send.at[ct, pl.ds(lax.rem(t * zps + at - 2 + 64, 64), count)],
            recv.at[gx, col, pl.ds(at, count)],
            f_send.at[piece, sx, sc], f_recv.at[piece, sx, sc],
            {"gx": t, "gz": gz_at[way % depth], "col": ct},
        )

    def edge_part(piece):
        at, count = PIECES[piece]
        return ((at, 2), (at + 2, count - 2)) if piece == 0 else (
            (at + count - 2, 2), (at, count - 2)
        )

    def f_start(piece, sx, ct):
        t = target(sx)
        if 0 < piece < last:
            f_copy(piece, sx, ct, PIECES[piece], 0).start()
            return
        end, way = (0, 1) if piece == 0 else (size - 1, -1)
        far, near = edge_part(piece)

        @pl.when(t != end)
        def _():
            f_copy(piece, sx, ct, PIECES[piece], 0).start()

        @pl.when(t == end)
        def _():
            f_copy(piece, sx, ct, near, 0).start()
            f_copy(piece, sx, ct, far, way).start()

    def f_own(piece, part):
        at, count = part
        return pltpu.make_async_copy(
            send.at[col, pl.ds(lax.rem(gx * zps + at - 2 + 64, 64), count)],
            recv.at[gx, col, pl.ds(at, count)], own_sem.at[piece],
        )

    def own_piece(piece, whole_one, near_one, far_one):
        if 0 < piece < last:
            whole_one(f_own(piece, PIECES[piece]))
            return
        end, way = (0, 1) if piece == 0 else (size - 1, -1)
        far, near = edge_part(piece)

        @pl.when(gx != end)
        def _():
            whole_one(f_own(piece, PIECES[piece]))

        @pl.when(gx == end)
        def _():
            near_one(f_own(piece, near))
            far_one(f_copy(piece, 0, col, far, way))

    def begin(copy):
        copy.start()

    def f_send_all(piece, ct):
        for sx in (2, 1, 3):
            f_start(piece, sx, ct)

        @pl.when(col != ct)
        def _():
            f_start(piece, 0, ct)

        @pl.when(col == ct)
        def _():
            own_piece(piece, begin, begin, begin)

    others = [(sx, sc) for sx in (2, 1, 3, 0) for sc in range(2) if sx or sc]

    def f_wait(piece, sx, sc):
        slot = recv.at[origin(sx), col_at[sc], pl.ds(*PIECES[piece])]
        return remote(
            slot, slot, f_send.at[piece, sx, sc], f_recv.at[piece, sx, sc],
            {"gx": target(sx), "gz": gz, "col": col_at[sc]},
        )

    turned_features(0)
    pl.semaphore_wait(barrier, everyone - 1)
    f_send_all(0, 0)
    turned_features(1)
    f_send_all(0, 1)

    ins[2].wait()
    turn[2, 0:128, :] = lab[...].astype(F32).T
    even, uneven = turn[2, pl.ds(0, 64, stride=2), :], turn[2, pl.ds(1, 64, stride=2), :]
    here = jnp.where(col == 0, even, pltpu.roll(even, 64, 1))
    there = jnp.where(col == 0, pltpu.roll(uneven, 64, 1), uneven)
    lab_rows[...] = jnp.where(lax.broadcasted_iota(jnp.int32, (64, 128), 1) < 64, here, there)
    edge_rows = [jnp.zeros((1, 128), F32)] * 16
    for t in range(size):
        edge_rows[2 * t] = lab_rows[pl.ds((zps * t - 1) % 64, 1), :]
        edge_rows[2 * t + 1] = lab_rows[pl.ds((zps * t + zps) % 64, 1), :]
    edge_rows = jnp.concatenate(edge_rows, axis=0).astype(BF16)
    for t in range(size):
        lab_send[t, 0] = lab_rows[pl.ds(zps * t, zps), :].astype(BF16)
        lab_send[t, 1] = edge_rows

    def l_copy(sx):
        return remote(
            lab_send.at[target(sx)], lab_recv.at[gx, pl.ds(0, 2)],
            l_send.at[0, sx], l_recv.at[0, sx], {"gx": target(sx)},
        )

    def l_far(sx, way):
        return remote(
            lab_send.at[target(sx), 1], lab_recv.at[gx, 2], l_send.at[1, sx], l_recv.at[1, sx],
            {"gx": target(sx), "gz": gz_at[way % depth]},
        )

    l_own = pltpu.make_async_copy(lab_send.at[gx], lab_recv.at[gx, pl.ds(0, 2)], own_sem.at[3])
    l_own.start()

    def at_ends(sx, act):
        @pl.when(target(sx) == 0)
        def _():
            act(l_far(sx, 1))

        @pl.when(target(sx) == size - 1)
        def _():
            act(l_far(sx, -1))

    for sx in range(size):
        if sx:
            l_copy(sx).start()
        at_ends(sx, begin)

    for copy in ins[3:]:
        copy.wait()
    params[...] = jnp.zeros((128, 128), F32)
    params[0:9, 0:32] = wall_w[...]
    params[16:20, 0:32] = class_w[...]
    params[64:96, 0:25] = tile_w[...]
    red[...] = params[...].T

    def pairs(ref, start):
        return ref[pl.ds(start + col * 16, 8, stride=2), :], ref[pl.ds(start + col * 16 + 1, 8, stride=2), :]

    def spread(both, q):
        low, high = (jnp.broadcast_to(rows[:, q : q + 1], (8, 128)) for rows in both)
        return jnp.where(first, low, high)

    tile_pairs, wall_pairs = pairs(params, 64), pairs(red, 0)
    for q in range(25):
        taps[q] = spread(tile_pairs, q)

    levels = stretch.shape[0]
    hot = lax.broadcasted_iota(jnp.int32, (levels, 64), 0) == index[...]
    params[32:41, 0:64] = dot(stretch[...], hot.astype(F32), ((0,), (0,)))
    band_t = params[32:48, 0:64]
    y_row = lax.broadcasted_iota(jnp.int32, (64, 128), 0)
    y_col = lax.rem(lax.broadcasted_iota(jnp.int32, (64, 128), 1), 64) // 2
    square_row = lax.broadcasted_iota(jnp.int32, (128, 128), 0)
    square_lane = lax.broadcasted_iota(jnp.int32, (128, 128), 1)
    k_of_lane = lax.rem(lax.broadcasted_iota(jnp.int32, (16, 128), 1) // 2 + 4, 64)
    k_of_lane = (k_of_lane == lax.broadcasted_iota(jnp.int32, (16, 128), 0)) & (
        lax.rem(lax.broadcasted_iota(jnp.int32, (16, 128), 1), 2) == 0
    )
    placed = dot(band_t, k_of_lane.astype(F32), ((0,), (0,)))
    for yh in range(2):
        ahead = dot(band_t, (y_row == y_col + 32 * yh).astype(F32))
        for k in range(9):
            m = k - 4
            value = spread(wall_pairs, k) * ahead[k : k + 1, :]
            inside = (y_lane + m >= 0) & (y_lane + m < 32)
            fore[k, yh] = jnp.where(inside, value, 0.0)
            across = (y_lane + m >= 32) if yh == 0 else (y_lane + m < 0)
            fore[k, 2 + yh] = jnp.where(across, value, 0.0)
        rows_y = lax.broadcasted_iota(jnp.int32, (128, 64), 0) % 64 // 2 + 32 * yh
        at_y = rows_y == lax.broadcasted_iota(jnp.int32, (128, 64), 1)
        value = dot(at_y.astype(F32), placed)
        shift = lax.rem(square_lane // 2 + 4, 64) - 4 + square_row % 64 // 2
        inner = jnp.where((shift >= 0) & (shift < 32), value, 0.0)
        outer = jnp.where((shift >= 0) & (shift < 32), 0.0, value)
        band_tile[yh] = pltpu.roll(inner, 0, 1, stride=1, stride_axis=0)
        band_tile[2 + yh] = pltpu.roll(outer, 64, 1, stride=1, stride_axis=0)

    @pl.loop(0, 8, unroll=2)
    def _(cp):
        for yh in range(2):
            tile = jnp.zeros((128, 128), F32)
            for k in range(9):
                line = fore[k, yh, pl.ds(cp, 1), :]
                tile = jnp.where(square_row == square_lane + 2 * (k - 4), line, tile)
            wide[cp, 128 * yh : 128 * yh + 128, 128 * yh : 128 * yh + 128] = tile.astype(BF16)
            wide_t[cp, 128 * yh : 128 * yh + 128, 128 * yh : 128 * yh + 128] = tile.T.astype(BF16)
            tile = jnp.zeros((128, 128), F32)
            for k in range(5, 9) if yh == 0 else range(4):
                line = fore[k, 2 + yh, pl.ds(cp, 1), :]
                far = 2 * (k - 4) - 64 if yh == 0 else 2 * (k - 4) + 64
                tile = jnp.where(square_row == square_lane + far, line, tile)
            low, high = 128 - 128 * yh, 128 * yh
            wide[cp, low : low + 128, high : high + 128] = tile.astype(BF16)
            wide_t[cp, high : high + 128, low : low + 128] = tile.T.astype(BF16)

    chan = lax.broadcasted_iota(jnp.int32, (128, 128), 0)
    unit = lax.rem(lax.broadcasted_iota(jnp.int32, (128, 128), 1), 8)
    half_row = lax.broadcasted_iota(jnp.int32, (HALF, 128), 0)
    half_z = lax.broadcasted_iota(jnp.int32, (HALF, 128), 1) // 8
    half_k = lax.rem(half_row, 8) // 2
    same_z = (half_row // 8) * 2 + lax.rem(half_row, 2) == half_z
    classes[...] = jnp.zeros((128, 128), F32)
    for par in range(2):
        rows = dot(params[16:24, :], (chan == col * 16 + 2 * unit + par).astype(F32))
        value = jnp.zeros((HALF, 128), F32)
        for k in range(4):
            value = jnp.where(same_z & (half_k == k), rows[k : k + 1, :], value)
        classes[pl.ds(HALF * par, HALF), :] = value
    classes_t[...] = classes[...].T

    def arrived(block):
        for sx, sc in others:
            f_wait(block, sx, sc).wait_recv()
        own_piece(
            block, lambda copy: copy.wait(), lambda copy: copy.wait(), lambda copy: copy.wait_recv()
        )
        low, high = PIECES[block][0], sum(PIECES[block])

        @pl.loop(0, 2 * size)
        def _(t):
            for zp in range(low, high):
                pair = recv[t // 2, lax.rem(t, 2), zp].astype(F32)
                field[t, 2 * zp] = pair[0:8]
                field[t, 2 * zp + 1] = pair[8:16]

        between(seen(field), odd, 2 * low, 2 * high)

    def seen(ref):
        return lambda t, z: ref[t, z]

    def seen_rows(ref):
        return lambda t, z: ref[lax.rem(t, 2), spot(z, t // 2), :]

    def between(src, dst, low, high):
        partner = square_lane + 1 - 2 * lax.rem(square_lane, 2)
        swap = (square_row == partner).astype(F32).astype(BF16)

        @pl.loop(0, 2 * size, unroll=4)
        def _(t):
            after = lax.rem(t + 2, 2 * size)
            mixed = [jnp.where(x_even, src(after, z), src(t, z)) for z in range(low, high)]
            mixed = jnp.concatenate(mixed, axis=0).astype(BF16)
            swapped = jnp.dot(mixed, swap, preferred_element_type=F32)
            for z in range(low, high):
                dst[t, z] = swapped[8 * (z - low) : 8 * (z - low) + 8]

    def filtered(src, mid, t, low, count, flip, put):
        before, after = lax.rem(t + 2 * size - 2, 2 * size), lax.rem(t + 2, 2 * size)
        totals = [None] * count
        for z in range(count + 4):
            at = low + z - 2
            views = (src(before, at), mid[before, at], src(t, at), mid[t, at], src(after, at))
            for j in range(5):
                if 0 <= z - j < count:
                    for i in range(5):
                        q = 5 * (4 - i) + 4 - j if flip else 5 * i + j
                        term = taps[q] * views[i]
                        old = totals[z - j]
                        totals[z - j] = term if old is None else old + term
            if z >= 4:
                put(z - 4, totals)

    def spot(z, p):
        return pl.ds(pl.multiple_of((z * size + p) * 8, 8), 8)

    def unit_rows(z, count, cp):
        return pl.ds(z * size * 8 + cp, count * size, stride=8)

    def unit_of(ref, z, count, cp):
        at = unit_rows(z, count, cp)
        return jnp.concatenate([ref[0, at, :], ref[1, at, :]], axis=1).astype(BF16)

    def p_copy(block):
        return remote(
            part_out.at[block], part_in.at[block], p_send.at[block], p_recv.at[block],
            {"col": 1 - col},
        )

    def ahead_of(block):
        base = 2 + BLOCK * block

        @pl.loop(0, 2 * size)
        def _(t):
            def put(z, totals):
                smooth[lax.rem(t, 2), spot(base + z, t // 2), :] = rounded(totals[z])

            filtered(seen(field), odd, t, base, BLOCK, False, put)

        @pl.loop(0, 8, unroll=8)
        def _(cp):
            both = jnp.dot(
                unit_of(smooth, base, BLOCK, cp), wide[cp], preferred_element_type=F32
            )
            for yh in range(2):
                wall[yh, unit_rows(0, BLOCK, cp), :] = both[:, 128 * yh : 128 * yh + 128]

        @pl.loop(0, BLOCK)
        def _(z):
            at = pl.ds(pl.multiple_of(8 * z, 8), 8)
            for p in range(size):
                for yh in range(2):
                    value = wall[yh, spot(z, p), :]
                    sig = jax.nn.sigmoid(value)
                    lanes = slice(128 * yh, 128 * yh + 128)
                    hid[block, p, at, lanes] = value * sig
                    slope[block, p, at, lanes] = sig * (1.0 + value * (1.0 - sig))

        left_half = lax.rem(lax.broadcasted_iota(jnp.int32, (HALF, 256), 1), 128) < 64

        @pl.loop(0, size, unroll=size)
        def _(p):
            part = split_dot(classes[0:ROWS, 0:ROWS], hid[block, p])
            part_out[block, p] = jnp.where(left_half, part[0:HALF], part[HALF:ROWS])
            lanes = pl.ds(pl.multiple_of(128 * col, 128), 128)
            for zp in range(BLOCK // 2):
                at = slice(8 * zp, 8 * zp + 8)
                mark = lab_win[p, pl.ds(BLOCK // 2 * block + zp, 1), :]
                mark = jnp.broadcast_to(mark, (8, 128))
                mark = jnp.where(lax.rem(row, 2) == 0, mark, pltpu.roll(mark, 64, 1))
                hit = first & (mark == (row // 2).astype(F32))
                part_out[block, p, at, lanes] = part_out[block, p, at, lanes] - jnp.where(hit, 1.0, 0.0)

        p_copy(block).start()

    def back_of(block):
        base = 2 + BLOCK * block
        p_copy(block).wait_recv()
        left_half = lax.rem(lax.broadcasted_iota(jnp.int32, (HALF, 256), 1), 128) < 64

        @pl.loop(0, size, unroll=size)
        def _(p):
            err = part_out[block, p] + part_in[block, p]
            swapped = jnp.concatenate(
                [pltpu.roll(err[:, 0:128], 64, 1), pltpu.roll(err[:, 128:256], 64, 1)], axis=1
            )
            err = err + swapped
            both = jnp.concatenate(
                [jnp.where(left_half, err, 0.0), jnp.where(left_half, 0.0, err)], axis=0
            )
            grad = split_dot(classes_t[0:ROWS, 0:ROWS], both) * slope[block, p]
            for z in range(BLOCK):
                for yh in range(2):
                    gwall[yh, spot(base + z, p), :] = rounded(
                        grad[8 * z : 8 * z + 8, 128 * yh : 128 * yh + 128]
                    )
            new = cast_dot(both, hid[block, p], ((1,), (1,)))
            gram[block, p] = new

        @pl.loop(0, 8, unroll=8)
        def _(cp):
            both = jnp.dot(
                unit_of(gwall, base, BLOCK, cp), wide_t[cp], preferred_element_type=F32
            )
            for yh in range(2):
                at = unit_rows(base, BLOCK, cp)
                gsm[yh, at, :] = rounded(both[:, 128 * yh : 128 * yh + 128])

        between(seen_rows(gsm), godd, base, base + BLOCK)

    def g_spot(block):
        low = 4 if block == 0 else BLOCK * block
        return low, BLOCK * block + BLOCK - low

    def g_copy(back, step):
        at, many = RETURNS[back]
        p, yh = target(step // 2), lax.rem(col + step, 2)
        return remote(
            gout.at[2 * p + yh, pl.ds(at, many)],
            ghome.at[col, pl.ds(gx * zps + at, many)],
            g_send.at[back, step], g_recv.at[back, step], {"gx": p, "col": yh},
        )

    def g_near(back):
        at, many = RETURNS[back]
        return pltpu.make_async_copy(
            gout.at[2 * gx + col, pl.ds(at, many)],
            ghome.at[col, pl.ds(gx * zps + at, many)],
            g_recv.at[back, 0],
        )

    def g_wait(back, step):
        at, many = RETURNS[back]
        slot = ghome.at[col_at[step % 2], pl.ds(origin(step // 2) * zps + at, many)]
        return remote(
            slot, slot, g_send.at[back, step], g_recv.at[back, step],
            {"gx": target(step // 2), "col": col_at[step % 2]},
        )

    def home(block):
        low, count = g_spot(block)

        @pl.loop(0, 2 * size)
        def _(turn_at):
            step = lax.rem(turn_at + 4, 2 * size)
            t = 2 * target(step // 2) + lax.rem(col + step, 2)

            def put(z, totals):
                if z % 2:
                    pair = jnp.concatenate([totals[z - 1], totals[z]], axis=0)
                    gout[t, (low - 4 + z) // 2] = pair.astype(BF16)

            filtered(seen_rows(gsm), godd, t, low, count, True, put)

            @pl.when(step > 0)
            def _():
                g_copy(block, step).start()

            @pl.when(step == 0)
            def _():
                g_near(block).start()

    def labels_in():
        at_end = (gx == 0) | (gx == size - 1)
        for sx in range(size):
            if sx:
                at = lab_recv.at[origin(sx), pl.ds(0, 2)]
                remote(
                    at, at, l_send.at[0, sx], l_recv.at[0, sx], {"gx": target(sx)}
                ).wait_recv()

            @pl.when(at_end)
            def _(sx=sx):
                at = lab_recv.at[origin(sx), 2]
                remote(
                    at, at, l_send.at[1, sx], l_recv.at[1, sx], {"gx": target(sx), "gz": right}
                ).wait_recv()
                lab_wide[origin(sx), 2] = lab_recv[origin(sx), 2].astype(F32)

        l_own.wait()
        low_edge = 2 - (gx + size - 1) // size
        high_edge = 1 + (gx + 1) // size
        for p in range(size):
            lab_win[p, 1 : 1 + zps, :] = lab_recv[p, 0].astype(F32)
            lab_wide[p, 1] = lab_recv[p, 1].astype(F32)
            lab_win[p, 0:1, :] = lab_wide[p, low_edge, pl.ds(2 * gx, 1), :]
            lab_win[p, 1 + zps : 2 + zps, :] = lab_wide[p, high_edge, pl.ds(2 * gx + 1, 1), :]

    def next_piece(piece):
        for sx, sc in others:
            f_wait(piece - 1, sx, sc).wait_send()
        for ct in range(2):
            f_send_all(piece, ct)

    next_piece(1)
    arrived(0)
    labels_in()
    ahead_of(0)
    next_piece(2)
    arrived(1)
    ahead_of(1)
    back_of(0)
    home(0)
    arrived(2)
    ahead_of(2)
    back_of(1)
    home(1)
    back_of(2)
    home(2)

    def tile_body(it, sums25):
        t, base = it // 4, 4 + 8 * lax.rem(it, 4)
        before, after = lax.rem(t + 2 * size - 2, 2 * size), lax.rem(t + 2, 2 * size)
        grads = [seen_rows(gsm)(t, base + z) for z in range(8)]
        news = list(sums25)
        for z in range(12):
            at = base + z - 2
            views = (
                field[before, at], odd[before, at], field[t, at], odd[t, at], field[after, at]
            )
            for j in range(5):
                if 0 <= z - j < 8:
                    for i in range(5):
                        news[5 * i + j] = news[5 * i + j] + views[i] * grads[z - j]
        return tuple(news)

    sums25 = lax.fori_loop(
        0, 8 * size, tile_body, tuple(jnp.zeros((8, 128), F32) for q in range(25))
    )
    for q in range(25):
        acc[8 * q : 8 * q + 8, :] = sums25[q]

    @pl.loop(0, 8, unroll=8)
    def _(cp):
        grads, fields = unit_of(gwall, 4, OWN, cp), unit_of(smooth, 4, OWN, cp)
        both = cast_dot(grads, fields, ((0,), (0,)))
        for par in range(2):
            wall_acc[par, cp] = jnp.zeros((8, 128), F32)
        for yh in range(2):
            here, far = slice(128 * yh, 128 * yh + 128), slice(128 - 128 * yh, 256 - 128 * yh)
            for g in range(16):
                at = slice(128 * yh + 8 * g, 128 * yh + 8 * g + 8)
                tile = both[at, here] * band_tile[yh, 8 * g : 8 * g + 8, :]
                if g % 8 == (0 if yh else 7):
                    edge = both[at, far] * band_tile[2 + yh, 8 * g : 8 * g + 8, :]
                    tile = tile + pltpu.roll(edge, 64, 1)
                wall_acc[g // 8, cp] = wall_acc[g // 8, cp] + pltpu.roll(tile, (128 - 8 * g) % 128, 1)

    inner_row = lax.rem(lax.broadcasted_iota(jnp.int32, (64, 128), 0), 8)
    halves = lax.broadcasted_iota(jnp.int32, (128, 128), 0) // 64
    parity = lax.rem(lax.broadcasted_iota(jnp.int32, (128, 128), 1), 2)
    lines = dot(acc[...], (halves == parity).astype(F32))
    total = jnp.zeros((8, 128), F32)
    for q in range(25):
        total = jnp.where(lane // 2 == q, lines[8 * q : 8 * q + 8, :], total)

    full_row = lax.broadcasted_iota(jnp.int32, (ROWS, ROWS), 0)
    full_lane = lax.broadcasted_iota(jnp.int32, (ROWS, ROWS), 1)
    row_z = lax.rem(full_row, HALF) // 8 * 2 + lax.rem(full_row, 2)
    matrix = jnp.zeros((ROWS, ROWS), F32)
    for block in range(BLOCKS):
        base = 2 + BLOCK * block
        value = gram[block, 0]
        for p in range(1, size):
            value = value + gram[block, p]
        keep = (row_z == full_lane // 8) & (row_z + base >= 4) & (row_z + base < 4 + OWN)
        matrix = matrix + jnp.where(keep, value, 0.0)
    gather = (
        lax.broadcasted_iota(jnp.int32, (8, ROWS), 0)
        == lax.rem(lax.broadcasted_iota(jnp.int32, (8, ROWS), 1), 8)
    ).astype(F32)
    by_row = dot(gather, matrix, ((1,), (1,)))
    source_row = lax.broadcasted_iota(jnp.int32, (ROWS, 128), 0)
    place = 2 * (34 + lax.rem(source_row, 8) // 2) + source_row // HALF
    place = place == lax.broadcasted_iota(jnp.int32, (ROWS, 128), 1)
    total = total + dot(by_row, place.astype(F32))
    stack = (
        lax.broadcasted_iota(jnp.int32, (8, 64), 0)
        == lax.broadcasted_iota(jnp.int32, (8, 64), 1) // 8
    ).astype(F32)
    for par in range(2):
        value = wall_acc[par].reshape(64, 128)
        for r in range(1, 8):
            value = jnp.where(inner_row == r, pltpu.roll(value, 128 - r, 1), value)
        by_lane = dot(stack, value)
        source = lax.rem(square_row // 2 + 4, 64)
        place = (lax.rem(square_row, 2) == 0) & (source < 9) & (
            square_lane == 2 * (25 + source) + par
        )
        total = total + dot(by_lane, place.astype(F32))
    mine[...] = total

    def r_copy(n):
        return remote(mine, sums.at[me], r_send.at[n + 1], r_recv.at[n + 1], coords(*steps[n]))

    r_own = pltpu.make_async_copy(mine, sums.at[me], r_recv.at[0])
    r_own.start()

    for n in range(len(steps)):
        r_copy(n).start()

    for back in range(BLOCKS):
        for step in range(1, 2 * size):
            g_wait(back, step).wait_recv()
        g_near(back).wait()

    for n, (sx, sz, sc) in enumerate(steps):
        place = (origin(sx) * depth + gz_at[-sz % depth]) * 2 + col_at[sc]
        remote(
            sums.at[place], sums.at[place], r_send.at[n + 1], r_recv.at[n + 1], coords(sx, sz, sc)
        ).wait_recv()
    r_own.wait()
    for piece in (2,):
        for sx, sc in others:
            f_wait(piece, sx, sc).wait_send()
    pl.when(gx == 0)(lambda: f_copy(0, 0, col, edge_part(0)[0], 1).wait_send())
    pl.when(gx == size - 1)(lambda: f_copy(last, 0, col, edge_part(last)[0], -1).wait_send())
    for sx in range(size):
        if sx:
            l_copy(sx).wait_send()
        at_ends(sx, lambda copy: copy.wait_send())
    for block in range(BLOCKS):
        p_copy(block).wait_send()
    for back in range(BLOCKS):
        for step in range(1, 2 * size):
            g_copy(back, step).wait_send()

    for n in range(len(steps)):
        r_copy(n).wait_send()


def last_kernel(volume, home, sums, out, tile_out, wall_out, class_out, turn, red):
    members = sums.shape[0] // 2

    for side in range(2):
        @pl.loop(0, 64, unroll=8)
        def _(zp, side=side):
            at = pl.ds(pl.multiple_of(side * 1024 + zp * 16, 16), 16)
            turn[at, :] = home[side, zp].astype(F32)

    for cp in range(16):
        block = turn[pl.ds(cp // 8 * 1024 + cp % 8, 128, stride=8), :].T
        out[pl.ds(2 * cp, 2)] = block.reshape(2, 64, 128).astype(BF16)

    spot = lax.broadcasted_iota(jnp.int32, (128, 128), 0)
    want = 2 * lax.broadcasted_iota(jnp.int32, (128, 128), 1)
    red[...] = jnp.zeros((128, 128), F32)
    for half in range(2):
        total = sums[half]
        for member in range(1, members):
            total = total + sums[2 * member + half]
        total = total / volume
        for par in range(2):
            red[pl.ds(half * 16 + par, 8, stride=2), :] = dot(
                total, (spot == want + par).astype(F32)
            )
    turned = red[...].T
    tile_out[...] = red[0:32, 0:25]
    wall_out[...] = turned[25:34, 0:32]
    class_out[...] = turned[34:38, 0:32]


def regional(
    size, depth, volume,
    features, labels, grid_index, stretch, tile_filter, wall_filter, class_weight,
):
    chans = features.shape[0]
    levels = stretch.shape[0]
    everyone = size * depth * 2
    dma = pltpu.SemaphoreType.DMA
    far = pl.BlockSpec(memory_space=pl.ANY)
    wide = pltpu.VMEM((2 * size, WIN, 8, 128), F32)
    rows = pltpu.VMEM((2, WIN * size * 8, 128), F32)
    block = pltpu.VMEM((BLOCKS, size, ROWS, 256), F32)
    half = pltpu.VMEM((BLOCKS, size, HALF, 256), F32)
    home, sums = pl.pallas_call(
        functools.partial(region_kernel, (size, depth, volume)),
        out_shape=(
            jax.ShapeDtypeStruct((2, 64, 16, 128), BF16),
            jax.ShapeDtypeStruct((everyone, 8, 128), F32),
        ),
        in_specs=[far] * 7,
        out_specs=(far, far),
        scratch_shapes=[
            pltpu.VMEM((chans, 64, 128), BF16),
            pltpu.VMEM((128, 128), jnp.int32),
            pltpu.VMEM((1, 64), jnp.int32),
            pltpu.VMEM((levels, 9), F32),
            pltpu.VMEM((chans, 25), F32),
            pltpu.VMEM((9, chans), F32),
            pltpu.VMEM((4, chans), F32),
            pltpu.VMEM((3, 1024, 128), F32),
            pltpu.VMEM((2, 64, 16, 128), BF16),
            pltpu.VMEM((size, 2, WIN // 2, 16, 128), BF16),
            pltpu.VMEM((64, 128), F32),
            pltpu.VMEM((size, 2, 16, 128), BF16),
            pltpu.VMEM((size, 3, 16, 128), BF16),
            pltpu.VMEM((size, 3, 16, 128), F32),
            pltpu.VMEM((size, 24, 128), F32),
            wide, wide, rows, rows, rows, wide,
            block, block, half, half,
            pltpu.VMEM((25, 8, 128), F32),
            pltpu.VMEM((9, 4, 8, 128), F32),
            pltpu.VMEM((8, 256, 256), BF16),
            pltpu.VMEM((8, 256, 256), BF16),
            pltpu.VMEM((4, 128, 128), F32),
            pltpu.VMEM((2, ROWS * size, 128), F32),
            pltpu.VMEM((2, 8, 8, 128), F32),
            pltpu.VMEM((25 * 8, 128), F32),
            pltpu.VMEM((BLOCKS, size, ROWS, ROWS), F32),
            pltpu.VMEM((128, 128), F32),
            pltpu.VMEM((128, 128), F32),
            pltpu.VMEM((128, 128), F32),
            pltpu.VMEM((2 * size, OWN // 2, 16, 128), BF16),
            pltpu.VMEM((8, 128), F32),
            pltpu.VMEM((128, 128), F32),
            dma((8,)), dma((4,)),
            dma((len(PIECES), size, 2)), dma((len(PIECES), size, 2)),
            dma((2, size)), dma((2, size)),
            dma((BLOCKS,)), dma((BLOCKS,)),
            dma((BLOCKS, 2 * size)), dma((BLOCKS, 2 * size)),
            dma((everyone,)), dma((everyone,)),
        ],
        compiler_params=pltpu.CompilerParams(
            collective_id=0, has_side_effects=True, vmem_limit_bytes=63 * 1024 * 1024
        ),
    )(
        features.reshape(chans, 64, 128), labels.reshape(128, 128), grid_index.reshape(1, 64),
        stretch, tile_filter, wall_filter.T, class_weight,
    )
    def whole(*shape):
        return pl.BlockSpec(shape, lambda: (0,) * len(shape))

    grad, tile_grad, wall_grad, class_grad = pl.pallas_call(
        functools.partial(last_kernel, volume),
        out_shape=(
            jax.ShapeDtypeStruct((chans, 64, 128), BF16),
            jax.ShapeDtypeStruct((chans, 25), F32),
            jax.ShapeDtypeStruct((9, chans), F32),
            jax.ShapeDtypeStruct((4, chans), F32),
        ),
        in_specs=[
            whole(2, 64, 16, 128),
            whole(everyone, 8, 128),
        ],
        out_specs=(
            whole(chans, 64, 128),
            whole(chans, 25), whole(9, chans), whole(4, chans),
        ),
        scratch_shapes=[pltpu.VMEM((2048, 128), F32), pltpu.VMEM((128, 128), F32)],
    )(home, sums)
    return grad.reshape(features.shape), tile_grad, wall_grad.T, class_grad


def shards(features, labels, grid_index, stretch, tile_filter, wall_filter, class_weight):
    chans, rows, cells_x, cells_z = features.shape
    size, depth = lax.axis_size("gx"), lax.axis_size("gz")
    volume = labels.shape[0] * cells_x * size * cells_z * depth
    cpg = chans // size
    if 128 // size == OWN:
        return regional(
            size, depth, volume,
            features, labels, grid_index, stretch, tile_filter, wall_filter, class_weight,
        )
    chunks = min(4, cpg)
    per_dest = max(cpg // 4, 1) * 8
    xs = 2 * size
    everyone = size * depth * 2
    onehot = (grid_index[:, None] == jnp.arange(stretch.shape[0], dtype=jnp.int32)).astype(F32)
    bands = jnp.dot(onehot, stretch, precision=lax.Precision.HIGHEST)
    dma = pltpu.SemaphoreType.DMA
    vmem = pl.BlockSpec(memory_space=pltpu.VMEM)
    smem = pl.BlockSpec(memory_space=pltpu.SMEM)
    grad, tile_grad, wall_grad, class_grad = pl.pallas_call(
        functools.partial(kernel, (size, depth, cpg, chunks, volume)),
        out_shape=(
            jax.ShapeDtypeStruct((chans, 64, 128), BF16),
            jax.ShapeDtypeStruct((chans, 25), F32),
            jax.ShapeDtypeStruct((9, chans), F32),
            jax.ShapeDtypeStruct((4, chans), F32),
        ),
        in_specs=[vmem, vmem, vmem, smem, smem, smem],
        out_specs=(vmem, vmem, vmem, vmem),
        scratch_shapes=[
            pltpu.VMEM((size, cpg, 64, 128), BF16),
            pltpu.VMEM((80, 9), F32),
            pltpu.VMEM((size, per_dest, 128), F32),
            pltpu.VMEM((2, size, per_dest, 128), F32),
            pltpu.VMEM((5, cpg, xs, 32, 128), F32),
            pltpu.VMEM((cpg, xs, 48, 128), F32),
            pltpu.VMEM((max(cpg, size), 64, 128), F32),
            pltpu.VMEM((cpg, 9, 48, 128), F32),
            pltpu.VMEM((9, 48, 128), F32),
            pltpu.VMEM((cpg, xs, 32, 128), F32),
            pltpu.VMEM((cpg, xs, 32, 128), F32),
            pltpu.VMEM((256, 128), F32),
            pltpu.VMEM((size, 256, 128), BF16),
            pltpu.VMEM((size, 256, 128), BF16),
            pltpu.VMEM((size, 256, 128), BF16),
            pltpu.VMEM((cpg, xs, 48, 128), F32),
            pltpu.VMEM((cpg, xs, 32, 128), F32),
            pltpu.VMEM((cpg, xs // 8, 8, 128), F32),
            pltpu.VMEM((2, cpg, xs // 8, 8, 128), F32),
            pltpu.VMEM((5, cpg, xs, 32, 128), F32),
            pltpu.VMEM((size, cpg, 64, 128), BF16),
            pltpu.VMEM((size, 64, 128), F32),
            pltpu.VMEM((cpg, 40, 8, 128), F32),
            pltpu.VMEM((128, 128), F32),
            pltpu.VMEM((everyone, 8, 128), F32),
            dma((chunks, size)), dma((chunks, size)), dma(()),
            dma((2, size)), dma((2, size)),
            dma((cpg,)), dma((cpg,)),
            dma((size,)), dma((size,)),
            dma((size,)), dma((size,)),
            dma((size,)), dma((size,)),
            dma((2, cpg)), dma((2, cpg)),
            dma((chunks, size)), dma((chunks, size)),
            dma((everyone,)), dma((everyone,)),
        ],
        compiler_params=pltpu.CompilerParams(
            collective_id=0, has_side_effects=True, vmem_limit_bytes=48 * 1024 * 1024
        ),
    )(
        features.reshape(chans, 64, 128), labels.reshape(128, 128), bands,
        tile_filter, wall_filter.T, class_weight,
    )
    return grad.reshape(features.shape), tile_grad, wall_grad.T, class_grad


def solution(mesh):
    return jax.shard_map(
        shards,
        mesh=mesh,
        in_specs=(
            P(None, "col", ("group", "gx"), "gz"),
            P(None, ("group", "gx"), "gz"),
            P(),
            P(),
            P(),
            P(),
            P(),
        ),
        out_specs=(
            P(None, "col", ("group", "gx"), "gz"),
            P("group", None),
            P("group", None),
            P("group", None),
        ),
        check_vma=False,
    )
```

```python
import functools

import jax
import jax.numpy as jnp
from jax import lax
from jax.experimental import pallas as pl
from jax.experimental.pallas import tpu as pltpu
from jax.sharding import PartitionSpec as P

F32 = jnp.float32
BF16 = jnp.bfloat16
MESH = pl.DeviceIdType.MESH


def fold(value):
    total = value[0:8]
    for row in range(8, value.shape[0], 8):
        total = total + value[row : row + 8]
    return total


def rounded(value):
    return value.astype(BF16).astype(F32)


def kernel(
    dims,
    feat, labels, bands, tile_w, wall_w, class_w,
    out, tile_out, wall_out, class_out,
    recv, band_pad, halo_out, halo_in, zfeat, smooth, stage, taps, band_rows, hid, slope,
    part_own, part_out, part_in, err, gwall, gsm, ghalo_out, ghalo_in, zgrad, gout, gstage,
    acc, red, sums,
    a_send, a_recv, own_sem, h_send, h_recv, s_send, s_recv, p_send, p_recv, e_send, e_recv,
    w_send, w_recv, g_send, g_recv, o_send, o_recv, r_send, r_recv,
):
    size, depth, cpg, chunks, volume = dims
    per = cpg // chunks
    xs = 2 * size
    xgroups = xs // 8
    everyone = size * depth * 2
    gx, gz, col = lax.axis_index("gx"), lax.axis_index("gz"), lax.axis_index("col")
    me = (gx * depth + gz) * 2 + col
    other = 1 - col
    right, left = lax.rem(gz + 1, depth), lax.rem(gz + depth - 1, depth)
    chan0 = gx * cpg

    def peer(step):
        return lax.rem(gx + step, size)

    def source(step):
        return lax.rem(gx + size - step, size)

    def coords(step):
        index = lax.rem(me + step, everyone)
        return {
            "gx": index // (2 * depth),
            "gz": lax.rem(index // 2, depth),
            "col": lax.rem(index, 2),
        }

    barrier = pltpu.get_barrier_semaphore()

    @pl.loop(1, everyone)
    def _(step):
        pl.semaphore_signal(barrier, inc=1, device_id=coords(step), device_id_type=MESH)

    pl.semaphore_wait(barrier, everyone - 1)

    def remote(src, dst, send, rec, device):
        return pltpu.make_async_remote_copy(
            src_ref=src, dst_ref=dst, send_sem=send, recv_sem=rec,
            device_id=device, device_id_type=MESH,
        )

    def a_copy(chunk, step):
        return remote(
            feat.at[pl.ds(peer(step) * cpg + chunk * per, per)],
            recv.at[step, pl.ds(chunk * per, per)],
            a_send.at[chunk, step], a_recv.at[chunk, step], {"gx": peer(step)},
        )

    def h_copy(way, step):
        return remote(
            halo_out.at[peer(step)], halo_in.at[way, step],
            h_send.at[way, step], h_recv.at[way, step],
            {"gx": peer(step), "gz": right if way == 0 else left},
        )

    own_copy = pltpu.make_async_copy(feat.at[pl.ds(chan0, cpg)], recv.at[0], own_sem)
    own_copy.start()
    for step in range(1, size):
        a_copy(0, step).start()

    lane = lax.broadcasted_iota(jnp.int32, (8, 128), 1)
    quad = lane // 4

    @pl.loop(0, size)
    def _(group):
        for first in range(0, cpg, 4):
            packed = jnp.zeros((8, 128), F32)
            for c in range(first, min(first + 4, cpg)):
                stage[c] = feat[group * cpg + c].astype(F32)
                for xl in range(2):
                    rows = stage[c, pl.ds(xl, 32, stride=2), :]
                    for t in range(4):
                        m = (c - first) * 8 + xl * 4 + t
                        turned = pltpu.roll(rows[8 * t : 8 * t + 8], (2 + 4 * m) % 128, 1)
                        packed = jnp.where(quad == m, turned, packed)
            halo_out[group, pl.ds(first // 4 * 8, 8), :] = packed

    for way in range(2):
        for step in range(size):
            h_copy(way, step).start()
    for chunk in range(1, chunks):
        for step in range(1, size):
            a_copy(chunk, step).start()

    band_pad[0:8] = jnp.zeros((8, 9), F32)
    band_pad[8:72] = bands[...]
    band_pad[72:80] = jnp.zeros((8, 9), F32)
    for k in range(9):
        band_rows[k] = jnp.broadcast_to(band_pad[pl.ds(32 * col, 48), k : k + 1], (48, 128))

    @pl.loop(0, cpg)
    def _(c):
        for k in range(9):
            taps[c, k] = wall_w[k, chan0 + c] * band_rows[k]
        for x_group in range(0, xs, 8):
            blank = jnp.zeros((8, 8, 128), F32)
            smooth[c, pl.ds(x_group, 8), pl.ds(pl.multiple_of(40 * col, 8), 8), :] = blank
            gwall[c, pl.ds(x_group, 8), pl.ds(pl.multiple_of(40 * col, 8), 8), :] = blank
        for q in range(40):
            acc[c, q] = jnp.zeros((8, 128), F32)

    red[...] = jnp.zeros((128, 128), F32)

    def shifts(value, edge):
        return (
            pltpu.roll(jnp.where(lane >= 126, edge, value), 2, 1),
            pltpu.roll(jnp.where(lane == 127, edge, value), 1, 1),
            value,
            pltpu.roll(jnp.where(lane == 0, edge, value), 127, 1),
            pltpu.roll(jnp.where(lane < 2, edge, value), 126, 1),
        )

    def filtered(field, c, x, flip):
        total = None
        for i in range(5):
            at = lax.rem(x + (4 - i if flip else i) - 2 + xs, xs)
            for j in range(5):
                term = tile_w[chan0 + c, 5 * i + j] * field[4 - j if flip else j, c, at]
                total = term if total is None else total + term
        return total

    def y_copy(ref, index, send, rec):
        src = pl.multiple_of(32 - 24 * col, 8)
        dst = pl.multiple_of(40 * col, 8)
        return remote(
            ref.at[index + (pl.ds(src, 8),)], ref.at[index + (pl.ds(dst, 8),)],
            send, rec, {"col": other},
        )

    def s_copy(c):
        return y_copy(smooth, (c, pl.ds(0, xs)), s_send.at[c], s_recv.at[c])

    own_copy.wait()
    for way in range(2):
        for step in range(size):
            h_copy(way, step).wait_recv()

    def edges_of(ref_left, ref_right):
        return jnp.where(lax.rem(lane, 4) < 2, ref_left, ref_right)

    for chunk in range(chunks):
        for step in range(1, size):
            a_copy(chunk, step).wait_recv()
        for c in range(chunk * per, chunk * per + per):

            @pl.loop(0, size, unroll=2)
            def _(step, c=c):
                s = source(step)
                stage[step] = recv[step, c].astype(F32)
                at = pl.ds(c // 4 * 8, 8)
                packed = edges_of(halo_in[0, step, at, :], halo_in[1, step, at, :])
                for xl in range(2):
                    rows = stage[step, pl.ds(xl, 32, stride=2), :]
                    for t in range(4):
                        m = c % 4 * 8 + xl * 4 + t
                        edge = pltpu.roll(packed, (126 - 4 * m) % 128, 1)
                        moved = shifts(rows[8 * t : 8 * t + 8], edge)
                        for j in range(5):
                            zfeat[j, c, 2 * s + xl, pl.ds(8 * t, 8), :] = moved[j]

            @pl.loop(0, xs, unroll=4)
            def _(x, c=c):
                smooth[c, x, pl.ds(8, 32), :] = rounded(filtered(zfeat, c, x, False))

            s_copy(c).start()

    for c in range(cpg):
        s_copy(c).wait_recv()

    def p_copy(step):
        return remote(
            part_out.at[step], part_in.at[step], p_send.at[step], p_recv.at[step],
            {"gx": peer(step)},
        )

    def scores_at(x):
        def body(c, totals):
            wall = None
            for k in range(9):
                term = taps[c, k, pl.ds(8, 32), :] * smooth[c, x, pl.ds(4 + k, 32), :]
                wall = term if wall is None else wall + term
            sig = jax.nn.sigmoid(wall)
            hidden = wall * sig
            hid[c, x] = hidden
            slope[c, x] = sig * (1.0 + wall * (1.0 - sig))
            return tuple(
                total + class_w[k, chan0 + c] * hidden for k, total in enumerate(totals)
            )

        return lax.fori_loop(
            0, cpg, body, tuple(jnp.zeros((32, 128), F32) for k in range(4)), unroll=min(4, cpg)
        )

    @pl.loop(1, size)
    def _(step):
        for xl in range(2):
            totals = scores_at(2 * peer(step) + xl)
            for k in range(4):
                part_out[step, pl.ds((2 * k + xl) * 32, 32), :] = totals[k].astype(BF16)
        p_copy(step).start()

    for xl in range(2):
        totals = scores_at(2 * gx + xl)
        for k in range(4):
            part_own[pl.ds((2 * k + xl) * 32, 32), :] = totals[k]

    @pl.loop(1, size)
    def _(step):
        p_copy(step).wait_recv()
        part_own[...] = part_own[...] + part_in[step].astype(F32)

    for xl in range(2):
        marks = labels[pl.ds(64 * col + xl, 32, stride=2), :]
        for k in range(4):
            at = pl.ds((2 * k + xl) * 32, 32)
            err[0, at, :] = (part_own[at, :] - jnp.where(marks == k, 1.0, 0.0)).astype(BF16)

    def e_copy(step):
        return remote(
            err.at[0], err.at[step], e_send.at[step], e_recv.at[step], {"gx": peer(step)}
        )

    for step in range(1, size):
        e_copy(step).start()

    def w_copy(step):
        return y_copy(
            gwall, (pl.ds(0, cpg), pl.ds(2 * source(step), 2)), w_send.at[step], w_recv.at[step]
        )

    def wall_grads(step):
        for xl in range(2):
            x = 2 * source(step) + xl
            errors = [err[step, pl.ds((2 * k + xl) * 32, 32), :].astype(F32) for k in range(4)]

            @pl.loop(0, cpg, unroll=min(4, cpg))
            def _(c):
                hidden = hid[c, x]
                grad = None
                for k in range(4):
                    term = class_w[k, chan0 + c] * errors[k]
                    grad = term if grad is None else grad + term
                    acc[c, 34 + k] = acc[c, 34 + k] + fold(errors[k] * hidden)
                gwall[c, x, pl.ds(8, 32), :] = rounded(grad * slope[c, x])

        w_copy(step).start()

    wall_grads(0)

    @pl.loop(1, size)
    def _(step):
        e_copy(step).wait_recv()
        wall_grads(step)

    @pl.loop(0, size)
    def _(step):
        w_copy(step).wait_recv()

    def g_copy(way, c):
        return remote(
            ghalo_out.at[c], ghalo_in.at[way, c], g_send.at[way, c], g_recv.at[way, c],
            {"gz": right if way == 0 else left},
        )

    @pl.loop(0, cpg)
    def _(c):
        def body(x, sums9):
            grad = gwall[c, x, pl.ds(8, 32), :]
            total = None
            news = []
            for k in range(9):
                term = taps[c, k, pl.ds(12 - k, 32), :] * gwall[c, x, pl.ds(12 - k, 32), :]
                total = term if total is None else total + term
                product = grad * band_rows[k, pl.ds(8, 32), :] * smooth[c, x, pl.ds(4 + k, 32), :]
                news.append(sums9[k] + fold(product))
            gsm[c, x] = rounded(total)
            return tuple(news)

        sums9 = lax.fori_loop(0, xs, body, tuple(jnp.zeros((8, 128), F32) for k in range(9)), unroll=2)
        for k in range(9):
            acc[c, 25 + k] = sums9[k]

        @pl.loop(0, xgroups)
        def _(group):
            packed = jnp.zeros((8, 128), F32)
            for m in range(32):
                piece = gsm[c, group * 8 + m // 4, pl.ds(m % 4 * 8, 8), :]
                packed = jnp.where(quad == m, pltpu.roll(piece, (2 + 4 * m) % 128, 1), packed)
            ghalo_out[c, group] = packed

        for way in range(2):
            g_copy(way, c).start()

    def o_copy(chunk, step):
        return remote(
            gout.at[peer(step), pl.ds(chunk * per, per)],
            out.at[pl.ds(chan0 + chunk * per, per)],
            o_send.at[chunk, step], o_recv.at[chunk, step], {"gx": peer(step)},
        )

    @pl.loop(0, chunks)
    def _(chunk):
        @pl.loop(0, per)
        def _(lower):
            c = chunk * per + lower
            for way in range(2):
                g_copy(way, c).wait_recv()

            @pl.loop(0, xgroups)
            def _(group):
                packed = edges_of(ghalo_in[0, c, group], ghalo_in[1, c, group])
                for m in range(32):
                    at = pl.ds(m % 4 * 8, 8)
                    x = group * 8 + m // 4
                    edge = pltpu.roll(packed, (126 - 4 * m) % 128, 1)
                    moved = shifts(gsm[c, x, at, :], edge)
                    for j in range(5):
                        zgrad[j, c, x, at, :] = moved[j]

            @pl.loop(0, size, unroll=2)
            def _(s):
                for xl in range(2):
                    gstage[s, pl.ds(xl, 32, stride=2), :] = filtered(zgrad, c, 2 * s + xl, True)
                gout[s, c] = gstage[s].astype(BF16)

            out[chan0 + c] = gout[gx, c]

        for step in range(1, size):
            o_copy(chunk, step).start()

    row = lax.broadcasted_iota(jnp.int32, (8, 128), 0)

    @pl.loop(0, cpg)
    def _(c):
        def body(x, sums25):
            grad = gsm[c, x]
            news = []
            for i in range(5):
                at = lax.rem(x + i - 2 + xs, xs)
                for j in range(5):
                    news.append(sums25[5 * i + j] + fold(zfeat[j, c, at] * grad))
            return tuple(news)

        sums25 = lax.fori_loop(0, xs, body, tuple(jnp.zeros((8, 128), F32) for q in range(25)), unroll=2)
        for q in range(38):
            value = sums25[q] if q < 25 else acc[c, q]
            red[pl.ds(q, 1), :] = jnp.sum(value, axis=0, keepdims=True)
        line = lax.dot_general(
            jnp.ones((8, 128), F32), red[...], (((1,), (1,)), ((), ())),
            precision=lax.Precision.HIGHEST, preferred_element_type=F32,
        )
        before = jnp.where(c == 0, jnp.zeros((8, 128), F32), sums[me])
        sums[me] = jnp.where(row == c, line, before)

    def r_copy(step):
        return remote(sums.at[me], sums.at[me], r_send.at[step], r_recv.at[step], coords(step))

    @pl.loop(1, everyone)
    def _(step):
        r_copy(step).start()

    @pl.loop(1, everyone)
    def _(step):
        r_copy(step).wait_recv()

    @pl.loop(0, size)
    def _(group):
        total = sums[group * depth * 2]
        for member in range(1, depth * 2):
            total = total + sums[group * depth * 2 + member]
        red[pl.ds(group * cpg, cpg), :] = total[0:cpg] / volume

    turned = red[...].T
    chans = size * cpg
    tile_out[...] = red[0:chans, 0:25]
    wall_out[...] = turned[25:34, 0:chans]
    class_out[...] = turned[34:38, 0:chans]

    for chunk in range(chunks):
        for step in range(1, size):
            o_copy(chunk, step).wait()
            a_copy(chunk, step).wait_send()
    for way in range(2):
        for step in range(size):
            h_copy(way, step).wait_send()
        for c in range(cpg):
            g_copy(way, c).wait_send()
    for c in range(cpg):
        s_copy(c).wait_send()
    for step in range(1, size):
        p_copy(step).wait_send()
        e_copy(step).wait_send()
    for step in range(size):
        w_copy(step).wait_send()

    @pl.loop(1, everyone)
    def _(step):
        r_copy(step).wait_send()


OWN = 32
WIN = OWN + 8
BLOCK = 12
BLOCKS = (WIN - 4) // BLOCK
ROWS = BLOCK * 8
HALF = ROWS // 2
PIECES = ((0, 8), (8, 6), (14, 6))
RETURNS = ((0, 4), (4, 6), (10, 6))
WANTED = 38
HIGH = lax.Precision.HIGHEST


def cast_dot(a, b, dims=((1,), (0,))):
    return lax.dot_general(
        a.astype(BF16), b.astype(BF16), (dims, ((), ())), preferred_element_type=F32
    )


def split_dot(a, b):
    a_high, b_high = a.astype(BF16), b.astype(BF16)
    a_low, b_low = (a - a_high.astype(F32)).astype(BF16), (b - b_high.astype(F32)).astype(BF16)
    return cast_dot(a_high, b_high) + (cast_dot(a_high, b_low) + cast_dot(a_low, b_high))


def dot(a, b, dims=((1,), (0,))):
    return lax.dot_general(a, b, (dims, ((), ())), precision=HIGH, preferred_element_type=F32)


def region_kernel(
    dims,
    feat_h, lab_h, index_h, stretch_h, tile_h, wall_h, class_h,
    ghome, sums,
    feat, lab, index, stretch, tile_w, wall_w, class_w,
    turn, send, recv, lab_rows, lab_send, lab_recv, lab_wide, lab_win,
    field, odd, smooth, gwall, gsm, godd, hid, slope, part_out, part_in,
    taps, fore, wide, wide_t, band_tile, wall, wall_acc, acc, gram, params, classes, classes_t,
    gout, mine, red,
    in_sem, own_sem, f_send, f_recv, l_send, l_recv, p_send, p_recv, g_send, g_recv, r_send, r_recv,
):
    size, depth, volume = dims
    everyone = size * depth * 2
    gx, gz, col = lax.axis_index("gx"), lax.axis_index("gz"), lax.axis_index("col")
    me = (gx * depth + gz) * 2 + col
    right, left = lax.rem(gz + 1, depth), lax.rem(gz + depth - 1, depth)
    zps = OWN // 2
    lane = lax.broadcasted_iota(jnp.int32, (8, 128), 1)
    row = lax.broadcasted_iota(jnp.int32, (8, 128), 0)
    first = lane < 64
    y_lane = lax.rem(lane, 64) // 2
    x_even = lax.rem(lane, 2) == 0

    ins = [
        pltpu.make_async_copy(src, dst, in_sem.at[n])
        for n, (src, dst) in enumerate((
            (feat_h.at[pl.ds(0, 16)], feat.at[pl.ds(0, 16)]),
            (feat_h.at[pl.ds(16, 16)], feat.at[pl.ds(16, 16)]),
            (lab_h, lab), (index_h, index), (stretch_h, stretch),
            (tile_h, tile_w), (wall_h, wall_w), (class_h, class_w),
        ))
    ]
    for copy in ins:
        copy.start()

    gx_at = [lax.rem(gx + n, size) for n in range(size)]
    gz_at = [lax.rem(gz + n, depth) for n in range(depth)]
    col_at = [col, 1 - col]
    steps = [
        (sx, sz, sc)
        for sx in range(size) for sz in range(depth) for sc in range(2) if sx or sz or sc
    ]

    def coords(sx, sz, sc):
        return {"gx": gx_at[sx], "gz": gz_at[sz], "col": col_at[sc]}

    barrier = pltpu.get_barrier_semaphore()
    for step in steps:
        pl.semaphore_signal(barrier, inc=1, device_id=coords(*step), device_id_type=MESH)

    def remote(src, dst, sent, got, device):
        return pltpu.make_async_remote_copy(
            src_ref=src, dst_ref=dst, send_sem=sent, recv_sem=got,
            device_id=device, device_id_type=MESH,
        )

    def target(sx):
        return gx_at[sx] if isinstance(sx, int) else lax.rem(gx + sx, size)

    def origin(sx):
        return gx_at[-sx % size]

    def turned_features(side):
        ins[side].wait()
        for cp in range(8):
            block = feat[pl.ds(side * 16 + 2 * cp, 2)].astype(F32).reshape(128, 128)
            turn[side, pl.ds(cp, 128, stride=8), :] = block.T

        @pl.loop(0, 64, unroll=8)
        def _(zp):
            at = pl.ds(pl.multiple_of(zp * 16, 16), 16)
            send[side, zp] = turn[side, at, :].astype(BF16)

    last = len(PIECES) - 1

    def f_copy(piece, sx, ct, part, way):
        t, sc = target(sx), col_at[ct] if isinstance(ct, int) else 0
        at, count = part
        return remote(
            send.at[ct, pl.ds(lax.rem(t * zps + at - 2 + 64, 64), count)],
            recv.at[gx, col, pl.ds(at, count)],
            f_send.at[piece, sx, sc], f_recv.at[piece, sx, sc],
            {"gx": t, "gz": gz_at[way % depth], "col": ct},
        )

    def edge_part(piece):
        at, count = PIECES[piece]
        return ((at, 2), (at + 2, count - 2)) if piece == 0 else (
            (at + count - 2, 2), (at, count - 2)
        )

    def f_start(piece, sx, ct):
        t = target(sx)
        if 0 < piece < last:
            f_copy(piece, sx, ct, PIECES[piece], 0).start()
            return
        end, way = (0, 1) if piece == 0 else (size - 1, -1)
        far, near = edge_part(piece)

        @pl.when(t != end)
        def _():
            f_copy(piece, sx, ct, PIECES[piece], 0).start()

        @pl.when(t == end)
        def _():
            f_copy(piece, sx, ct, near, 0).start()
            f_copy(piece, sx, ct, far, way).start()

    def f_own(piece, part):
        at, count = part
        return pltpu.make_async_copy(
            send.at[col, pl.ds(lax.rem(gx * zps + at - 2 + 64, 64), count)],
            recv.at[gx, col, pl.ds(at, count)], own_sem.at[piece],
        )

    def own_piece(piece, whole_one, near_one, far_one):
        if 0 < piece < last:
            whole_one(f_own(piece, PIECES[piece]))
            return
        end, way = (0, 1) if piece == 0 else (size - 1, -1)
        far, near = edge_part(piece)

        @pl.when(gx != end)
        def _():
            whole_one(f_own(piece, PIECES[piece]))

        @pl.when(gx == end)
        def _():
            near_one(f_own(piece, near))
            far_one(f_copy(piece, 0, col, far, way))

    def begin(copy):
        copy.start()

    def f_send_all(piece, ct):
        for sx in (2, 1, 3):
            f_start(piece, sx, ct)

        @pl.when(col != ct)
        def _():
            f_start(piece, 0, ct)

        @pl.when(col == ct)
        def _():
            own_piece(piece, begin, begin, begin)

    others = [(sx, sc) for sx in (2, 1, 3, 0) for sc in range(2) if sx or sc]

    def f_wait(piece, sx, sc):
        slot = recv.at[origin(sx), col_at[sc], pl.ds(*PIECES[piece])]
        return remote(
            slot, slot, f_send.at[piece, sx, sc], f_recv.at[piece, sx, sc],
            {"gx": target(sx), "gz": gz, "col": col_at[sc]},
        )

    turned_features(0)
    pl.semaphore_wait(barrier, everyone - 1)
    f_send_all(0, 0)
    turned_features(1)
    f_send_all(0, 1)

    ins[2].wait()
    turn[2, 0:128, :] = lab[...].astype(F32).T
    even, uneven = turn[2, pl.ds(0, 64, stride=2), :], turn[2, pl.ds(1, 64, stride=2), :]
    here = jnp.where(col == 0, even, pltpu.roll(even, 64, 1))
    there = jnp.where(col == 0, pltpu.roll(uneven, 64, 1), uneven)
    lab_rows[...] = jnp.where(lax.broadcasted_iota(jnp.int32, (64, 128), 1) < 64, here, there)
    edge_rows = [jnp.zeros((1, 128), F32)] * 16
    for t in range(size):
        edge_rows[2 * t] = lab_rows[pl.ds((zps * t - 1) % 64, 1), :]
        edge_rows[2 * t + 1] = lab_rows[pl.ds((zps * t + zps) % 64, 1), :]
    edge_rows = jnp.concatenate(edge_rows, axis=0).astype(BF16)
    for t in range(size):
        lab_send[t, 0] = lab_rows[pl.ds(zps * t, zps), :].astype(BF16)
        lab_send[t, 1] = edge_rows

    def l_copy(sx):
        return remote(
            lab_send.at[target(sx)], lab_recv.at[gx, pl.ds(0, 2)],
            l_send.at[0, sx], l_recv.at[0, sx], {"gx": target(sx)},
        )

    def l_far(sx, way):
        return remote(
            lab_send.at[target(sx), 1], lab_recv.at[gx, 2], l_send.at[1, sx], l_recv.at[1, sx],
            {"gx": target(sx), "gz": gz_at[way % depth]},
        )

    l_own = pltpu.make_async_copy(lab_send.at[gx], lab_recv.at[gx, pl.ds(0, 2)], own_sem.at[3])
    l_own.start()

    def at_ends(sx, act):
        @pl.when(target(sx) == 0)
        def _():
            act(l_far(sx, 1))

        @pl.when(target(sx) == size - 1)
        def _():
            act(l_far(sx, -1))

    for sx in range(size):
        if sx:
            l_copy(sx).start()
        at_ends(sx, begin)

    for copy in ins[3:]:
        copy.wait()
    params[...] = jnp.zeros((128, 128), F32)
    params[0:9, 0:32] = wall_w[...]
    params[16:20, 0:32] = class_w[...]
    params[64:96, 0:25] = tile_w[...]
    red[...] = params[...].T

    def pairs(ref, start):
        return ref[pl.ds(start + col * 16, 8, stride=2), :], ref[pl.ds(start + col * 16 + 1, 8, stride=2), :]

    def spread(both, q):
        low, high = (jnp.broadcast_to(rows[:, q : q + 1], (8, 128)) for rows in both)
        return jnp.where(first, low, high)

    tile_pairs, wall_pairs = pairs(params, 64), pairs(red, 0)
    for q in range(25):
        taps[q] = spread(tile_pairs, q)

    levels = stretch.shape[0]
    hot = lax.broadcasted_iota(jnp.int32, (levels, 64), 0) == index[...]
    params[32:41, 0:64] = dot(stretch[...], hot.astype(F32), ((0,), (0,)))
    band_t = params[32:48, 0:64]
    y_row = lax.broadcasted_iota(jnp.int32, (64, 128), 0)
    y_col = lax.rem(lax.broadcasted_iota(jnp.int32, (64, 128), 1), 64) // 2
    square_row = lax.broadcasted_iota(jnp.int32, (128, 128), 0)
    square_lane = lax.broadcasted_iota(jnp.int32, (128, 128), 1)
    k_of_lane = lax.rem(lax.broadcasted_iota(jnp.int32, (16, 128), 1) // 2 + 4, 64)
    k_of_lane = (k_of_lane == lax.broadcasted_iota(jnp.int32, (16, 128), 0)) & (
        lax.rem(lax.broadcasted_iota(jnp.int32, (16, 128), 1), 2) == 0
    )
    placed = dot(band_t, k_of_lane.astype(F32), ((0,), (0,)))
    for yh in range(2):
        ahead = dot(band_t, (y_row == y_col + 32 * yh).astype(F32))
        for k in range(9):
            m = k - 4
            value = spread(wall_pairs, k) * ahead[k : k + 1, :]
            inside = (y_lane + m >= 0) & (y_lane + m < 32)
            fore[k, yh] = jnp.where(inside, value, 0.0)
            across = (y_lane + m >= 32) if yh == 0 else (y_lane + m < 0)
            fore[k, 2 + yh] = jnp.where(across, value, 0.0)
        rows_y = lax.broadcasted_iota(jnp.int32, (128, 64), 0) % 64 // 2 + 32 * yh
        at_y = rows_y == lax.broadcasted_iota(jnp.int32, (128, 64), 1)
        value = dot(at_y.astype(F32), placed)
        shift = lax.rem(square_lane // 2 + 4, 64) - 4 + square_row % 64 // 2
        inner = jnp.where((shift >= 0) & (shift < 32), value, 0.0)
        outer = jnp.where((shift >= 0) & (shift < 32), 0.0, value)
        band_tile[yh] = pltpu.roll(inner, 0, 1, stride=1, stride_axis=0)
        band_tile[2 + yh] = pltpu.roll(outer, 64, 1, stride=1, stride_axis=0)

    @pl.loop(0, 8, unroll=2)
    def _(cp):
        for yh in range(2):
            tile = jnp.zeros((128, 128), F32)
            for k in range(9):
                line = fore[k, yh, pl.ds(cp, 1), :]
                tile = jnp.where(square_row == square_lane + 2 * (k - 4), line, tile)
            wide[cp, 128 * yh : 128 * yh + 128, 128 * yh : 128 * yh + 128] = tile.astype(BF16)
            wide_t[cp, 128 * yh : 128 * yh + 128, 128 * yh : 128 * yh + 128] = tile.T.astype(BF16)
            tile = jnp.zeros((128, 128), F32)
            for k in range(5, 9) if yh == 0 else range(4):
                line = fore[k, 2 + yh, pl.ds(cp, 1), :]
                far = 2 * (k - 4) - 64 if yh == 0 else 2 * (k - 4) + 64
                tile = jnp.where(square_row == square_lane + far, line, tile)
            low, high = 128 - 128 * yh, 128 * yh
            wide[cp, low : low + 128, high : high + 128] = tile.astype(BF16)
            wide_t[cp, high : high + 128, low : low + 128] = tile.T.astype(BF16)

    chan = lax.broadcasted_iota(jnp.int32, (128, 128), 0)
    unit = lax.rem(lax.broadcasted_iota(jnp.int32, (128, 128), 1), 8)
    half_row = lax.broadcasted_iota(jnp.int32, (HALF, 128), 0)
    half_z = lax.broadcasted_iota(jnp.int32, (HALF, 128), 1) // 8
    half_k = lax.rem(half_row, 8) // 2
    same_z = (half_row // 8) * 2 + lax.rem(half_row, 2) == half_z
    classes[...] = jnp.zeros((128, 128), F32)
    for par in range(2):
        rows = dot(params[16:24, :], (chan == col * 16 + 2 * unit + par).astype(F32))
        value = jnp.zeros((HALF, 128), F32)
        for k in range(4):
            value = jnp.where(same_z & (half_k == k), rows[k : k + 1, :], value)
        classes[pl.ds(HALF * par, HALF), :] = value
    classes_t[...] = classes[...].T

    def arrived(block):
        for sx, sc in others:
            f_wait(block, sx, sc).wait_recv()
        own_piece(
            block, lambda copy: copy.wait(), lambda copy: copy.wait(), lambda copy: copy.wait_recv()
        )
        low, high = PIECES[block][0], sum(PIECES[block])

        @pl.loop(0, 2 * size)
        def _(t):
            for zp in range(low, high):
                pair = recv[t // 2, lax.rem(t, 2), zp].astype(F32)
                field[t, 2 * zp] = pair[0:8]
                field[t, 2 * zp + 1] = pair[8:16]

        between(seen(field), odd, 2 * low, 2 * high)

    def seen(ref):
        return lambda t, z: ref[t, z]

    def seen_rows(ref):
        return lambda t, z: ref[lax.rem(t, 2), spot(z, t // 2), :]

    def between(src, dst, low, high):
        partner = square_lane + 1 - 2 * lax.rem(square_lane, 2)
        swap = (square_row == partner).astype(F32).astype(BF16)

        @pl.loop(0, 2 * size, unroll=4)
        def _(t):
            after = lax.rem(t + 2, 2 * size)
            mixed = [jnp.where(x_even, src(after, z), src(t, z)) for z in range(low, high)]
            mixed = jnp.concatenate(mixed, axis=0).astype(BF16)
            swapped = jnp.dot(mixed, swap, preferred_element_type=F32)
            for z in range(low, high):
                dst[t, z] = swapped[8 * (z - low) : 8 * (z - low) + 8]

    def filtered(src, mid, t, low, count, flip, put):
        before, after = lax.rem(t + 2 * size - 2, 2 * size), lax.rem(t + 2, 2 * size)
        totals = [None] * count
        for z in range(count + 4):
            at = low + z - 2
            views = (src(before, at), mid[before, at], src(t, at), mid[t, at], src(after, at))
            for j in range(5):
                if 0 <= z - j < count:
                    for i in range(5):
                        q = 5 * (4 - i) + 4 - j if flip else 5 * i + j
                        term = taps[q] * views[i]
                        old = totals[z - j]
                        totals[z - j] = term if old is None else old + term
            if z >= 4:
                put(z - 4, totals)

    def spot(z, p):
        return pl.ds(pl.multiple_of((z * size + p) * 8, 8), 8)

    def unit_rows(z, count, cp):
        return pl.ds(z * size * 8 + cp, count * size, stride=8)

    def unit_of(ref, z, count, cp):
        at = unit_rows(z, count, cp)
        return jnp.concatenate([ref[0, at, :], ref[1, at, :]], axis=1).astype(BF16)

    def p_copy(block):
        return remote(
            part_out.at[block], part_in.at[block], p_send.at[block], p_recv.at[block],
            {"col": 1 - col},
        )

    def ahead_of(block):
        base = 2 + BLOCK * block

        @pl.loop(0, 2 * size)
        def _(t):
            def put(z, totals):
                smooth[lax.rem(t, 2), spot(base + z, t // 2), :] = rounded(totals[z])

            filtered(seen(field), odd, t, base, BLOCK, False, put)

        @pl.loop(0, 8, unroll=8)
        def _(cp):
            both = jnp.dot(
                unit_of(smooth, base, BLOCK, cp), wide[cp], preferred_element_type=F32
            )
            for yh in range(2):
                wall[yh, unit_rows(0, BLOCK, cp), :] = both[:, 128 * yh : 128 * yh + 128]

        @pl.loop(0, BLOCK)
        def _(z):
            at = pl.ds(pl.multiple_of(8 * z, 8), 8)
            for p in range(size):
                for yh in range(2):
                    value = wall[yh, spot(z, p), :]
                    sig = jax.nn.sigmoid(value)
                    lanes = slice(128 * yh, 128 * yh + 128)
                    hid[block, p, at, lanes] = value * sig
                    slope[block, p, at, lanes] = sig * (1.0 + value * (1.0 - sig))

        left_half = lax.rem(lax.broadcasted_iota(jnp.int32, (HALF, 256), 1), 128) < 64

        @pl.loop(0, size, unroll=size)
        def _(p):
            part = split_dot(classes[0:ROWS, 0:ROWS], hid[block, p])
            part_out[block, p] = jnp.where(left_half, part[0:HALF], part[HALF:ROWS])
            lanes = pl.ds(pl.multiple_of(128 * col, 128), 128)
            for zp in range(BLOCK // 2):
                at = slice(8 * zp, 8 * zp + 8)
                mark = lab_win[p, pl.ds(BLOCK // 2 * block + zp, 1), :]
                mark = jnp.broadcast_to(mark, (8, 128))
                mark = jnp.where(lax.rem(row, 2) == 0, mark, pltpu.roll(mark, 64, 1))
                hit = first & (mark == (row // 2).astype(F32))
                part_out[block, p, at, lanes] = part_out[block, p, at, lanes] - jnp.where(hit, 1.0, 0.0)

        p_copy(block).start()

    def back_of(block):
        base = 2 + BLOCK * block
        p_copy(block).wait_recv()
        left_half = lax.rem(lax.broadcasted_iota(jnp.int32, (HALF, 256), 1), 128) < 64

        @pl.loop(0, size, unroll=size)
        def _(p):
            err = part_out[block, p] + part_in[block, p]
            swapped = jnp.concatenate(
                [pltpu.roll(err[:, 0:128], 64, 1), pltpu.roll(err[:, 128:256], 64, 1)], axis=1
            )
            err = err + swapped
            both = jnp.concatenate(
                [jnp.where(left_half, err, 0.0), jnp.where(left_half, 0.0, err)], axis=0
            )
            grad = split_dot(classes_t[0:ROWS, 0:ROWS], both) * slope[block, p]
            for z in range(BLOCK):
                for yh in range(2):
                    gwall[yh, spot(base + z, p), :] = rounded(
                        grad[8 * z : 8 * z + 8, 128 * yh : 128 * yh + 128]
                    )
            new = cast_dot(both, hid[block, p], ((1,), (1,)))
            gram[block, p] = new

        @pl.loop(0, 8, unroll=8)
        def _(cp):
            both = jnp.dot(
                unit_of(gwall, base, BLOCK, cp), wide_t[cp], preferred_element_type=F32
            )
            for yh in range(2):
                at = unit_rows(base, BLOCK, cp)
                gsm[yh, at, :] = rounded(both[:, 128 * yh : 128 * yh + 128])

        between(seen_rows(gsm), godd, base, base + BLOCK)

    def g_spot(block):
        low = 4 if block == 0 else BLOCK * block
        return low, BLOCK * block + BLOCK - low

    def g_copy(back, step):
        at, many = RETURNS[back]
        p, yh = target(step // 2), lax.rem(col + step, 2)
        return remote(
            gout.at[2 * p + yh, pl.ds(at, many)],
            ghome.at[col, pl.ds(gx * zps + at, many)],
            g_send.at[back, step], g_recv.at[back, step], {"gx": p, "col": yh},
        )

    def g_near(back):
        at, many = RETURNS[back]
        return pltpu.make_async_copy(
            gout.at[2 * gx + col, pl.ds(at, many)],
            ghome.at[col, pl.ds(gx * zps + at, many)],
            g_recv.at[back, 0],
        )

    def g_wait(back, step):
        at, many = RETURNS[back]
        slot = ghome.at[col_at[step % 2], pl.ds(origin(step // 2) * zps + at, many)]
        return remote(
            slot, slot, g_send.at[back, step], g_recv.at[back, step],
            {"gx": target(step // 2), "col": col_at[step % 2]},
        )

    def home(block):
        low, count = g_spot(block)

        @pl.loop(0, 2 * size)
        def _(turn_at):
            step = lax.rem(turn_at + 4, 2 * size)
            t = 2 * target(step // 2) + lax.rem(col + step, 2)

            def put(z, totals):
                if z % 2:
                    pair = jnp.concatenate([totals[z - 1], totals[z]], axis=0)
                    gout[t, (low - 4 + z) // 2] = pair.astype(BF16)

            filtered(seen_rows(gsm), godd, t, low, count, True, put)

            @pl.when(step > 0)
            def _():
                g_copy(block, step).start()

            @pl.when(step == 0)
            def _():
                g_near(block).start()

    def labels_in():
        at_end = (gx == 0) | (gx == size - 1)
        for sx in range(size):
            if sx:
                at = lab_recv.at[origin(sx), pl.ds(0, 2)]
                remote(
                    at, at, l_send.at[0, sx], l_recv.at[0, sx], {"gx": target(sx)}
                ).wait_recv()

            @pl.when(at_end)
            def _(sx=sx):
                at = lab_recv.at[origin(sx), 2]
                remote(
                    at, at, l_send.at[1, sx], l_recv.at[1, sx], {"gx": target(sx), "gz": right}
                ).wait_recv()
                lab_wide[origin(sx), 2] = lab_recv[origin(sx), 2].astype(F32)

        l_own.wait()
        low_edge = 2 - (gx + size - 1) // size
        high_edge = 1 + (gx + 1) // size
        for p in range(size):
            lab_win[p, 1 : 1 + zps, :] = lab_recv[p, 0].astype(F32)
            lab_wide[p, 1] = lab_recv[p, 1].astype(F32)
            lab_win[p, 0:1, :] = lab_wide[p, low_edge, pl.ds(2 * gx, 1), :]
            lab_win[p, 1 + zps : 2 + zps, :] = lab_wide[p, high_edge, pl.ds(2 * gx + 1, 1), :]

    def next_piece(piece):
        for sx, sc in others:
            f_wait(piece - 1, sx, sc).wait_send()
        for ct in range(2):
            f_send_all(piece, ct)

    next_piece(1)
    arrived(0)
    labels_in()
    next_piece(2)
    ahead_of(0)
    arrived(1)
    ahead_of(1)
    back_of(0)
    home(0)
    arrived(2)
    ahead_of(2)
    back_of(1)
    home(1)
    back_of(2)
    home(2)

    def tile_body(it, sums25):
        t, base = it // 4, 4 + 8 * lax.rem(it, 4)
        before, after = lax.rem(t + 2 * size - 2, 2 * size), lax.rem(t + 2, 2 * size)
        grads = [seen_rows(gsm)(t, base + z) for z in range(8)]
        news = list(sums25)
        for z in range(12):
            at = base + z - 2
            views = (
                field[before, at], odd[before, at], field[t, at], odd[t, at], field[after, at]
            )
            for j in range(5):
                if 0 <= z - j < 8:
                    for i in range(5):
                        news[5 * i + j] = news[5 * i + j] + views[i] * grads[z - j]
        return tuple(news)

    sums25 = lax.fori_loop(
        0, 8 * size, tile_body, tuple(jnp.zeros((8, 128), F32) for q in range(25))
    )
    for q in range(25):
        acc[8 * q : 8 * q + 8, :] = sums25[q]

    @pl.loop(0, 8, unroll=8)
    def _(cp):
        grads, fields = unit_of(gwall, 4, OWN, cp), unit_of(smooth, 4, OWN, cp)
        both = cast_dot(grads, fields, ((0,), (0,)))
        for par in range(2):
            wall_acc[par, cp] = jnp.zeros((8, 128), F32)
        for yh in range(2):
            here, far = slice(128 * yh, 128 * yh + 128), slice(128 - 128 * yh, 256 - 128 * yh)
            for g in range(16):
                at = slice(128 * yh + 8 * g, 128 * yh + 8 * g + 8)
                tile = both[at, here] * band_tile[yh, 8 * g : 8 * g + 8, :]
                if g % 8 == (0 if yh else 7):
                    edge = both[at, far] * band_tile[2 + yh, 8 * g : 8 * g + 8, :]
                    tile = tile + pltpu.roll(edge, 64, 1)
                wall_acc[g // 8, cp] = wall_acc[g // 8, cp] + pltpu.roll(tile, (128 - 8 * g) % 128, 1)

    inner_row = lax.rem(lax.broadcasted_iota(jnp.int32, (64, 128), 0), 8)
    halves = lax.broadcasted_iota(jnp.int32, (128, 128), 0) // 64
    parity = lax.rem(lax.broadcasted_iota(jnp.int32, (128, 128), 1), 2)
    lines = dot(acc[...], (halves == parity).astype(F32))
    total = jnp.zeros((8, 128), F32)
    for q in range(25):
        total = jnp.where(lane // 2 == q, lines[8 * q : 8 * q + 8, :], total)

    full_row = lax.broadcasted_iota(jnp.int32, (ROWS, ROWS), 0)
    full_lane = lax.broadcasted_iota(jnp.int32, (ROWS, ROWS), 1)
    row_z = lax.rem(full_row, HALF) // 8 * 2 + lax.rem(full_row, 2)
    matrix = jnp.zeros((ROWS, ROWS), F32)
    for block in range(BLOCKS):
        base = 2 + BLOCK * block
        value = gram[block, 0]
        for p in range(1, size):
            value = value + gram[block, p]
        keep = (row_z == full_lane // 8) & (row_z + base >= 4) & (row_z + base < 4 + OWN)
        matrix = matrix + jnp.where(keep, value, 0.0)
    gather = (
        lax.broadcasted_iota(jnp.int32, (8, ROWS), 0)
        == lax.rem(lax.broadcasted_iota(jnp.int32, (8, ROWS), 1), 8)
    ).astype(F32)
    by_row = dot(gather, matrix, ((1,), (1,)))
    source_row = lax.broadcasted_iota(jnp.int32, (ROWS, 128), 0)
    place = 2 * (34 + lax.rem(source_row, 8) // 2) + source_row // HALF
    place = place == lax.broadcasted_iota(jnp.int32, (ROWS, 128), 1)
    total = total + dot(by_row, place.astype(F32))
    stack = (
        lax.broadcasted_iota(jnp.int32, (8, 64), 0)
        == lax.broadcasted_iota(jnp.int32, (8, 64), 1) // 8
    ).astype(F32)
    for par in range(2):
        value = wall_acc[par].reshape(64, 128)
        for r in range(1, 8):
            value = jnp.where(inner_row == r, pltpu.roll(value, 128 - r, 1), value)
        by_lane = dot(stack, value)
        source = lax.rem(square_row // 2 + 4, 64)
        place = (lax.rem(square_row, 2) == 0) & (source < 9) & (
            square_lane == 2 * (25 + source) + par
        )
        total = total + dot(by_lane, place.astype(F32))
    mine[...] = total

    def r_copy(n):
        return remote(mine, sums.at[me], r_send.at[n + 1], r_recv.at[n + 1], coords(*steps[n]))

    r_own = pltpu.make_async_copy(mine, sums.at[me], r_recv.at[0])
    r_own.start()

    for n in range(len(steps)):
        r_copy(n).start()

    for back in range(BLOCKS):
        for step in range(1, 2 * size):
            g_wait(back, step).wait_recv()
        g_near(back).wait()

    for n, (sx, sz, sc) in enumerate(steps):
        place = (origin(sx) * depth + gz_at[-sz % depth]) * 2 + col_at[sc]
        remote(
            sums.at[place], sums.at[place], r_send.at[n + 1], r_recv.at[n + 1], coords(sx, sz, sc)
        ).wait_recv()
    r_own.wait()
    for piece in (2,):
        for sx, sc in others:
            f_wait(piece, sx, sc).wait_send()
    pl.when(gx == 0)(lambda: f_copy(0, 0, col, edge_part(0)[0], 1).wait_send())
    pl.when(gx == size - 1)(lambda: f_copy(last, 0, col, edge_part(last)[0], -1).wait_send())
    for sx in range(size):
        if sx:
            l_copy(sx).wait_send()
        at_ends(sx, lambda copy: copy.wait_send())
    for block in range(BLOCKS):
        p_copy(block).wait_send()
    for back in range(BLOCKS):
        for step in range(1, 2 * size):
            g_copy(back, step).wait_send()

    for n in range(len(steps)):
        r_copy(n).wait_send()


def last_kernel(volume, home, sums, out, tile_out, wall_out, class_out, turn, red):
    members = sums.shape[0] // 2

    for side in range(2):
        @pl.loop(0, 64, unroll=8)
        def _(zp, side=side):
            at = pl.ds(pl.multiple_of(side * 1024 + zp * 16, 16), 16)
            turn[at, :] = home[side, zp].astype(F32)

    for cp in range(16):
        block = turn[pl.ds(cp // 8 * 1024 + cp % 8, 128, stride=8), :].T
        out[pl.ds(2 * cp, 2)] = block.reshape(2, 64, 128).astype(BF16)

    spot = lax.broadcasted_iota(jnp.int32, (128, 128), 0)
    want = 2 * lax.broadcasted_iota(jnp.int32, (128, 128), 1)
    red[...] = jnp.zeros((128, 128), F32)
    for half in range(2):
        total = sums[half]
        for member in range(1, members):
            total = total + sums[2 * member + half]
        total = total / volume
        for par in range(2):
            red[pl.ds(half * 16 + par, 8, stride=2), :] = dot(
                total, (spot == want + par).astype(F32)
            )
    turned = red[...].T
    tile_out[...] = red[0:32, 0:25]
    wall_out[...] = turned[25:34, 0:32]
    class_out[...] = turned[34:38, 0:32]


def regional(
    size, depth, volume,
    features, labels, grid_index, stretch, tile_filter, wall_filter, class_weight,
):
    chans = features.shape[0]
    levels = stretch.shape[0]
    everyone = size * depth * 2
    dma = pltpu.SemaphoreType.DMA
    far = pl.BlockSpec(memory_space=pl.ANY)
    wide = pltpu.VMEM((2 * size, WIN, 8, 128), F32)
    rows = pltpu.VMEM((2, WIN * size * 8, 128), F32)
    block = pltpu.VMEM((BLOCKS, size, ROWS, 256), F32)
    half = pltpu.VMEM((BLOCKS, size, HALF, 256), F32)
    home, sums = pl.pallas_call(
        functools.partial(region_kernel, (size, depth, volume)),
        out_shape=(
            jax.ShapeDtypeStruct((2, 64, 16, 128), BF16),
            jax.ShapeDtypeStruct((everyone, 8, 128), F32),
        ),
        in_specs=[far] * 7,
        out_specs=(far, far),
        scratch_shapes=[
            pltpu.VMEM((chans, 64, 128), BF16),
            pltpu.VMEM((128, 128), jnp.int32),
            pltpu.VMEM((1, 64), jnp.int32),
            pltpu.VMEM((levels, 9), F32),
            pltpu.VMEM((chans, 25), F32),
            pltpu.VMEM((9, chans), F32),
            pltpu.VMEM((4, chans), F32),
            pltpu.VMEM((3, 1024, 128), F32),
            pltpu.VMEM((2, 64, 16, 128), BF16),
            pltpu.VMEM((size, 2, WIN // 2, 16, 128), BF16),
            pltpu.VMEM((64, 128), F32),
            pltpu.VMEM((size, 2, 16, 128), BF16),
            pltpu.VMEM((size, 3, 16, 128), BF16),
            pltpu.VMEM((size, 3, 16, 128), F32),
            pltpu.VMEM((size, 24, 128), F32),
            wide, wide, rows, rows, rows, wide,
            block, block, half, half,
            pltpu.VMEM((25, 8, 128), F32),
            pltpu.VMEM((9, 4, 8, 128), F32),
            pltpu.VMEM((8, 256, 256), BF16),
            pltpu.VMEM((8, 256, 256), BF16),
            pltpu.VMEM((4, 128, 128), F32),
            pltpu.VMEM((2, ROWS * size, 128), F32),
            pltpu.VMEM((2, 8, 8, 128), F32),
            pltpu.VMEM((25 * 8, 128), F32),
            pltpu.VMEM((BLOCKS, size, ROWS, ROWS), F32),
            pltpu.VMEM((128, 128), F32),
            pltpu.VMEM((128, 128), F32),
            pltpu.VMEM((128, 128), F32),
            pltpu.VMEM((2 * size, OWN // 2, 16, 128), BF16),
            pltpu.VMEM((8, 128), F32),
            pltpu.VMEM((128, 128), F32),
            dma((8,)), dma((4,)),
            dma((len(PIECES), size, 2)), dma((len(PIECES), size, 2)),
            dma((2, size)), dma((2, size)),
            dma((BLOCKS,)), dma((BLOCKS,)),
            dma((BLOCKS, 2 * size)), dma((BLOCKS, 2 * size)),
            dma((everyone,)), dma((everyone,)),
        ],
        compiler_params=pltpu.CompilerParams(
            collective_id=0, has_side_effects=True, vmem_limit_bytes=63 * 1024 * 1024
        ),
    )(
        features.reshape(chans, 64, 128), labels.reshape(128, 128), grid_index.reshape(1, 64),
        stretch, tile_filter, wall_filter.T, class_weight,
    )
    def whole(*shape):
        return pl.BlockSpec(shape, lambda: (0,) * len(shape))

    grad, tile_grad, wall_grad, class_grad = pl.pallas_call(
        functools.partial(last_kernel, volume),
        out_shape=(
            jax.ShapeDtypeStruct((chans, 64, 128), BF16),
            jax.ShapeDtypeStruct((chans, 25), F32),
            jax.ShapeDtypeStruct((9, chans), F32),
            jax.ShapeDtypeStruct((4, chans), F32),
        ),
        in_specs=[
            whole(2, 64, 16, 128),
            whole(everyone, 8, 128),
        ],
        out_specs=(
            whole(chans, 64, 128),
            whole(chans, 25), whole(9, chans), whole(4, chans),
        ),
        scratch_shapes=[pltpu.VMEM((2048, 128), F32), pltpu.VMEM((128, 128), F32)],
    )(home, sums)
    return grad.reshape(features.shape), tile_grad, wall_grad.T, class_grad


def shards(features, labels, grid_index, stretch, tile_filter, wall_filter, class_weight):
    chans, rows, cells_x, cells_z = features.shape
    size, depth = lax.axis_size("gx"), lax.axis_size("gz")
    volume = labels.shape[0] * cells_x * size * cells_z * depth
    cpg = chans // size
    if 128 // size == OWN:
        return regional(
            size, depth, volume,
            features, labels, grid_index, stretch, tile_filter, wall_filter, class_weight,
        )
    chunks = min(4, cpg)
    per_dest = max(cpg // 4, 1) * 8
    xs = 2 * size
    everyone = size * depth * 2
    onehot = (grid_index[:, None] == jnp.arange(stretch.shape[0], dtype=jnp.int32)).astype(F32)
    bands = jnp.dot(onehot, stretch, precision=lax.Precision.HIGHEST)
    dma = pltpu.SemaphoreType.DMA
    vmem = pl.BlockSpec(memory_space=pltpu.VMEM)
    smem = pl.BlockSpec(memory_space=pltpu.SMEM)
    grad, tile_grad, wall_grad, class_grad = pl.pallas_call(
        functools.partial(kernel, (size, depth, cpg, chunks, volume)),
        out_shape=(
            jax.ShapeDtypeStruct((chans, 64, 128), BF16),
            jax.ShapeDtypeStruct((chans, 25), F32),
            jax.ShapeDtypeStruct((9, chans), F32),
            jax.ShapeDtypeStruct((4, chans), F32),
        ),
        in_specs=[vmem, vmem, vmem, smem, smem, smem],
        out_specs=(vmem, vmem, vmem, vmem),
        scratch_shapes=[
            pltpu.VMEM((size, cpg, 64, 128), BF16),
            pltpu.VMEM((80, 9), F32),
            pltpu.VMEM((size, per_dest, 128), F32),
            pltpu.VMEM((2, size, per_dest, 128), F32),
            pltpu.VMEM((5, cpg, xs, 32, 128), F32),
            pltpu.VMEM((cpg, xs, 48, 128), F32),
            pltpu.VMEM((max(cpg, size), 64, 128), F32),
            pltpu.VMEM((cpg, 9, 48, 128), F32),
            pltpu.VMEM((9, 48, 128), F32),
            pltpu.VMEM((cpg, xs, 32, 128), F32),
            pltpu.VMEM((cpg, xs, 32, 128), F32),
            pltpu.VMEM((256, 128), F32),
            pltpu.VMEM((size, 256, 128), BF16),
            pltpu.VMEM((size, 256, 128), BF16),
            pltpu.VMEM((size, 256, 128), BF16),
            pltpu.VMEM((cpg, xs, 48, 128), F32),
            pltpu.VMEM((cpg, xs, 32, 128), F32),
            pltpu.VMEM((cpg, xs // 8, 8, 128), F32),
            pltpu.VMEM((2, cpg, xs // 8, 8, 128), F32),
            pltpu.VMEM((5, cpg, xs, 32, 128), F32),
            pltpu.VMEM((size, cpg, 64, 128), BF16),
            pltpu.VMEM((size, 64, 128), F32),
            pltpu.VMEM((cpg, 40, 8, 128), F32),
            pltpu.VMEM((128, 128), F32),
            pltpu.VMEM((everyone, 8, 128), F32),
            dma((chunks, size)), dma((chunks, size)), dma(()),
            dma((2, size)), dma((2, size)),
            dma((cpg,)), dma((cpg,)),
            dma((size,)), dma((size,)),
            dma((size,)), dma((size,)),
            dma((size,)), dma((size,)),
            dma((2, cpg)), dma((2, cpg)),
            dma((chunks, size)), dma((chunks, size)),
            dma((everyone,)), dma((everyone,)),
        ],
        compiler_params=pltpu.CompilerParams(
            collective_id=0, has_side_effects=True, vmem_limit_bytes=48 * 1024 * 1024
        ),
    )(
        features.reshape(chans, 64, 128), labels.reshape(128, 128), bands,
        tile_filter, wall_filter.T, class_weight,
    )
    return grad.reshape(features.shape), tile_grad, wall_grad.T, class_grad


def solution(mesh):
    return jax.shard_map(
        shards,
        mesh=mesh,
        in_specs=(
            P(None, "col", ("group", "gx"), "gz"),
            P(None, ("group", "gx"), "gz"),
            P(),
            P(),
            P(),
            P(),
            P(),
        ),
        out_specs=(
            P(None, "col", ("group", "gx"), "gz"),
            P("group", None),
            P("group", None),
            P("group", None),
        ),
        check_vma=False,
    )
```
